32 devices in a mesh: lon: 8 (over z, y), lat: 2 (over x), lev: 2 (over core).
Axes of the slice: x: 2, y: 2, z: 4, core: 2. Of those that a mesh axis runs over, the one named last changes fastest.
Arguments:
- adjoint_in: float32 [9, 16, 32, 1024], P(None, 'lev', 'lat', 'lon'), may hold values from -6 to 6
- trajectory: bfloat16 [3, 9, 16, 32, 1024], P(None, None, 'lev', 'lat', 'lon'), may hold values from 0.5 to 2
- courant: float32 [2, 16, 32, 1024], P(None, 'lev', 'lat', 'lon'), may hold values from -0.4 to 0.4
- mixing: float32 [16, 32, 1024], P('lev', 'lat', 'lon'), may hold values from 0.02 to 0.2
- coag_rates: float32 [6, 16], replicated, may hold values from 0.02 to 0.2
- settle_speed: float32 [8, 9], replicated, may hold values from 0.01 to 0.2
- settle_class: int32 [16], replicated, may hold values from 0 to 7
- emis_profile: float32 [16], replicated, may hold values from 0.1 to 1
- emis_coef: float32 [9], replicated, may hold values from 0.5 to 2
- land_mask: int32 [32, 1024], P('lat', 'lon'), may hold values 0 or 1
- source_mask: int32 [32, 1024], P('lat', 'lon'), may hold values 0 or 1
Outputs:
- adjoint_out: float32 [9, 16, 32, 1024], P(None, 'lev', 'lat', 'lon')
- emis_grad: float32 [3, 32, 1024], P(None, 'lat', 'lon')
The draws below stay inside these ranges and needn't reach their ends.
All inputs are finite; a program needn't handle non-finite values. No bound on the sum of `land_mask` or of `source_mask` on one device may be relied on, other than what follows from the above.
Results may differ from the reference program's by a relative error of at most 0.0003.
Values may be sent and summed in bfloat16 or wider, within the bound.
No kernel may reach another device: no remote copies, remote signals or barrier semaphores. Data moves between devices by JAX's collectives and lax.ppermute only.
A program may use at most 64 MiB of HBM per device.

```python
import math
import jax
import jax.numpy as jnp
from jax import lax

MODES = 3
TRACERS = 9
NCLASS = 8
STEPS = 3
NX = 1024
NY = 32
NLEV = 16


def place_ends(result, key, least, largest):
    extent = result.shape
    index_at = [jax.random.randint(jax.random.fold_in(key, axis), (), 0, extent[axis]) for axis in range(len(extent))]
    result = result.at[tuple(index_at)].set(least)
    longest = extent.index(max(extent))
    index_at[longest] = (index_at[longest] + 1) % extent[longest]
    return result.at[tuple(index_at)].set(largest)


def block_levels(own_key, shape, cuts, smallest, largest):
    def one(dim, blocks):
        heights = jax.random.uniform(jax.random.fold_in(jax.random.fold_in(own_key, 6), dim), (blocks,), jnp.float32, smallest / len(cuts), largest / len(cuts))
        return jnp.repeat(jnp.exp(heights), shape[dim] // blocks).reshape((-1,) + (1,) * (len(shape) - dim - 1))

    level = one(*cuts[0])
    for cut in cuts[1:]:
        level = level * one(*cut)
    return level


def scatter_about(own_key, shape, scale, most, split=(), kind=jnp.bfloat16):
    values = jax.random.normal(own_key, shape, jnp.float32) * scale
    if len(split) > 0:
        values = block_levels(own_key, shape, split, -0.22, 0.18) * values
    return jnp.clip(values, min=-most, max=most).astype(kind)


def setup_inputs(seed: int = 0) -> dict:
    keys = jax.random.split(jax.random.key(seed), 12)
    return {
        "adjoint_in": scatter_about(keys[0], (TRACERS, NLEV, NY, NX), 1.0, 6.0, ((1, 2), (2, 2), (3, 8)), jnp.float32),
        "trajectory": jnp.clip(0.5 + 1.5 * jax.random.uniform(keys[1], (STEPS, TRACERS, NLEV, NY, NX), jnp.float32) ** block_levels(keys[1], (STEPS, TRACERS, NLEV, NY, NX), ((2, 2), (3, 2), (4, 8)), -0.2, 0.2), 0.5, 2.0).astype(jnp.bfloat16),
        "courant": jnp.clip(jax.random.uniform(keys[2], (2, NLEV, NY, NX), jnp.float32, -0.4, 0.4) * block_levels(keys[2], (2, NLEV, NY, NX), ((1, 2), (2, 2), (3, 8)), -0.4, 0.0), -0.4, 0.4),
        "mixing": jnp.clip(jnp.exp(math.log(0.2) - 2.3025851 * jax.random.uniform(keys[3], (NLEV, NY, NX), jnp.float32) ** block_levels(keys[3], (NLEV, NY, NX), ((0, 2), (1, 2), (2, 8)), -0.2, 0.2)), 0.02, 0.2),
        "coag_rates": jnp.clip(jnp.exp(jax.random.uniform(keys[4], (6, NLEV), jnp.float32, math.log(0.02), math.log(0.2))), 0.02, 0.2),
        "settle_speed": jnp.clip(jnp.exp(jax.random.uniform(keys[5], (NCLASS, TRACERS), jnp.float32, math.log(0.01), math.log(0.2))), 0.01, 0.2),
        "settle_class": place_ends(jax.random.randint(keys[6], (NLEV,), 0, NCLASS), jax.random.fold_in(keys[6], 1), 0, NCLASS - 1).astype(jnp.int32),
        "emis_profile": jnp.clip(jnp.exp(jax.random.uniform(keys[7], (NLEV,), jnp.float32, math.log(0.1), math.log(1.0))), 0.1, 1.0),
        "emis_coef": jnp.clip(jax.random.uniform(keys[8], (TRACERS,), jnp.float32, 0.5, 2.0), 0.5, 2.0),
        "land_mask": place_ends((jax.random.randint(keys[9], (NY, NX), 0, 2) < 1).astype(jnp.int32), jax.random.fold_in(keys[9], 1), 0, 1),
        "source_mask": place_ends((jax.random.randint(keys[10], (NY, NX), 0, 3) < 1).astype(jnp.int32), jax.random.fold_in(keys[10], 1), 0, 1),
    }


def slab(field, axis, start, length):
    return lax.slice_in_dim(field, start, start + length, axis=axis)

def transport(padded, courant_pad, axis, length):
    courant_wide = courant_pad[None]
    diff_face = slab(padded, axis, 0, length + 3) - slab(padded, axis, 1, length + 3)
    face_speed = slab(courant_wide, axis, 0, length + 3)
    forward_part = jnp.maximum(face_speed, 0.0) * diff_face
    backward_part = jnp.minimum(face_speed, 0.0) * diff_face
    return -1.5 * slab(forward_part, axis, 2, length) + 0.5 * slab(forward_part, axis, 3, length) - 1.5 * slab(backward_part, axis, 1, length) + 0.5 * slab(backward_part, axis, 0, length)

def vertical(padded, mixing_pad, speeds, deposit):
    depth_count = padded.shape[1] - 2
    mixing_below = mixing_pad[:depth_count]
    mixing_above = mixing_pad[1:depth_count + 1]
    speed_level = speeds[:, :, None, None]
    centre = padded[:, 1:depth_count + 1]
    return centre * (1.0 - mixing_above - mixing_below - speed_level - deposit) + padded[:, :depth_count] * (mixing_below + speed_level) + padded[:, 2:] * mixing_above

def coag_increment(state, rates):
    rate_grid = rates[:, :, None, None]
    number = [state[0], state[3], state[6]]
    volume = [state[1], state[4], state[7]]
    moment_six = [state[2], state[5], state[8]]
    pair_rate = {(0, 1): rate_grid[3], (0, 2): rate_grid[4], (1, 2): rate_grid[5]}
    outputs = []
    for mode_index in range(3):
        d_number = -rate_grid[mode_index] * number[mode_index] * number[mode_index]
        d_volume = jnp.zeros_like(number[mode_index])
        d_moment = rate_grid[mode_index] * volume[mode_index] * volume[mode_index]
        for other_mode in range(3):
            if other_mode > mode_index:
                pair = pair_rate[mode_index, other_mode]
                d_number = d_number - pair * number[mode_index] * number[other_mode]
                d_volume = d_volume - pair * volume[mode_index] * number[other_mode]
                d_moment = d_moment - pair * moment_six[mode_index] * number[other_mode]
            if other_mode < mode_index:
                pair = pair_rate[other_mode, mode_index]
                d_volume = d_volume + pair * volume[other_mode] * number[mode_index]
                d_moment = d_moment + pair * (moment_six[other_mode] * number[mode_index] + 2.0 * volume[other_mode] * volume[mode_index])
        outputs.extend([d_number, d_volume, d_moment])
    return jnp.stack(outputs)

def coag_adjoint(adjoint, state, rates):
    primal_out, pullback = jax.vjp(lambda value: coag_increment(value, rates), state)
    return adjoint + pullback(adjoint)[0]

def emission_part(adjoint, profile, emis_coef, source):
    weighted = adjoint * (emis_coef[:, None, None, None] * profile[None, :, None, None])
    per_tracer = lax.optimization_barrier(jnp.sum(weighted, axis=1))
    per_mode = lax.optimization_barrier(jnp.sum(per_tracer.reshape(3, 3, per_tracer.shape[1], per_tracer.shape[2]), axis=1))
    return per_mode * source

def reference(adjoint_in, trajectory, courant, mixing, coag_rates, settle_speed, settle_class, emis_profile, emis_coef, land_mask, source_mask):
    east = courant[0]
    north = courant[1].at[:, -1, :].set(0.0)
    mixing_top = mixing.at[-1].set(0.0)
    choose = (settle_class[:, None] == jnp.arange(NCLASS, dtype=jnp.int32)[None, :]).astype(jnp.float32)
    speeds = jnp.dot(choose, settle_speed, precision=lax.Precision.HIGHEST).T
    surface = (jnp.arange(NLEV, dtype=jnp.int32) == 0).astype(jnp.float32)
    deposit = (0.1 + 0.3 * land_mask.astype(jnp.float32))[None] * surface[:, None, None]
    source = source_mask.astype(jnp.float32)
    mixing_pad = jnp.pad(mixing_top, ((1, 1), (0, 0), (0, 0)))
    east_pad = jnp.pad(east, ((0, 0), (0, 0), (2, 2)), mode='wrap')
    north_pad = jnp.pad(north, ((0, 0), (2, 2), (0, 0)))
    adjoint = adjoint_in
    emis_grad = jnp.zeros((MODES, NY, NX), jnp.float32)
    for step_index in range(STEPS - 1, -1, -1):
        emis_grad = emis_grad + emission_part(adjoint, emis_profile, emis_coef, source)
        adjoint = coag_adjoint(adjoint, trajectory[step_index].astype(jnp.float32), coag_rates)
        level_pad = jnp.pad(adjoint, ((0, 0), (1, 1), (0, 0), (0, 0)))
        adjoint = vertical(level_pad, mixing_pad, speeds, deposit)
        lon_pad = jnp.pad(adjoint, ((0, 0), (0, 0), (0, 0), (2, 2)), mode='wrap')
        lat_pad = jnp.pad(adjoint, ((0, 0), (0, 0), (2, 2), (0, 0)))
        adjoint = adjoint + transport(lon_pad, east_pad, 3, NX) + transport(lat_pad, north_pad, 2, NY)
    return (adjoint, emis_grad)
```

```python
import jax
import jax.numpy as jnp
from jax import lax
from jax.experimental import pallas as pl
from jax.experimental.pallas import tpu as pltpu
from jax.sharding import PartitionSpec as P

F32 = jnp.float32
BF16 = jnp.bfloat16
VMEM = pl.BlockSpec(memory_space=pltpu.VMEM)
SMEM = pl.BlockSpec(memory_space=pltpu.SMEM)
PAIRS = ((0, 1, 3), (0, 2, 4), (1, 2, 5))
LAT_TILES = 133
LON_TILES = 52
CORNER_TILES = 26


def iota(shape, axis):
    return lax.broadcasted_iota(jnp.int32, shape, axis)


def split(value):
    high = value.astype(BF16)
    low = (value - high.astype(F32)).astype(BF16)
    return high, low


def stack_rows(top, bottom):
    return jnp.concatenate([top, bottom], axis=0)


def halves(tile):
    wide = tile.astype(F32)
    return wide[:8], wide[8:]


def coag(adj, state, rate):
    out = list(adj)
    kn = {}
    for m, p, q in PAIRS:
        kn[m, p] = rate[q] * state[3 * p]
    for m in range(3):
        total = (2.0 * rate[m]) * state[3 * m]
        for p in range(m + 1, 3):
            total = total + kn[m, p]
        out[3 * m] = out[3 * m] - total * adj[3 * m]
        out[3 * m + 1] = out[3 * m + 1] + (2.0 * rate[m]) * (state[3 * m + 1] * adj[3 * m + 2])
    for m, p, q in PAIRS:
        d_vol = adj[3 * p + 1] - adj[3 * m + 1]
        d_six = adj[3 * p + 2] - adj[3 * m + 2]
        inner = d_vol * state[3 * m + 1] + d_six * state[3 * m + 2] - adj[3 * m] * state[3 * m]
        cross = (2.0 * rate[q]) * adj[3 * p + 2]
        out[3 * p] = out[3 * p] + rate[q] * inner
        out[3 * m + 1] = out[3 * m + 1] + (kn[m, p] * d_vol + cross * state[3 * p + 1])
        out[3 * p + 1] = out[3 * p + 1] + cross * state[3 * m + 1]
        out[3 * m + 2] = out[3 * m + 2] + kn[m, p] * d_six
    return out


def lane_roll(value, shift):
    return pltpu.roll(value, shift, 1)


def weights(east, north):
    pos = jnp.maximum(east, 0.0)
    neg = jnp.minimum(east, 0.0)
    pos_1 = lane_roll(pos, 127)
    neg_1 = lane_roll(neg, 1)
    neg_2 = lane_roll(neg, 2)
    n_pos = jnp.maximum(north[2], 0.0)
    n_pos_1 = jnp.maximum(north[3], 0.0)
    n_neg_1 = jnp.minimum(north[1], 0.0)
    n_neg_2 = jnp.minimum(north[0], 0.0)
    centre = 1.0 + 1.5 * ((neg_1 - pos) + (n_neg_1 - n_pos))
    return (
        centre,
        0.5 * neg_2,
        -1.5 * neg_1 - 0.5 * neg_2,
        1.5 * pos + 0.5 * pos_1,
        -0.5 * pos_1,
        0.5 * n_neg_2,
        -1.5 * n_neg_1 - 0.5 * n_neg_2,
        1.5 * n_pos + 0.5 * n_pos_1,
        -0.5 * n_pos_1,
    )


def transported(rows, w):
    mid = rows[2]
    lon = (w[1] * lane_roll(mid, 2) + w[2] * lane_roll(mid, 1)) + (
        w[3] * lane_roll(mid, 127) + w[4] * lane_roll(mid, 126)
    )
    lat = (w[5] * rows[0] + w[6] * rows[1]) + (w[7] * rows[3] + w[8] * rows[4])
    return w[0] * mid + (lon + lat)


def level_scalars(z, rate_ref, speed_ref, class_ref):
    rate = [rate_ref[q, z] for q in range(6)]
    kind = class_ref[z]
    speed = [speed_ref[kind, t] for t in range(9)]
    return rate, speed


def halo_lanes(core, rows):
    lane = iota((rows, 128), 1)
    return jnp.where(core == 0, (lane >= 120).astype(jnp.int32), (lane < 8).astype(jnp.int32)) > 0


def lat_pack_kernel(lat_count, adj_ref, traj_ref, wind_ref, mix_ref, land_ref, *outs):
    lat = lax.axis_index("lat")

    def fill(out_ref, high_rows):
        base = 8 if high_rows else 0
        sub = iota((8, 128), 0)
        keep = (sub >= 2) if high_rows else (sub < 6)

        def rolled(value, shift):
            return pltpu.roll(value, shift, 0)

        def tracer(t, _):
            v2s = []
            for l in range(8):
                adj = adj_ref[t, l, base : base + 8, :]
                high = adj.astype(BF16).astype(F32)
                low = adj - high
                tr = [traj_ref[k, t, l].astype(F32)[base : base + 8] for k in range(3)]
                if high_rows:
                    extra = (rolled(tr[0], 2), rolled(tr[1], 2), rolled(tr[1], 4))
                else:
                    extra = (rolled(tr[0], 6), rolled(tr[1], 6), rolled(tr[1], 4))
                v0 = jnp.where(keep, high, extra[0])
                v1 = jnp.where(keep, low, extra[1])
                v2s.append(jnp.where(keep, tr[2], extra[2]))
                out_ref[t * 8 + l] = stack_rows(v0, v1).astype(BF16)
            for j in range(4):
                out_ref[72 + t * 4 + j] = stack_rows(v2s[2 * j], v2s[2 * j + 1]).astype(BF16)
            return 0

        lax.fori_loop(0, 9, tracer, 0)

        def level(l, _):
            for q in range(3):
                value = (mix_ref[l] if q == 2 else wind_ref[1 - q, l])[base : base + 8]
                high = value.astype(BF16).astype(F32)
                out_ref[108 + q * 8 + l] = stack_rows(high, value - high).astype(BF16)
            return 0

        lax.fori_loop(0, 8, level, 0)
        land = land_ref[base : base + 8, :].astype(F32)
        out_ref[132] = stack_rows(land, jnp.zeros_like(land)).astype(BF16)

    if lat_count == 2:
        pl.when(lat == 0)(lambda: fill(outs[0], True))
        pl.when(lat == 1)(lambda: fill(outs[0], False))
    else:
        fill(outs[0], True)
        fill(outs[1], False)


def lon_pack_kernel(lat_count, *refs):
    own, other = refs[0:4], refs[4:8]
    land_ref = refs[8]
    out_ref = refs[9]
    corners = refs[10:-1]
    pk = refs[-1]
    core = lax.axis_index("lev")
    lat = lax.axis_index("lat")
    edge = jnp.where(core == 0, 0, 120)
    slot = iota((16, 128), 1) // 8

    def gather(read):
        acc = jnp.zeros((16, 128), F32)
        for s in range(2):
            for l in range(8):
                z = 8 * jnp.bitwise_xor(s, core) + l
                shift = lax.rem(8 * z - edge + 128, 128)
                acc = jnp.where(slot == z, lane_roll(read((own, other)[s], l), shift), acc)
        return acc

    def adj_kind(t, _):
        pk[t] = gather(lambda r, l: r[0][t, l])
        return 0

    lax.fori_loop(0, 9, adj_kind, 0)
    pk[9] = gather(lambda r, l: r[2][1, l])
    pk[10] = gather(lambda r, l: r[2][0, l])
    pk[11] = gather(lambda r, l: r[3][l])
    for k in range(3):

        def traj_kind(t, _):
            pk[12 + 9 * k + t] = gather(lambda r, l: r[1][k, t, l].astype(F32))
            return 0

        lax.fori_loop(0, 9, traj_kind, 0)
    land = land_ref[...].astype(F32)
    pk[39] = jnp.where(slot == 0, lane_roll(land, lax.rem(128 - edge, 128)), 0.0)

    def emit_pair(f, _):
        high, low = split(pk[f])
        out_ref[2 * f] = high
        out_ref[2 * f + 1] = low
        return 0

    lax.fori_loop(0, 12, emit_pair, 0)

    def emit_one(f, _):
        out_ref[24 + f] = pk[12 + f].astype(BF16)
        return 0

    lax.fori_loop(0, 28, emit_one, 0)

    def corner(ref, base):
        rows = pl.ds(base, 8)
        for f in range(12):
            value = pk[f, rows, :]
            high = value.astype(BF16).astype(F32)
            ref[f] = stack_rows(high, value - high).astype(BF16)
        for t in range(9):
            ref[12 + t] = stack_rows(pk[12 + 18 + t, rows, :], pk[12 + 9 + t, rows, :]).astype(BF16)
        for j in range(5):
            ref[21 + j] = stack_rows(
                pk[12 + 2 * j, rows, :], pk[39 if j == 4 else 13 + 2 * j, rows, :]
            ).astype(BF16)

    if lat_count == 2:
        corner(corners[0], pl.multiple_of(jnp.where(lat == 0, 8, 0), 8))
    else:
        corner(corners[0], 8)
        corner(corners[1], 0)


def interior_kernel(lat_count, *refs):
    own, other = refs[0:4], refs[4:8]
    land_ref, lon_ref = refs[8:10]
    rate_ref, speed_ref, class_ref, prof_ref, coef_ref = refs[10:15]
    ce_ref, te_ref, we_ref, le_ref, out_ref, em_ref = refs[15:21]
    a_s, b_s, c_s, w_s, n_s, e_s, d_s = refs[21:]
    core = lax.axis_index("lev")
    lat = lax.axis_index("lat")
    edge = jnp.where(core == 0, 120, 0)
    halo = halo_lanes(core, 16)
    row = iota((16, 128), 0)
    blocks = [pl.ds(pl.multiple_of(jnp.where(lat == 0, 8, 0), 8), 8)] if lat_count == 2 else [pl.ds(8, 8), pl.ds(0, 8)]
    zero = jnp.zeros((16, 128), F32)

    def unslot(value, z):
        return lane_roll(value, lax.rem(edge + 128 - 8 * z, 128))

    def paired(f):
        return lon_ref[2 * f].astype(F32) + lon_ref[2 * f + 1].astype(F32)

    land_halo = unslot(lon_ref[51].astype(F32), 0)
    deposit = 0.1 + 0.3 * jnp.where(halo, land_halo, land_ref[...].astype(F32))
    e_s[16] = deposit
    for e, block in enumerate(blocks):
        le_ref[e] = e_s[16, block, :]
    last_lat = lat == lat_count - 1

    def zero_pads(t, _):
        b_s[t, 0] = zero
        b_s[t, 17] = zero
        for z in range(16):
            c_s[t, z, 0:8, :] = zero[:8]
            c_s[t, z, 24:32, :] = zero[:8]
        return 0

    lax.fori_loop(0, 9, zero_pads, 0)
    d_s[0] = zero

    for s in range(2):
        r = (own, other)[s]

        def assemble(l, _):
            z = 8 * jnp.bitwise_xor(s, core) + l
            for t in range(9):
                a_s[t, z] = jnp.where(halo, unslot(paired(t), z), r[0][t, l])
            north = jnp.where(halo, unslot(paired(9), z), r[2][1, l])
            north = jnp.where((row == 15) & last_lat, 0.0, north)
            east = jnp.where(halo, unslot(paired(10), z), r[2][0, l])
            mix = jnp.where(halo, unslot(paired(11), z), r[3][l])
            n_s[z, 0:8, :] = zero[:8]
            n_s[z, 8:24, :] = north
            n_s[z, 24:32, :] = zero[:8]
            e_s[z] = east
            d_s[z + 1] = jnp.where(z == 15, 0.0, mix)
            for e, block in enumerate(blocks):
                we_ref[e, 0, z] = n_s[z, pl.ds(block.start + 8, 8), :]
                we_ref[e, 1, z] = e_s[z, block, :]
                we_ref[e, 2, z] = d_s[z + 1, block, :]
            shifted = [n_s[z, 6 + i : 22 + i, :] for i in range(4)]
            for i, value in enumerate(weights(east, shifted)):
                w_s[i, z] = value
            return 0

        lax.fori_loop(0, 8, assemble, 0)

    em = [zero, zero, zero]
    for step in range(3):
        k = 2 - step
        for s in range(2):
            r = (own, other)[s]

            def react(l, sums):
                z = 8 * jnp.bitwise_xor(s, core) + l
                rate = [rate_ref[q, z] for q in range(6)]
                share = prof_ref[z]
                adj = [a_s[t, z] for t in range(9)]
                sums = [
                    sums[m] + sum((share * coef_ref[3 * m + j]) * adj[3 * m + j] for j in range(3)) for m in range(3)
                ]
                state = []
                for t in range(9):
                    value = r[1][k, t, l].astype(F32)
                    state.append(jnp.where(halo, unslot(lon_ref[24 + 9 * k + t].astype(F32), z), value))
                done = coag(adj, state, rate)
                for t in range(9):
                    b_s[t, z + 1] = done[t]
                if k < 2:
                    for t in range(9):
                        if lat_count == 2:
                            te_ref[0, k, t, z] = jnp.where(lat == 0, state[t][8:], state[t][:8])
                        else:
                            te_ref[0, k, t, z] = state[t][8:]
                            te_ref[1, k, t, z] = state[t][:8]
                return sums

            if s == 0:
                sums = [zero, zero, zero]
            sums = lax.fori_loop(0, 8, react, sums)
        if step > 0:
            low, high = 2 * step, 15 - 2 * step
            if lat_count == 2:
                good = ((row <= high) | (lat != 0)) & ((row >= low) | (lat == 0))
            else:
                good = (row <= high) & (row >= low)
            sums = [jnp.where(good, v, 0.0) for v in sums]
        em = [em[m] + sums[m] for m in range(3)]

        def mixed(z, _):
            kind = class_ref[z]
            below, above = d_s[z], d_s[z + 1]
            base = 1.0 - above - below
            base = jnp.where(z == 0, base - deposit, base)
            for t in range(9):
                speed = speed_ref[kind, t]
                value = b_s[t, z + 1] * (base - speed) + b_s[t, z] * (below + speed) + b_s[t, z + 2] * above
                c_s[t, z, 8:24, :] = value
                for e, block in enumerate(blocks):
                    ce_ref[e, step, t, z] = c_s[t, z, pl.ds(block.start + 8, 8), :]
            return 0

        lax.fori_loop(0, 16, mixed, 0)

        def moved(z, _):
            for rb in range(2):
                w = [w_s[i, z, 8 * rb : 8 * rb + 8, :] for i in range(9)]
                for t in range(9):
                    rows = [c_s[t, z, 8 * rb + 6 + i : 8 * rb + 14 + i, :] for i in range(5)]
                    value = transported(rows, w)
                    if step < 2:
                        a_s[t, z, 8 * rb : 8 * rb + 8, :] = value
                    else:
                        out_ref[t, z, 8 * rb : 8 * rb + 8, :] = value
            return 0

        lax.fori_loop(0, 16, moved, 0)
    for m in range(3):
        em_ref[m] = em[m]


def edge_kernel(lat_count, *refs):
    edges = 1 if lat_count == 2 else 2
    ce_ref, te_ref, we_ref, le_ref, out_ref, em_ref = refs[0:6]
    lat_refs = refs[6 : 6 + 2 * edges]
    corner_refs = refs[6 + 2 * edges : 6 + 3 * edges]
    rate_ref, speed_ref, class_ref, prof_ref, coef_ref = refs[6 + 3 * edges : 11 + 3 * edges]
    keep_ref, send_ref = refs[11 + 3 * edges : 13 + 3 * edges]
    b_s, c_s, t_s, n_s, e_s, d_s, l_s, a_s, em_s, fin_s = refs[13 + 3 * edges :]
    core = lax.axis_index("lev")
    lat = lax.axis_index("lat")
    edge = jnp.where(core == 0, 120, 0)
    halo = halo_lanes(core, 8)
    sub = iota((8, 128), 0)
    zero = jnp.zeros((8, 128), F32)

    def unslot(value, z):
        return lane_roll(value, lax.rem(edge + 128 - 8 * z, 128))

    def rolled(value, shift):
        return pltpu.roll(value, shift, 0)

    def run(upper, e):
        own_at, halo_at = (0, 8) if upper else (8, 0)
        corner_ref = corner_refs[e]
        keep = (sub < 6) if upper else (sub >= 2)

        def corner_pair(tile, z):
            top, bottom = halves(corner_ref[tile])
            return unslot(top, z), unslot(bottom, z)

        _, land_c = corner_pair(25, 0)
        land_l, _ = halves(lat_refs[2 * e][132])
        l_s[pl.ds(halo_at, 8), :] = 0.1 + 0.3 * jnp.where(halo, land_c, land_l)
        l_s[pl.ds(own_at, 8), :] = le_ref[e]
        d_s[0] = jnp.zeros((16, 128), F32)

        def pads(t, _):
            b_s[t, 0] = zero
            b_s[t, 17] = zero
            for z in range(16):
                c_s[t, z, 0:8, :] = zero
                c_s[t, z, 24:32, :] = zero
            return 0

        lax.fori_loop(0, 9, pads, 0)

        for s in range(2):
            msg = lat_refs[2 * e + s]

            def receive(pair, _):
                for i in range(2):
                    l = 2 * pair + i
                    z = 8 * jnp.bitwise_xor(s, core) + l
                    rate = [rate_ref[q, z] for q in range(6)]
                    adj, state = [], []
                    for t in range(9):
                        v0, v1 = halves(msg[t * 8 + l])
                        v2 = halves(msg[72 + t * 4 + pair])[i]
                        high, low = corner_pair(t, z)
                        adj.append(jnp.where(halo, high + low, jnp.where(keep, v0 + v1, 0.0)))
                        tr2, tr1 = corner_pair(12 + t, z)
                        tile, part = divmod(t, 2)
                        tr0 = unslot(halves(corner_ref[21 + tile])[part], z)
                        state.append(jnp.where(halo, tr2, v2))
                        if upper:
                            own1 = jnp.where(sub < 2, rolled(v1, 2), rolled(v2, 4))
                            own0 = rolled(v0, 2)
                        else:
                            own1 = jnp.where(sub >= 6, rolled(v1, 6), rolled(v2, 4))
                            own0 = rolled(v0, 6)
                        t_s[1, t, z, pl.ds(halo_at, 8), :] = jnp.where(halo, tr1, own1)
                        t_s[0, t, z, pl.ds(halo_at, 8), :] = jnp.where(halo, tr0, own0)
                        t_s[1, t, z, pl.ds(own_at, 8), :] = te_ref[e, 1, t, z]
                        t_s[0, t, z, pl.ds(own_at, 8), :] = te_ref[e, 0, t, z]
                    done = coag(adj, state, rate)
                    for t in range(9):
                        b_s[t, z + 1] = done[t]
                    winds = []
                    for q in range(3):
                        high, low = halves(msg[108 + q * 8 + l])
                        c_high, c_low = corner_pair(9 + q, z)
                        winds.append(jnp.where(halo, c_high + c_low, high + low))
                    n_s[z, 0:8, :] = zero
                    n_s[z, 24:32, :] = zero
                    n_s[z, pl.ds(8 + halo_at, 8), :] = winds[0]
                    n_s[z, pl.ds(8 + own_at, 8), :] = we_ref[e, 0, z]
                    e_s[z, pl.ds(halo_at, 8), :] = winds[1]
                    e_s[z, pl.ds(own_at, 8), :] = we_ref[e, 1, z]
                    d_s[z + 1, pl.ds(halo_at, 8), :] = jnp.where(z == 15, 0.0, winds[2])
                    d_s[z + 1, pl.ds(own_at, 8), :] = we_ref[e, 2, z]
                return 0

            lax.fori_loop(0, 4, receive, 0)

        for m in range(3):
            for part in range(3):
                em_s[m, 8 * part : 8 * part + 8, :] = zero

        starts = (6, 4, 0) if upper else (2, 4, 8)
        at = halo_at
        for step in range(3):

            def mixed(z, _):
                kind = class_ref[z]
                below, above = d_s[z, at : at + 8, :], d_s[z + 1, at : at + 8, :]
                base = 1.0 - above - below
                base = jnp.where(z == 0, base - l_s[at : at + 8, :], base)
                for t in range(9):
                    speed = speed_ref[kind, t]
                    value = b_s[t, z + 1] * (base - speed) + b_s[t, z] * (below + speed) + b_s[t, z + 2] * above
                    c_s[t, z, 8 + own_at : 16 + own_at, :] = ce_ref[e, step, t, z]
                    c_s[t, z, 8 + at : 16 + at, :] = value
                return 0

            lax.fori_loop(0, 16, mixed, 0)
            at = starts[step]

            def moved(z, sums):
                shifted = [n_s[z, 6 + at + i : 14 + at + i, :] for i in range(4)]
                w = weights(e_s[z, at : at + 8, :], shifted)
                adj = []
                for t in range(9):
                    rows = [c_s[t, z, 6 + at + i : 14 + at + i, :] for i in range(5)]
                    adj.append(transported(rows, w))
                if step == 2:
                    for t in range(9):
                        fin_s[e, t, z] = adj[t]
                    return sums
                share = prof_ref[z]
                sums = [
                    sums[m] + sum((share * coef_ref[3 * m + j]) * adj[3 * m + j] for j in range(3)) for m in range(3)
                ]
                rate = [rate_ref[q, z] for q in range(6)]
                state = [t_s[1 - step, t, z, at : at + 8, :] for t in range(9)]
                done = coag(adj, state, rate)
                for t in range(9):
                    b_s[t, z + 1] = done[t]
                return sums

            sums = lax.fori_loop(0, 16, moved, [zero, zero, zero])
            if step < 2:
                buf_row = sub + at
                count = 2 + 2 * step
                if upper:
                    good = (buf_row >= 8 - count) & (buf_row < 8)
                else:
                    good = (buf_row >= 8) & (buf_row < 8 + count)
                for m in range(3):
                    em_s[m, at : at + 8, :] = em_s[m, at : at + 8, :] + jnp.where(good, sums[m], 0.0)
        for m in range(3):
            a_s[e, m] = em_s[m, own_at : own_at + 8, :]

    def finish(has_upper, has_lower, e_upper, e_lower):
        mine = (iota((16, 128), 1) < 64) == (core == 0)
        row8 = sub

        def rows_of(t, z):
            low = out_ref[t, z, 0:8, :]
            high = out_ref[t, z, 8:16, :]
            if has_upper:
                high = jnp.where(row8 >= 2, fin_s[e_upper, t, z], high)
            if has_lower:
                low = jnp.where(row8 < 6, fin_s[e_lower, t, z], low)
            return stack_rows(low, high)

        def tracer(t, _):
            for l in range(8):
                keep_ref[t, l] = rows_of(t, 8 * core + l)
            for l in range(4):
                z = 8 * (1 - core) + l
                send_ref[t * 4 + l] = jnp.where(mine, rows_of(t, z), lane_roll(rows_of(t, z + 4), 64))
            return 0

        lax.fori_loop(0, 9, tracer, 0)
        for m in range(3):
            low = em_ref[m, 0:8, :]
            high = em_ref[m, 8:16, :]
            if has_upper:
                high = high + a_s[e_upper, m]
            if has_lower:
                low = low + a_s[e_lower, m]
            send_ref[36 + m] = stack_rows(low, high)

    if lat_count == 2:

        def south():
            run(True, 0)
            finish(True, False, 0, 0)

        def north():
            run(False, 0)
            finish(False, True, 0, 0)

        pl.when(lat == 0)(south)
        pl.when(lat == 1)(north)
    else:
        run(True, 0)
        run(False, 1)
        finish(True, True, 0, 1)


def join_kernel(keep_ref, send_ref, recv_ref, source_ref, out_ref, em_ref):
    core = lax.axis_index("lev")
    mine = (iota((16, 128), 1) < 64) == (core == 0)

    def tracer(t, _):
        for l in range(4):
            got = recv_ref[t * 4 + l]
            out_ref[t, l] = jnp.where(mine, keep_ref[t, l], got)
            out_ref[t, l + 4] = jnp.where(mine, keep_ref[t, l + 4], lane_roll(got, 64))
        return 0

    lax.fori_loop(0, 9, tracer, 0)
    source = source_ref[...].astype(F32)
    for m in range(3):
        em_ref[m] = jnp.where(mine, send_ref[36 + m], recv_ref[36 + m]) * source


def shape(*dims, dtype=F32):
    return jax.ShapeDtypeStruct(dims, dtype)


def call(kernel, outs, scratch, *args, specs=None):
    return pl.pallas_call(
        kernel,
        out_shape=outs,
        in_specs=specs or [VMEM] * len(args),
        out_specs=[VMEM] * len(outs),
        scratch_shapes=scratch,
        compiler_params=pltpu.CompilerParams(vmem_limit_bytes=48 * 1024 * 1024),
    )(*args)


def shards(
    adjoint_in,
    trajectory,
    courant,
    mixing,
    coag_rates,
    settle_speed,
    settle_class,
    emis_profile,
    emis_coef,
    land_mask,
    source_mask,
):
    lat_count = lax.axis_size("lat")
    lon_count = lax.axis_size("lon")
    edges = 1 if lat_count == 2 else 2
    swap = [(0, 1), (1, 0)]

    def over_lev(value):
        return lax.ppermute(value, "lev", swap)

    def lat_moves(messages):
        if edges == 1:
            return [lax.ppermute(messages[0], "lat", swap)]
        up = [(j, j + 1) for j in range(lat_count - 1)]
        down = [(j + 1, j) for j in range(lat_count - 1)]
        return [lax.ppermute(messages[1], "lat", down), lax.ppermute(messages[0], "lat", up)]

    def corner_moves(messages):
        def pairs(shift):
            found = []
            for i in range(lon_count):
                for x in range(lat_count):
                    y = 1 - x if edges == 1 else x + shift
                    if 0 <= y < lat_count:
                        right, left = (i + 1) % lon_count, (i - 1) % lon_count
                        found.append(((i * lat_count + x) * 2 + 1, (right * lat_count + y) * 2))
                        found.append(((i * lat_count + x) * 2, (left * lat_count + y) * 2 + 1))
            return found

        axes = ("lon", "lat", "lev")
        if edges == 1:
            return [lax.ppermute(messages[0], axes, pairs(0))]
        return [lax.ppermute(messages[1], axes, pairs(-1)), lax.ppermute(messages[0], axes, pairs(1))]

    def bind(kernel):
        def run(*refs):
            return kernel(lat_count, *refs)

        return run

    own = (adjoint_in, trajectory, courant, mixing)
    other = tuple(over_lev(value) for value in own)
    lat_out = call(
        bind(lat_pack_kernel), [shape(LAT_TILES, 16, 128, dtype=BF16)] * edges, [], *own, land_mask
    )
    lat_in = lat_moves(lat_out)
    lon_out, *corner_out = call(
        bind(lon_pack_kernel),
        [shape(LON_TILES, 16, 128, dtype=BF16)] + [shape(CORNER_TILES, 16, 128, dtype=BF16)] * edges,
        [pltpu.VMEM((40, 16, 128), F32)],
        *own,
        *other,
        land_mask,
    )
    lon_pairs = []
    for i in range(lon_count):
        lon_pairs.append((2 * i + 1, 2 * ((i + 1) % lon_count)))
        lon_pairs.append((2 * i, 2 * ((i - 1) % lon_count) + 1))
    lon_in = lax.ppermute(lon_out, ("lon", "lev"), lon_pairs)
    corner_in = corner_moves(corner_out)
    scalars = (coag_rates, settle_speed, settle_class, emis_profile, emis_coef)
    inner = call(
        bind(interior_kernel),
        [
            shape(edges, 3, 9, 16, 8, 128),
            shape(edges, 2, 9, 16, 8, 128),
            shape(edges, 3, 16, 8, 128),
            shape(edges, 8, 128),
            shape(9, 16, 16, 128),
            shape(3, 16, 128),
        ],
        [
            pltpu.VMEM((9, 16, 16, 128), F32),
            pltpu.VMEM((9, 18, 16, 128), F32),
            pltpu.VMEM((9, 16, 32, 128), F32),
            pltpu.VMEM((9, 16, 16, 128), F32),
            pltpu.VMEM((16, 32, 128), F32),
            pltpu.VMEM((17, 16, 128), F32),
            pltpu.VMEM((17, 16, 128), F32),
        ],
        *own,
        *other,
        land_mask,
        lon_in,
        *scalars,
        specs=[VMEM] * 10 + [SMEM] * 5,
    )
    lat_all = []
    for value in lat_in:
        lat_all += [value, over_lev(value)]
    keep, send = call(
        bind(edge_kernel),
        [shape(9, 8, 16, 128), shape(39, 16, 128)],
        [
            pltpu.VMEM((9, 18, 8, 128), F32),
            pltpu.VMEM((9, 16, 32, 128), F32),
            pltpu.VMEM((2, 9, 16, 16, 128), F32),
            pltpu.VMEM((16, 32, 128), F32),
            pltpu.VMEM((16, 16, 128), F32),
            pltpu.VMEM((17, 16, 128), F32),
            pltpu.VMEM((16, 128), F32),
            pltpu.VMEM((edges, 3, 8, 128), F32),
            pltpu.VMEM((3, 24, 128), F32),
            pltpu.VMEM((edges, 9, 16, 8, 128), F32),
        ],
        *inner,
        *lat_all,
        *corner_in,
        *scalars,
        specs=[VMEM] * (6 + 3 * edges) + [SMEM] * 5,
    )
    recv = over_lev(send)
    out, emis = call(
        join_kernel, [shape(9, 8, 16, 128), shape(3, 16, 128)], [], keep, send, recv, source_mask
    )
    return (out, emis)


def solution(mesh):
    return jax.shard_map(
        shards,
        mesh=mesh,
        in_specs=(
            P(None, "lev", "lat", "lon"),
            P(None, None, "lev", "lat", "lon"),
            P(None, "lev", "lat", "lon"),
            P("lev", "lat", "lon"),
            P(),
            P(),
            P(),
            P(),
            P(),
            P("lat", "lon"),
            P("lat", "lon"),
        ),
        out_specs=(P(None, "lev", "lat", "lon"), P(None, "lat", "lon")),
        check_vma=False,
    )
```

```python
import jax
import jax.numpy as jnp
from jax import lax
from jax.experimental import pallas as pl
from jax.experimental.pallas import tpu as pltpu
from jax.sharding import PartitionSpec as P

F32 = jnp.float32
BF16 = jnp.bfloat16
VMEM = pl.BlockSpec(memory_space=pltpu.VMEM)
SMEM = pl.BlockSpec(memory_space=pltpu.SMEM)
PAIRS = ((0, 1, 3), (0, 2, 4), (1, 2, 5))
LAT_TILES = 132
LON_TILES = 42
CORNER_TILES = 21


def iota(shape, axis):
    return lax.broadcasted_iota(jnp.int32, shape, axis)


def split(value):
    high = value.astype(BF16)
    low = (value - high.astype(F32)).astype(BF16)
    return high, low


def stack_rows(top, bottom):
    return jnp.concatenate([top, bottom], axis=0)


def halves(tile):
    wide = tile.astype(F32)
    return wide[:8], wide[8:]


def coag(adj, state, rate):
    out = list(adj)
    kn = {}
    for m, p, q in PAIRS:
        kn[m, p] = rate[q] * state[3 * p]
    for m in range(3):
        total = (2.0 * rate[m]) * state[3 * m]
        for p in range(m + 1, 3):
            total = total + kn[m, p]
        out[3 * m] = out[3 * m] - total * adj[3 * m]
        out[3 * m + 1] = out[3 * m + 1] + (2.0 * rate[m]) * (state[3 * m + 1] * adj[3 * m + 2])
    for m, p, q in PAIRS:
        d_vol = adj[3 * p + 1] - adj[3 * m + 1]
        d_six = adj[3 * p + 2] - adj[3 * m + 2]
        inner = d_vol * state[3 * m + 1] + d_six * state[3 * m + 2] - adj[3 * m] * state[3 * m]
        cross = (2.0 * rate[q]) * adj[3 * p + 2]
        out[3 * p] = out[3 * p] + rate[q] * inner
        out[3 * m + 1] = out[3 * m + 1] + (kn[m, p] * d_vol + cross * state[3 * p + 1])
        out[3 * p + 1] = out[3 * p + 1] + cross * state[3 * m + 1]
        out[3 * m + 2] = out[3 * m + 2] + kn[m, p] * d_six
    return out


def lane_roll(value, shift):
    return pltpu.roll(value, shift, 1)


def weights(east, north):
    pos = jnp.maximum(east, 0.0)
    neg = jnp.minimum(east, 0.0)
    pos_1 = lane_roll(pos, 127)
    neg_1 = lane_roll(neg, 1)
    neg_2 = lane_roll(neg, 2)
    n_pos = jnp.maximum(north[2], 0.0)
    n_pos_1 = jnp.maximum(north[3], 0.0)
    n_neg_1 = jnp.minimum(north[1], 0.0)
    n_neg_2 = jnp.minimum(north[0], 0.0)
    centre = 1.0 + 1.5 * ((neg_1 - pos) + (n_neg_1 - n_pos))
    return (
        centre,
        0.5 * neg_2,
        -1.5 * neg_1 - 0.5 * neg_2,
        1.5 * pos + 0.5 * pos_1,
        -0.5 * pos_1,
        0.5 * n_neg_2,
        -1.5 * n_neg_1 - 0.5 * n_neg_2,
        1.5 * n_pos + 0.5 * n_pos_1,
        -0.5 * n_pos_1,
    )


def transported(rows, w):
    mid = rows[2]
    lon = (w[1] * lane_roll(mid, 2) + w[2] * lane_roll(mid, 1)) + (
        w[3] * lane_roll(mid, 127) + w[4] * lane_roll(mid, 126)
    )
    lat = (w[5] * rows[0] + w[6] * rows[1]) + (w[7] * rows[3] + w[8] * rows[4])
    return w[0] * mid + (lon + lat)


def level_scalars(z, rate_ref, speed_ref, class_ref):
    rate = [rate_ref[q, z] for q in range(6)]
    kind = class_ref[z]
    speed = [speed_ref[kind, t] for t in range(9)]
    return rate, speed


def halo_lanes(core, rows):
    lane = iota((rows, 128), 1)
    return jnp.where(core == 0, (lane >= 120).astype(jnp.int32), (lane < 8).astype(jnp.int32)) > 0


def load_kernel(*refs):
    given, kept, sems = refs[0:5], refs[5:10], refs[10]
    copies = [pltpu.make_async_copy(given[i], kept[i], sems.at[i]) for i in range(5)]
    for copy in copies:
        copy.start()
    for copy in copies:
        copy.wait()


def marked(mix, land, z):
    return jnp.where((land * (z == 0).astype(jnp.int32)) > 0, -mix, mix)


def lat_pack_kernel(lat_count, adj_ref, traj_ref, wind_ref, mix_ref, land_ref, *outs):
    core = lax.axis_index("lev")
    lat = lax.axis_index("lat")

    def fill(out_ref, high_rows):
        base = 8 if high_rows else 0
        sub = iota((8, 128), 0)
        keep = (sub >= 2) if high_rows else (sub < 6)

        def rolled(value, shift):
            return pltpu.roll(value, shift, 0)

        def tracer(t, _):
            v2s = []
            for l in range(8):
                adj = adj_ref[t, l, base : base + 8, :]
                high = adj.astype(BF16).astype(F32)
                low = adj - high
                tr = [traj_ref[k, t, l].astype(F32)[base : base + 8] for k in range(3)]
                if high_rows:
                    extra = (rolled(tr[0], 2), rolled(tr[1], 2), rolled(tr[1], 4))
                else:
                    extra = (rolled(tr[0], 6), rolled(tr[1], 6), rolled(tr[1], 4))
                v0 = jnp.where(keep, high, extra[0])
                v1 = jnp.where(keep, low, extra[1])
                v2s.append(jnp.where(keep, tr[2], extra[2]))
                out_ref[t * 8 + l] = stack_rows(v0, v1).astype(BF16)
            for j in range(4):
                out_ref[72 + t * 4 + j] = stack_rows(v2s[2 * j], v2s[2 * j + 1]).astype(BF16)
            return 0

        lax.fori_loop(0, 9, tracer, 0)

        def level(l, _):
            for q in range(3):
                if q == 2:
                    value = marked(mix_ref[l, base : base + 8, :], land_ref[base : base + 8, :], l + 8 * core)
                else:
                    value = wind_ref[1 - q, l, base : base + 8, :]
                high = value.astype(BF16).astype(F32)
                out_ref[108 + q * 8 + l] = stack_rows(high, value - high).astype(BF16)
            return 0

        lax.fori_loop(0, 8, level, 0)

    if lat_count == 2:
        pl.when(lat == 0)(lambda: fill(outs[0], True))
        pl.when(lat == 1)(lambda: fill(outs[0], False))
    else:
        fill(outs[0], True)
        fill(outs[1], False)


def lon_pack_kernel(lat_count, *refs):
    own, other = refs[0:4], refs[4:8]
    land_ref = refs[8]
    out_ref = refs[9]
    corners = refs[10:]
    core = lax.axis_index("lev")
    lat = lax.axis_index("lat")
    edge = jnp.where(core == 0, 0, 120)
    lane = iota((16, 128), 1)
    slot = lane // 8
    slot_16 = slot.astype(BF16)
    far = (jnp.bitwise_xor((lane // 4) % 2, core)).astype(F32).astype(BF16)
    zero_32 = jnp.zeros((16, 128), F32)
    zero_16 = jnp.zeros((16, 128), BF16)
    lowers = [lat == 1] if lat_count == 2 else [False, True]

    def gather(read, zero, at):
        acc = zero
        for s in range(2):
            for l in range(8):
                g = 8 * s + l
                shift = lax.rem(8 * g - edge + 128, 128)
                acc = jnp.where(at == g, lane_roll(read((own, other)[s], l, jnp.bitwise_xor(s, core)), shift), acc)
        return acc

    def emit(f, value):
        high, low = split(value)
        out_ref[2 * f] = high
        out_ref[2 * f + 1] = low
        for ref, lower in zip(corners, lowers):
            ref[f] = stack_rows(half(high, lower), half(low, lower)).astype(BF16)

    def half(tile, lower):
        top, bottom = halves(tile)
        return jnp.where(lower, top, bottom)

    def tracer(t, _):
        emit(t, gather(lambda r, l, h: r[0][t, l], zero_32, slot))
        tr = [gather(lambda r, l, h: r[1][k, t, l], zero_16, slot_16) for k in range(3)]
        both = jnp.where(far > 0, lane_roll(tr[0], jnp.where(core == 0, 4, 124)), tr[1])
        out_ref[24 + t] = tr[2]
        out_ref[33 + t] = both
        for ref, lower in zip(corners, lowers):
            ref[12 + t] = stack_rows(half(tr[2], lower), half(both, lower)).astype(BF16)
        return 0

    lax.fori_loop(0, 9, tracer, 0)
    emit(9, gather(lambda r, l, h: r[2][1, l], zero_32, slot))
    emit(10, gather(lambda r, l, h: r[2][0, l], zero_32, slot))
    land = land_ref[...]
    emit(11, gather(lambda r, l, h: marked(r[3][l], land, l + 8 * h) if l == 0 else r[3][l], zero_32, slot))


def zero_rows(ref, depth):
    zero = jnp.zeros((8, 128), F32)

    def clear(t, _):
        for z in range(depth):
            ref[t, z, 0:8, :] = zero
            ref[t, z, 24:32, :] = zero
        return 0

    lax.fori_loop(0, 9, clear, 0)


def zero_ends(ref):
    for t in range(9):
        for z in (0, 17):
            ref[t, z] = jnp.zeros(ref.shape[2:], F32)


def react(scalars, traj, a_in, b_s, z, sums):
    rate_ref, speed_ref, class_ref, prof_ref, coef_ref = scalars
    rate = [rate_ref[q, z] for q in range(6)]
    share = [prof_ref[z] * coef_ref[t] for t in range(9)]
    tiles = [traj(t).astype(F32) for t in range(9)]
    parts = []
    for rb in range(2):
        rows = slice(8 * rb, 8 * rb + 8)
        adj = [a_in(t, rows) for t in range(9)]
        done = coag(adj, [tile[rows] for tile in tiles], rate)
        for t in range(9):
            b_s[t, z + 1, rows, :] = done[t]
        parts.append([sums[rb][m] + sum(share[3 * m + j] * adj[3 * m + j] for j in range(3)) for m in range(3)])
    return parts


def mixed(scalars, b_s, d, deposit, c_out, z):
    rate_ref, speed_ref, class_ref, prof_ref, coef_ref = scalars
    kind = class_ref[z]
    below, above = d(z - 1), d(z)
    base = 1.0 - above - below
    base = jnp.where(z == 0, base - deposit, base)
    for t in range(9):
        speed = speed_ref[kind, t]
        c_out[t, z, 8:24, :] = (
            b_s[t, z + 1] * (base - speed) + b_s[t, z] * (below + speed) + b_s[t, z + 2] * above
        )


def moved(c_in, w_ref, a_to, z):
    for rb in range(2):
        rows = slice(8 * rb, 8 * rb + 8)
        w = [w_ref[i, z, rows, :] for i in range(9)]
        for t in range(9):
            shifted = [c_in[t, z, 8 * rb + 6 + i : 8 * rb + 14 + i, :] for i in range(5)]
            a_to[t, z, rows, :] = transported(shifted, w)


def no_sums():
    return [[jnp.zeros((8, 128), F32)] * 3, [jnp.zeros((8, 128), F32)] * 3]


def total(lat_count, step, sums):
    lat = lax.axis_index("lat")
    row = iota((16, 128), 0)
    sums = [stack_rows(sums[0][m], sums[1][m]) for m in range(3)]
    if step == 0:
        return sums
    low, high = 2 * step, 15 - 2 * step
    if lat_count == 2:
        good = ((row <= high) | (lat != 0)) & ((row >= low) | (lat == 0))
    else:
        good = (row <= high) & (row >= low)
    return [jnp.where(good, v, 0.0) for v in sums]


def pipeline(scalars, c_in, w_ref, a_s, b_s, traj_ref, k, d, deposit, c_out):
    def do_react(z, sums):
        return react(scalars, lambda t: traj_ref[k, t, z], lambda t, rows: a_s[t, z, rows, :], b_s, z, sums)

    def do_mixed(z):
        mixed(scalars, b_s, d, deposit, c_out, z)

    moved(c_in, w_ref, a_s, 0)
    moved(c_in, w_ref, a_s, 1)
    sums = do_react(0, no_sums())
    moved(c_in, w_ref, a_s, 2)
    sums = do_react(1, sums)

    def body(z, sums):
        do_mixed(z - 3)
        sums = do_react(z - 1, sums)
        moved(c_in, w_ref, a_s, z)
        return sums

    sums = lax.fori_loop(3, 16, body, sums)
    do_mixed(13)
    sums = do_react(15, sums)
    do_mixed(14)
    do_mixed(15)
    return sums


def first_kernel(lat_count, *refs):
    own, other = refs[0:4], refs[4:8]
    land_ref = refs[8]
    scalars = refs[9:14]
    c_out, em_ref = refs[14:16]
    b_s = refs[16]
    core = lax.axis_index("lev")
    zero_rows(c_out, 16)
    zero_ends(b_s)
    deposit = 0.1 + 0.3 * land_ref[...].astype(F32)

    def run(low, high):
        def level(r, z, l, sums):
            return react(scalars, lambda t: r[1][2, t, l], lambda t, rows: r[0][t, l, rows, :], b_s, z, sums)

        def top(z):
            return jnp.where(z == 7, 0.0, high[3][z])

        def mix(d, z):
            mixed(scalars, b_s, d, deposit, c_out, z)

        below_0 = jnp.zeros((16, 128), F32)
        sums = level(low, 0, 0, no_sums())
        sums = level(low, 1, 1, sums)
        mix(lambda z: below_0 if z < 0 else low[3][z], 0)
        sums = level(low, 2, 2, sums)

        def lower(z, sums):
            mix(lambda i: low[3][i], z - 2)
            return level(low, z, z, sums)

        sums = lax.fori_loop(3, 8, lower, sums)
        mix(lambda i: low[3][i], 6)
        sums = level(high, 8, 0, sums)
        mix(lambda i: low[3][i], 7)
        sums = level(high, 9, 1, sums)
        mix(lambda i: high[3][0] if i == 8 else low[3][7], 8)
        sums = level(high, 10, 2, sums)

        def upper(z, sums):
            mix(lambda i: high[3][i - 8], z - 2)
            return level(high, z, z - 8, sums)

        sums = lax.fori_loop(11, 16, upper, sums)
        mix(lambda i: high[3][i - 8], 14)
        mix(lambda i: high[3][6] if i == 14 else below_0, 15)
        sums = total(lat_count, 0, sums)
        for m in range(3):
            em_ref[m] = sums[m]

    pl.when(core == 0)(lambda: run(own, other))
    pl.when(core == 1)(lambda: run(other, own))


def second_kernel(lat_count, *refs):
    own, other = refs[0:4], refs[4:8]
    land_ref, lon_ref, c_own, em_in = refs[8:12]
    scalars = refs[12:17]
    rate_ref, speed_ref, class_ref, prof_ref, coef_ref = scalars
    traj_out, c_first, c_next, n_out, e_out, d_out, land_out, w_s, em_ref = refs[17:26]
    a_s, b_s, p_s = refs[26:]
    core = lax.axis_index("lev")
    lat = lax.axis_index("lat")
    edge = jnp.where(core == 0, 120, 0)
    halo = halo_lanes(core, 16)
    edge_f = jnp.where(core == 0, 123.5, 3.5).astype(F32)
    halo_16 = jnp.abs(iota((16, 128), 1).astype(F32) - edge_f).astype(BF16) <= jnp.full((16, 128), 3.5, BF16)
    row = iota((16, 128), 0)
    zero = jnp.zeros((16, 128), F32)
    z_lane = jnp.bitwise_xor(iota((8, 128), 1) // 8, 8 * (1 - core))
    zero_rows(c_first, 16)
    zero_rows(c_next, 16)
    zero_ends(b_s)
    d_out[0] = zero

    def shift_of(z):
        return lax.rem(edge + 128 - 8 * jnp.bitwise_xor(z, 8 * (1 - core)), 128)

    def by_lane(read):
        acc = jnp.zeros((8, 128), F32)
        for z in range(16):
            acc = jnp.where(z_lane == z, read(z), acc)
        return acc

    for f in range(9, 12):
        p_s[f] = lon_ref[2 * f].astype(F32) + lon_ref[2 * f + 1].astype(F32)
    rate = [by_lane(lambda z: rate_ref[q, z]) for q in range(6)]
    speeds = [by_lane(lambda z: speed_ref[class_ref[z], t]) for t in range(9)]
    for rb in range(2):
        rows = slice(8 * rb, 8 * rb + 8)
        adj = [(lon_ref[2 * t].astype(F32) + lon_ref[2 * t + 1].astype(F32))[rows] for t in range(9)]
        done = coag(adj, [lon_ref[24 + t].astype(F32)[rows] for t in range(9)], rate)
        mark = p_s[11, rows, :]
        land = ((mark < 0) & (z_lane == 0)).astype(F32)
        size = jnp.abs(mark)
        above = jnp.where(z_lane == 15, 0.0, size)
        below = jnp.where(z_lane == 0, 0.0, lane_roll(size, 8))
        base = 1.0 - above - below - jnp.where(z_lane == 0, 0.1 + 0.3 * land, 0.0)
        for t in range(9):
            under = jnp.where(z_lane == 0, 0.0, lane_roll(done[t], 8))
            p_s[t, rows, :] = (
                done[t] * (base - speeds[t]) + under * (below + speeds[t]) + lane_roll(done[t], 120) * above
            )
    land_halo = (lane_roll(p_s[11], shift_of(0)) < 0).astype(F32)
    deposit = 0.1 + 0.3 * jnp.where(halo, land_halo, land_ref[...].astype(F32))
    land_out[...] = deposit
    last_lat = lat == lat_count - 1

    for s in range(2):
        r = (own, other)[s]

        def assemble(l, _):
            z = 8 * jnp.bitwise_xor(s, core) + l
            shift = shift_of(z)
            for t in range(9):
                c_first[t, z, 8:24, :] = jnp.where(halo, lane_roll(p_s[t], shift), c_own[t, z, 8:24, :])
                traj_out[1, t, z] = jnp.where(halo_16, lane_roll(lon_ref[33 + t], shift), r[1][1, t, l])
                shift_0 = lax.rem(shift + jnp.where(core == 0, 4, 124), 128)
                traj_out[0, t, z] = jnp.where(halo_16, lane_roll(lon_ref[33 + t], shift_0), r[1][0, t, l])
            north = jnp.where(halo, lane_roll(p_s[9], shift), r[2][1, l])
            north = jnp.where((row == 15) & last_lat, 0.0, north)
            east = jnp.where(halo, lane_roll(p_s[10], shift), r[2][0, l])
            mix = jnp.where(halo, jnp.abs(lane_roll(p_s[11], shift)), r[3][l])
            n_out[z, 0:8, :] = zero[:8]
            n_out[z, 8:24, :] = north
            n_out[z, 24:32, :] = zero[:8]
            e_out[z] = east
            d_out[z + 1] = jnp.where(z == 15, 0.0, mix)
            return 0

        lax.fori_loop(0, 8, assemble, 0)

    def weigh(pair, _):
        for i in range(2):
            z = 2 * pair + i
            shifted = [n_out[z, 6 + j : 22 + j, :] for j in range(4)]
            for j, value in enumerate(weights(e_out[z], shifted)):
                w_s[j, z] = value
        return 0

    lax.fori_loop(0, 8, weigh, 0)
    sums = pipeline(
        scalars, c_first, w_s, a_s, b_s, traj_out, 1, lambda z: d_out[z + 1], land_out[...], c_next
    )
    sums = total(lat_count, 1, sums)
    for m in range(3):
        em_ref[m] = em_in[m] + sums[m]


def third_kernel(lat_count, *refs):
    traj_ref, d_ref, land_ref, w_ref, c_in, em_in = refs[0:6]
    scalars = refs[6:11]
    c_next, out_ref, em_ref = refs[11:14]
    a_s, b_s = refs[14:]
    zero_rows(c_next, 16)
    zero_ends(b_s)
    sums = pipeline(scalars, c_in, w_ref, a_s, b_s, traj_ref, 0, lambda z: d_ref[z + 1], land_ref[...], c_next)

    def last(pair, _):
        moved(c_next, w_ref, out_ref, 2 * pair)
        moved(c_next, w_ref, out_ref, 2 * pair + 1)
        return 0

    lax.fori_loop(0, 8, last, 0)
    sums = total(lat_count, 2, sums)
    for m in range(3):
        em_ref[m] = em_in[m] + sums[m]


def edge_kernel(lat_count, *refs):
    edges = 1 if lat_count == 2 else 2
    traj_ref, c_first, c_next, n_ref, e_ref, d_ref, land_ref, c_last, out_ref, em_ref = refs[0:10]
    lat_refs = refs[10 : 10 + 2 * edges]
    corner_refs = refs[10 + 2 * edges : 10 + 3 * edges]
    rate_ref, speed_ref, class_ref, prof_ref, coef_ref = refs[10 + 3 * edges : 15 + 3 * edges]
    keep_ref, send_ref = refs[15 + 3 * edges : 17 + 3 * edges]
    b_0, b_1, c_0, c_1, c_2, t_s, n_s, e_s, d_s, l_s, a_s, em_s, fin_s = refs[17 + 3 * edges :]
    core = lax.axis_index("lev")
    lat = lax.axis_index("lat")
    edge = jnp.where(core == 0, 120, 0)
    flip = 1 - core
    halo = halo_lanes(core, 8)
    sub = iota((8, 128), 0)
    zero = jnp.zeros((8, 128), F32)

    def rolled(value, shift):
        return pltpu.roll(value, shift, 0)

    def run(upper, e):
        own_at, halo_at = (0, 8) if upper else (8, 0)
        own_row = 8 if upper else 0
        corner_ref = corner_refs[e]
        keep = (sub < 6) if upper else (sub >= 2)
        starts = (6, 4, 0) if upper else (2, 4, 8)
        b_bufs, c_bufs = (b_0, b_1, b_0), (c_0, c_1, c_2)

        def shift_of(z):
            return lax.rem(edge + 128 - 8 * jnp.bitwise_xor(z, 8 * flip), 128)

        def corner_pair(tile, z):
            return halves(lane_roll(corner_ref[tile], shift_of(z)))

        land_c = sum(corner_pair(11, 0))
        land_l = jnp.where(core == 0, sum(halves(lat_refs[2 * e][124])), sum(halves(lat_refs[2 * e + 1][124])))
        l_s[pl.ds(halo_at, 8), :] = 0.1 + 0.3 * (jnp.where(halo, land_c, land_l) < 0).astype(F32)
        l_s[pl.ds(own_at, 8), :] = land_ref[pl.ds(own_row, 8), :]
        d_s[0] = jnp.zeros((16, 128), F32)

        def pads(t, _):
            for b in (b_0, b_1):
                b[t, 0] = zero
                b[t, 17] = zero
            for c in c_bufs:
                for z in range(16):
                    c[t, z, 0:8, :] = zero
                    c[t, z, 24:32, :] = zero
            return 0

        lax.fori_loop(0, 9, pads, 0)

        for s in range(2):
            msg = lat_refs[2 * e + s]

            def receive(pair, _):
                for i in range(2):
                    l = 2 * pair + i
                    z = 8 * jnp.bitwise_xor(s, core) + l
                    rate = [rate_ref[q, z] for q in range(6)]
                    adj, state = [], []
                    for t in range(9):
                        v0, v1 = halves(msg[t * 8 + l])
                        v2 = halves(msg[72 + t * 4 + pair])[i]
                        high, low = corner_pair(t, z)
                        adj.append(jnp.where(halo, high + low, jnp.where(keep, v0 + v1, 0.0)))
                        tr2, tr1 = corner_pair(12 + t, z)
                        tr0 = lane_roll(tr1, jnp.where(core == 0, 4, 124))
                        state.append(jnp.where(halo, tr2, v2))
                        if upper:
                            own1 = jnp.where(sub < 2, rolled(v1, 2), rolled(v2, 4))
                            own0 = rolled(v0, 2)
                        else:
                            own1 = jnp.where(sub >= 6, rolled(v1, 6), rolled(v2, 4))
                            own0 = rolled(v0, 6)
                        t_s[1, t, z, pl.ds(halo_at, 8), :] = jnp.where(halo, tr1, own1)
                        t_s[0, t, z, pl.ds(halo_at, 8), :] = jnp.where(halo, tr0, own0)
                        near = 1 if upper else 0
                        t_s[1, t, z, pl.ds(own_at, 8), :] = halves(traj_ref[1, t, z])[near]
                        t_s[0, t, z, pl.ds(own_at, 8), :] = halves(traj_ref[0, t, z])[near]
                    done = coag(adj, state, rate)
                    for t in range(9):
                        b_0[t, z + 1] = done[t]
                    winds = []
                    for q in range(3):
                        high, low = halves(msg[108 + q * 8 + l])
                        c_high, c_low = corner_pair(9 + q, z)
                        winds.append(jnp.where(halo, c_high + c_low, high + low))
                    n_s[z, 0:8, :] = zero
                    n_s[z, 24:32, :] = zero
                    n_s[z, pl.ds(8 + halo_at, 8), :] = winds[0]
                    n_s[z, pl.ds(8 + own_at, 8), :] = n_ref[z, pl.ds(8 + own_row, 8), :]
                    e_s[z, pl.ds(halo_at, 8), :] = winds[1]
                    e_s[z, pl.ds(own_at, 8), :] = e_ref[z, pl.ds(own_row, 8), :]
                    d_s[z + 1, pl.ds(halo_at, 8), :] = jnp.where(z == 15, 0.0, jnp.abs(winds[2]))
                    d_s[z + 1, pl.ds(own_at, 8), :] = d_ref[z + 1, pl.ds(own_row, 8), :]
                return 0

            lax.fori_loop(0, 4, receive, 0)

        for m in range(3):
            for part in range(3):
                em_s[m, 8 * part : 8 * part + 8, :] = zero

        def mix(step, z):
            at = halo_at if step == 0 else starts[step - 1]
            b, c = b_bufs[step], c_bufs[step]
            c_ref = (c_first, c_next, c_last)[step]
            kind = class_ref[z]
            below, above = d_s[z, at : at + 8, :], d_s[z + 1, at : at + 8, :]
            base = 1.0 - above - below
            base = jnp.where(z == 0, base - l_s[at : at + 8, :], base)
            for t in range(9):
                speed = speed_ref[kind, t]
                value = b[t, z + 1] * (base - speed) + b[t, z] * (below + speed) + b[t, z + 2] * above
                c[t, z, 8 + own_at : 16 + own_at, :] = c_ref[t, z, 8 + own_row : 16 + own_row, :]
                c[t, z, 8 + at : 16 + at, :] = value

        def move(step, z, sums):
            at = starts[step]
            c = c_bufs[step]
            shifted = [n_s[z, 6 + at + i : 14 + at + i, :] for i in range(4)]
            w = weights(e_s[z, at : at + 8, :], shifted)
            adj = []
            for t in range(9):
                rows = [c[t, z, 6 + at + i : 14 + at + i, :] for i in range(5)]
                adj.append(transported(rows, w))
            if step == 2:
                for t in range(9):
                    fin_s[e, t, z] = adj[t]
                return sums
            share = [prof_ref[z] * coef_ref[t] for t in range(9)]
            sums = [sums[m] + sum(share[3 * m + j] * adj[3 * m + j] for j in range(3)) for m in range(3)]
            rate = [rate_ref[q, z] for q in range(6)]
            state = [t_s[1 - step, t, z, at : at + 8, :] for t in range(9)]
            done = coag(adj, state, rate)
            for t in range(9):
                b_bufs[step + 1][t, z + 1] = done[t]
            return sums

        def count(step, sums):
            at = starts[step]
            buf_row = sub + at
            rows = 2 + 2 * step
            if upper:
                good = (buf_row >= 8 - rows) & (buf_row < 8)
            else:
                good = (buf_row >= 8) & (buf_row < 8 + rows)
            for m in range(3):
                em_s[m, at : at + 8, :] = em_s[m, at : at + 8, :] + jnp.where(good, sums[m], 0.0)

        none = [zero, zero, zero]
        mix(0, 0)
        mix(0, 1)
        sums = move(0, 0, none)
        mix(0, 2)
        sums = move(0, 1, sums)

        def first(z, sums):
            mix(0, z + 1)
            sums = move(0, z, sums)
            mix(1, z - 2)
            return sums

        sums = lax.fori_loop(2, 15, first, sums)
        sums = move(0, 15, sums)
        mix(1, 13)
        mix(1, 14)
        mix(1, 15)
        count(0, sums)
        sums = move(1, 0, none)
        sums = move(1, 1, sums)

        def second(z, sums):
            sums = move(1, z, sums)
            mix(2, z - 2)
            return sums

        sums = lax.fori_loop(2, 16, second, sums)
        mix(2, 14)
        mix(2, 15)
        count(1, sums)

        def third(pair, _):
            move(2, 2 * pair, none)
            move(2, 2 * pair + 1, none)
            return 0

        lax.fori_loop(0, 8, third, 0)
        for m in range(3):
            a_s[e, m] = em_s[m, own_at : own_at + 8, :]

    def finish(has_upper, has_lower, e_upper, e_lower):
        mine = (iota((16, 128), 1) < 64) == (core == 0)
        row8 = sub

        def rows_of(t, z):
            low = out_ref[t, z, 0:8, :]
            high = out_ref[t, z, 8:16, :]
            if has_upper:
                high = jnp.where(row8 >= 2, fin_s[e_upper, t, z], high)
            if has_lower:
                low = jnp.where(row8 < 6, fin_s[e_lower, t, z], low)
            return stack_rows(low, high)

        def tracer(t, _):
            for l in range(8):
                keep_ref[t, l] = rows_of(t, 8 * core + l)
            for l in range(4):
                z = 8 * (1 - core) + l
                send_ref[t * 4 + l] = jnp.where(mine, rows_of(t, z), lane_roll(rows_of(t, z + 4), 64))
            return 0

        lax.fori_loop(0, 9, tracer, 0)
        for m in range(3):
            low = em_ref[m, 0:8, :]
            high = em_ref[m, 8:16, :]
            if has_upper:
                high = high + a_s[e_upper, m]
            if has_lower:
                low = low + a_s[e_lower, m]
            send_ref[36 + m] = stack_rows(low, high)

    if lat_count == 2:

        def south():
            run(True, 0)
            finish(True, False, 0, 0)

        def north():
            run(False, 0)
            finish(False, True, 0, 0)

        pl.when(lat == 0)(south)
        pl.when(lat == 1)(north)
    else:
        run(True, 0)
        run(False, 1)
        finish(True, True, 0, 1)


def join_kernel(keep_ref, send_ref, recv_ref, source_ref, out_ref, em_ref):
    core = lax.axis_index("lev")
    mine = (iota((16, 128), 1) < 64) == (core == 0)

    def tracer(t, _):
        for l in range(4):
            got = recv_ref[t * 4 + l]
            out_ref[t, l] = jnp.where(mine, keep_ref[t, l], got)
            out_ref[t, l + 4] = jnp.where(mine, keep_ref[t, l + 4], lane_roll(got, 64))
        return 0

    lax.fori_loop(0, 9, tracer, 0)
    source = source_ref[...].astype(F32)
    for m in range(3):
        em_ref[m] = jnp.where(mine, send_ref[36 + m], recv_ref[36 + m]) * source


def shape(*dims, dtype=F32):
    return jax.ShapeDtypeStruct(dims, dtype)


def call(kernel, outs, scratch, *args, specs=None, mib=32):
    return pl.pallas_call(
        kernel,
        out_shape=outs,
        in_specs=specs or [VMEM] * len(args),
        out_specs=[VMEM] * len(outs),
        scratch_shapes=scratch,
        compiler_params=pltpu.CompilerParams(vmem_limit_bytes=mib * 1024 * 1024),
    )(*args)


def shards(
    adjoint_in,
    trajectory,
    courant,
    mixing,
    coag_rates,
    settle_speed,
    settle_class,
    emis_profile,
    emis_coef,
    land_mask,
    source_mask,
):
    lat_count = lax.axis_size("lat")
    lon_count = lax.axis_size("lon")
    edges = 1 if lat_count == 2 else 2
    swap = [(0, 1), (1, 0)]

    def over_lev(value):
        return lax.ppermute(value, "lev", swap)

    def lat_moves(messages):
        if edges == 1:
            return [lax.ppermute(messages[0], "lat", swap)]
        up = [(j, j + 1) for j in range(lat_count - 1)]
        down = [(j + 1, j) for j in range(lat_count - 1)]
        return [lax.ppermute(messages[1], "lat", down), lax.ppermute(messages[0], "lat", up)]

    def corner_moves(messages):
        def pairs(shift):
            found = []
            for i in range(lon_count):
                for x in range(lat_count):
                    y = 1 - x if edges == 1 else x + shift
                    if 0 <= y < lat_count:
                        right, left = (i + 1) % lon_count, (i - 1) % lon_count
                        found.append(((i * lat_count + x) * 2 + 1, (right * lat_count + y) * 2))
                        found.append(((i * lat_count + x) * 2, (left * lat_count + y) * 2 + 1))
            return found

        axes = ("lon", "lat", "lev")
        if edges == 1:
            return [lax.ppermute(messages[0], axes, pairs(0))]
        return [lax.ppermute(messages[1], axes, pairs(-1)), lax.ppermute(messages[0], axes, pairs(1))]

    def bind(kernel):
        def run(*refs):
            return kernel(lat_count, *refs)

        return run

    given = (adjoint_in, trajectory, courant, mixing)
    other = tuple(over_lev(value) for value in given)
    *own, land = call(
        load_kernel,
        [jax.ShapeDtypeStruct(v.shape, v.dtype) for v in given + (land_mask,)],
        [pltpu.SemaphoreType.DMA((5,))],
        *[pltpu.with_memory_space_constraint(v, pltpu.HBM) for v in given + (land_mask,)],
        specs=[pl.BlockSpec(memory_space=pltpu.HBM)] * 5,
        mib=16,
    )
    lon_out, *corner_out = call(
        bind(lon_pack_kernel),
        [shape(LON_TILES, 16, 128, dtype=BF16)] + [shape(CORNER_TILES, 16, 128, dtype=BF16)] * edges,
        [],
        *own,
        *other,
        land,
        mib=16,
    )
    lat_out = call(
        bind(lat_pack_kernel), [shape(LAT_TILES, 16, 128, dtype=BF16)] * edges, [], *own, land, mib=16
    )
    lat_in = lat_moves(lat_out)
    lon_pairs = []
    for i in range(lon_count):
        lon_pairs.append((2 * i + 1, 2 * ((i + 1) % lon_count)))
        lon_pairs.append((2 * i, 2 * ((i - 1) % lon_count) + 1))
    lon_in = lax.ppermute(lon_out, ("lon", "lev"), lon_pairs)
    corner_in = corner_moves(corner_out)
    scalars = (coag_rates, settle_speed, settle_class, emis_profile, emis_coef)
    state = pltpu.VMEM((9, 16, 16, 128), F32)
    between = pltpu.VMEM((9, 18, 16, 128), F32)
    padded = shape(9, 16, 32, 128)
    c_own, emis = call(
        bind(first_kernel),
        [padded, shape(3, 16, 128)],
        [between],
        *own,
        *other,
        land,
        *scalars,
        specs=[VMEM] * 9 + [SMEM] * 5,
    )
    lon_in, c_own = lax.optimization_barrier((lon_in, c_own))
    traj_all, c_first, c_next, north, east, mix, land_all, weight, emis = call(
        bind(second_kernel),
        [
            shape(2, 9, 16, 16, 128, dtype=BF16),
            padded,
            padded,
            shape(16, 32, 128),
            shape(16, 16, 128),
            shape(17, 16, 128),
            shape(16, 128),
            shape(9, 16, 16, 128),
            shape(3, 16, 128),
        ],
        [state, between, pltpu.VMEM((12, 16, 128), F32)],
        *own,
        *other,
        land,
        lon_in,
        c_own,
        emis,
        *scalars,
        specs=[VMEM] * 12 + [SMEM] * 5,
    )
    c_next, *lat_in = lax.optimization_barrier((c_next, *lat_in))
    c_last, final, emis = call(
        bind(third_kernel),
        [padded, shape(9, 16, 16, 128), shape(3, 16, 128)],
        [state, between],
        traj_all,
        mix,
        land_all,
        weight,
        c_next,
        emis,
        *scalars,
        specs=[VMEM] * 6 + [SMEM] * 5,
    )
    inner = (traj_all, c_first, c_next, north, east, mix, land_all, c_last, final, emis)
    lat_all = []
    for value in lat_in:
        lat_all += [value, over_lev(value)]
    keep, send = call(
        bind(edge_kernel),
        [shape(9, 8, 16, 128), shape(39, 16, 128)],
        [
            pltpu.VMEM((9, 18, 8, 128), F32),
            pltpu.VMEM((9, 18, 8, 128), F32),
            pltpu.VMEM((9, 16, 32, 128), F32),
            pltpu.VMEM((9, 16, 32, 128), F32),
            pltpu.VMEM((9, 16, 32, 128), F32),
            pltpu.VMEM((2, 9, 16, 16, 128), F32),
            pltpu.VMEM((16, 32, 128), F32),
            pltpu.VMEM((16, 16, 128), F32),
            pltpu.VMEM((17, 16, 128), F32),
            pltpu.VMEM((16, 128), F32),
            pltpu.VMEM((edges, 3, 8, 128), F32),
            pltpu.VMEM((3, 24, 128), F32),
            pltpu.VMEM((edges, 9, 16, 8, 128), F32),
        ],
        *inner,
        *lat_all,
        *corner_in,
        *scalars,
        specs=[VMEM] * (10 + 3 * edges) + [SMEM] * 5,
        mib=40,
    )
    recv = over_lev(send)
    out, emis = call(
        join_kernel, [shape(9, 8, 16, 128), shape(3, 16, 128)], [], keep, send, recv, source_mask
    )
    return (out, emis)


def solution(mesh):
    return jax.shard_map(
        shards,
        mesh=mesh,
        in_specs=(
            P(None, "lev", "lat", "lon"),
            P(None, None, "lev", "lat", "lon"),
            P(None, "lev", "lat", "lon"),
            P("lev", "lat", "lon"),
            P(),
            P(),
            P(),
            P(),
            P(),
            P("lat", "lon"),
            P("lat", "lon"),
        ),
        out_specs=(P(None, "lev", "lat", "lon"), P(None, "lat", "lon")),
        check_vma=False,
    )
```

```python
import jax
import jax.numpy as jnp
from jax import lax
from jax.experimental import pallas as pl
from jax.experimental.pallas import tpu as pltpu
from jax.sharding import PartitionSpec as P

F32 = jnp.float32
BF16 = jnp.bfloat16
VMEM = pl.BlockSpec(memory_space=pltpu.VMEM)
SMEM = pl.BlockSpec(memory_space=pltpu.SMEM)
PAIRS = ((0, 1, 3), (0, 2, 4), (1, 2, 5))
LAT_TILES = 132
LON_TILES = 42


def iota(shape, axis):
    return lax.broadcasted_iota(jnp.int32, shape, axis)


def split(value):
    high = value.astype(BF16)
    low = (value - high.astype(F32)).astype(BF16)
    return high, low


def stack_rows(top, bottom):
    return jnp.concatenate([top, bottom], axis=0)


def halves(tile):
    wide = tile.astype(F32)
    return wide[:8], wide[8:]


def coag(adj, state, rate):
    out = list(adj)
    kn = {}
    for m, p, q in PAIRS:
        kn[m, p] = rate[q] * state[3 * p]
    for m in range(3):
        total = (2.0 * rate[m]) * state[3 * m]
        for p in range(m + 1, 3):
            total = total + kn[m, p]
        out[3 * m] = out[3 * m] - total * adj[3 * m]
        out[3 * m + 1] = out[3 * m + 1] + (2.0 * rate[m]) * (state[3 * m + 1] * adj[3 * m + 2])
    for m, p, q in PAIRS:
        d_vol = adj[3 * p + 1] - adj[3 * m + 1]
        d_six = adj[3 * p + 2] - adj[3 * m + 2]
        inner = d_vol * state[3 * m + 1] + d_six * state[3 * m + 2] - adj[3 * m] * state[3 * m]
        cross = (2.0 * rate[q]) * adj[3 * p + 2]
        out[3 * p] = out[3 * p] + rate[q] * inner
        out[3 * m + 1] = out[3 * m + 1] + (kn[m, p] * d_vol + cross * state[3 * p + 1])
        out[3 * p + 1] = out[3 * p + 1] + cross * state[3 * m + 1]
        out[3 * m + 2] = out[3 * m + 2] + kn[m, p] * d_six
    return out


def lane_roll(value, shift):
    return pltpu.roll(value, shift, 1)


def weights(east, north):
    pos = jnp.maximum(east, 0.0)
    neg = jnp.minimum(east, 0.0)
    pos_1 = lane_roll(pos, 127)
    neg_1 = lane_roll(neg, 1)
    neg_2 = lane_roll(neg, 2)
    n_pos = jnp.maximum(north[2], 0.0)
    n_pos_1 = jnp.maximum(north[3], 0.0)
    n_neg_1 = jnp.minimum(north[1], 0.0)
    n_neg_2 = jnp.minimum(north[0], 0.0)
    centre = 1.0 + 1.5 * ((neg_1 - pos) + (n_neg_1 - n_pos))
    return (
        centre,
        0.5 * neg_2,
        -1.5 * neg_1 - 0.5 * neg_2,
        1.5 * pos + 0.5 * pos_1,
        -0.5 * pos_1,
        0.5 * n_neg_2,
        -1.5 * n_neg_1 - 0.5 * n_neg_2,
        1.5 * n_pos + 0.5 * n_pos_1,
        -0.5 * n_pos_1,
    )


def transported(rows, w):
    mid = rows[2]
    lon = (w[1] * lane_roll(mid, 2) + w[2] * lane_roll(mid, 1)) + (
        w[3] * lane_roll(mid, 127) + w[4] * lane_roll(mid, 126)
    )
    lat = (w[5] * rows[0] + w[6] * rows[1]) + (w[7] * rows[3] + w[8] * rows[4])
    return w[0] * mid + (lon + lat)


def level_scalars(z, rate_ref, speed_ref, class_ref):
    rate = [rate_ref[q, z] for q in range(6)]
    kind = class_ref[z]
    speed = [speed_ref[kind, t] for t in range(9)]
    return rate, speed


def halo_lanes(core, rows):
    lane = iota((rows, 128), 1)
    return jnp.where(core == 0, (lane >= 120).astype(jnp.int32), (lane < 8).astype(jnp.int32)) > 0


def load_kernel(*refs):
    given, kept, sems = refs[0:5], refs[5:10], refs[10]
    copies = [pltpu.make_async_copy(given[i], kept[i], sems.at[i]) for i in range(5)]
    for copy in copies:
        copy.start()
    for copy in copies:
        copy.wait()


def marked(mix, land, z):
    return jnp.where((land * (z == 0).astype(jnp.int32)) > 0, -mix, mix)


def lat_pack_kernel(lat_count, adj_ref, traj_ref, wind_ref, mix_ref, land_ref, *outs):
    core = lax.axis_index("lev")
    lat = lax.axis_index("lat")

    def fill(out_ref, high_rows):
        base = 8 if high_rows else 0
        sub = iota((8, 128), 0)
        keep = (sub >= 2) if high_rows else (sub < 6)

        def rolled(value, shift):
            return pltpu.roll(value, shift, 0)

        def tracer(t, _):
            v2s = []
            for l in range(8):
                adj = adj_ref[t, l, base : base + 8, :]
                high = adj.astype(BF16).astype(F32)
                low = adj - high
                tr = [traj_ref[k, t, l].astype(F32)[base : base + 8] for k in range(3)]
                if high_rows:
                    extra = (rolled(tr[0], 2), rolled(tr[1], 2), rolled(tr[1], 4))
                else:
                    extra = (rolled(tr[0], 6), rolled(tr[1], 6), rolled(tr[1], 4))
                v0 = jnp.where(keep, high, extra[0])
                v1 = jnp.where(keep, low, extra[1])
                v2s.append(jnp.where(keep, tr[2], extra[2]))
                out_ref[t * 8 + l] = stack_rows(v0, v1).astype(BF16)
            for j in range(4):
                out_ref[72 + t * 4 + j] = stack_rows(v2s[2 * j], v2s[2 * j + 1]).astype(BF16)
            return 0

        lax.fori_loop(0, 9, tracer, 0)

        def level(l, _):
            for q in range(3):
                if q == 2:
                    value = marked(mix_ref[l, base : base + 8, :], land_ref[base : base + 8, :], l + 8 * core)
                else:
                    value = wind_ref[1 - q, l, base : base + 8, :]
                high = value.astype(BF16).astype(F32)
                out_ref[108 + q * 8 + l] = stack_rows(high, value - high).astype(BF16)
            return 0

        lax.fori_loop(0, 8, level, 0)

    if lat_count == 2:
        pl.when(lat == 0)(lambda: fill(outs[0], True))
        pl.when(lat == 1)(lambda: fill(outs[0], False))
    else:
        fill(outs[0], True)
        fill(outs[1], False)


def lon_pack_kernel(lat_count, *refs):
    own, other = refs[0:4], refs[4:8]
    land_ref = refs[8]
    out_ref = refs[9]
    core = lax.axis_index("lev")
    edge = jnp.where(core == 0, 0, 120)
    lane = iota((16, 128), 1)
    slot = lane // 8
    slot_16 = slot.astype(BF16)
    far = (jnp.bitwise_xor((lane // 4) % 2, core)).astype(F32).astype(BF16)
    zero_32 = jnp.zeros((16, 128), F32)
    zero_16 = jnp.zeros((16, 128), BF16)

    def gather(read, zero, at):
        acc = zero
        for s in range(2):
            for l in range(8):
                g = 8 * s + l
                shift = lax.rem(8 * g - edge + 128, 128)
                acc = jnp.where(at == g, lane_roll(read((own, other)[s], l, jnp.bitwise_xor(s, core)), shift), acc)
        return acc

    def emit(f, value):
        high, low = split(value)
        out_ref[2 * f] = high
        out_ref[2 * f + 1] = low

    def tracer(t, _):
        emit(t, gather(lambda r, l, h: r[0][t, l], zero_32, slot))
        tr = [gather(lambda r, l, h: r[1][k, t, l], zero_16, slot_16) for k in range(3)]
        both = jnp.where(far > 0, lane_roll(tr[0], jnp.where(core == 0, 4, 124)), tr[1])
        out_ref[24 + t] = tr[2]
        out_ref[33 + t] = both
        return 0

    lax.fori_loop(0, 9, tracer, 0)
    emit(9, gather(lambda r, l, h: r[2][1, l], zero_32, slot))
    emit(10, gather(lambda r, l, h: r[2][0, l], zero_32, slot))
    land = land_ref[...]
    emit(11, gather(lambda r, l, h: marked(r[3][l], land, l + 8 * h) if l == 0 else r[3][l], zero_32, slot))


def zero_rows(ref, depth):
    zero = jnp.zeros((8, 128), F32)

    def clear(t, _):
        for z in range(depth):
            ref[t, z, 0:8, :] = zero
            ref[t, z, 24:32, :] = zero
        return 0

    lax.fori_loop(0, 9, clear, 0)


def zero_ends(ref):
    for t in range(9):
        for z in (0, 17):
            ref[t, z] = jnp.zeros(ref.shape[2:], F32)


def react(scalars, traj, a_in, b_s, z, sums):
    rate_ref, speed_ref, class_ref, prof_ref, coef_ref = scalars
    rate = [rate_ref[q, z] for q in range(6)]
    share = [prof_ref[z] * coef_ref[t] for t in range(9)]
    tiles = [traj(t).astype(F32) for t in range(9)]
    parts = []
    for rb in range(2):
        rows = slice(8 * rb, 8 * rb + 8)
        adj = [a_in(t, rows) for t in range(9)]
        done = coag(adj, [tile[rows] for tile in tiles], rate)
        for t in range(9):
            b_s[t, z + 1, rows, :] = done[t]
        parts.append([sums[rb][m] + sum(share[3 * m + j] * adj[3 * m + j] for j in range(3)) for m in range(3)])
    return parts


def mixed(scalars, b_s, d, deposit, c_out, z):
    rate_ref, speed_ref, class_ref, prof_ref, coef_ref = scalars
    kind = class_ref[z]
    below, above = d(z - 1), d(z)
    base = 1.0 - above - below
    base = jnp.where(z == 0, base - deposit, base)
    for t in range(9):
        speed = speed_ref[kind, t]
        c_out[t, z, 8:24, :] = (
            b_s[t, z + 1] * (base - speed) + b_s[t, z] * (below + speed) + b_s[t, z + 2] * above
        )


def moved(c_in, w_ref, a_to, z):
    for rb in range(2):
        rows = slice(8 * rb, 8 * rb + 8)
        w = [w_ref[i, z, rows, :] for i in range(9)]
        for t in range(9):
            shifted = [c_in[t, z, 8 * rb + 6 + i : 8 * rb + 14 + i, :] for i in range(5)]
            a_to[t, z, rows, :] = transported(shifted, w)


def no_sums():
    return [[jnp.zeros((8, 128), F32)] * 3, [jnp.zeros((8, 128), F32)] * 3]


def total(lat_count, step, sums):
    lat = lax.axis_index("lat")
    row = iota((16, 128), 0)
    sums = [stack_rows(sums[0][m], sums[1][m]) for m in range(3)]
    if step == 0:
        return sums
    low, high = 2 * step, 15 - 2 * step
    if lat_count == 2:
        good = ((row <= high) | (lat != 0)) & ((row >= low) | (lat == 0))
    else:
        good = (row <= high) & (row >= low)
    return [jnp.where(good, v, 0.0) for v in sums]


def pipeline(stages, carry=None):
    stages = sorted(stages, key=lambda stage: -stage[0])
    depth = stages[0][0]

    def at(z, carry):
        for lag, stage in stages:
            if not isinstance(z, int) or 0 <= z - lag < 16:
                carry = stage(z - lag, carry)
        return carry

    for z in range(depth):
        carry = at(z, carry)
    carry = lax.fori_loop(depth, 16, at, carry)
    for z in range(16, 16 + depth):
        carry = at(z, carry)
    return carry


def first_kernel(lat_count, *refs):
    own, other = refs[0:4], refs[4:8]
    land_ref = refs[8]
    scalars = refs[9:14]
    c_out, em_ref, traj_out, wind_out, mix_out = refs[14:19]
    b_s = refs[19]
    core = lax.axis_index("lev")
    zero_rows(c_out, 16)
    zero_ends(b_s)
    deposit = 0.1 + 0.3 * land_ref[...].astype(F32)
    nothing = jnp.zeros((16, 128), F32)

    def run(low, high):
        def level(r, z, l, sums):
            for k in range(2):
                for t in range(9):
                    traj_out[k, t, z] = r[1][k, t, l]
            for i in range(2):
                wind_out[i, z] = r[2][i, l]
            mix_out[z] = r[3][l]
            return react(scalars, lambda t: r[1][2, t, l], lambda t, rows: r[0][t, l, rows, :], b_s, z, sums)

        def mix(z):
            def d(i):
                if isinstance(i, int) and i in (-1, 15):
                    return nothing
                return mix_out[i]

            mixed(scalars, b_s, d, deposit, c_out, z)

        sums = no_sums()
        for z in range(3):
            sums = level(low, z, z, sums)
        mix(0)

        def lower(z, sums):
            mix(z - 2)
            return level(low, z, z, sums)

        sums = lax.fori_loop(3, 8, lower, sums)

        def upper(z, sums):
            mix(z - 2)
            return level(high, z, z - 8, sums)

        sums = lax.fori_loop(8, 16, upper, sums)
        mix(14)
        mix(15)
        sums = total(lat_count, 0, sums)
        for m in range(3):
            em_ref[m] = sums[m]

    pl.when(core == 0)(lambda: run(own, other))
    pl.when(core == 1)(lambda: run(other, own))


def second_kernel(lat_count, *refs):
    land_ref, lon_ref, c_own, em_in, traj_own, wind_own, mix_own = refs[0:7]
    scalars = refs[7:12]
    rate_ref, speed_ref, class_ref, prof_ref, coef_ref = scalars
    traj_out, c_first, c_next, n_out, e_out, d_out, land_out, w_s, em_ref = refs[12:21]
    a_s, b_s, p_s = refs[21:]
    core = lax.axis_index("lev")
    lat = lax.axis_index("lat")
    edge = jnp.where(core == 0, 120, 0)
    halo = halo_lanes(core, 16)
    edge_f = jnp.where(core == 0, 123.5, 3.5).astype(F32)
    halo_16 = jnp.abs(iota((16, 128), 1).astype(F32) - edge_f).astype(BF16) <= jnp.full((16, 128), 3.5, BF16)
    row = iota((16, 128), 0)
    zero = jnp.zeros((16, 128), F32)
    z_lane = jnp.bitwise_xor(iota((8, 128), 1) // 8, 8 * (1 - core))
    zero_rows(c_first, 16)
    zero_rows(c_next, 16)
    zero_ends(b_s)
    d_out[0] = zero

    def shift_of(z):
        return lax.rem(edge + 128 - 8 * jnp.bitwise_xor(z, 8 * (1 - core)), 128)

    def by_lane(read):
        acc = jnp.zeros((8, 128), F32)
        for z in range(16):
            acc = jnp.where(z_lane == z, read(z), acc)
        return acc

    for f in range(9, 12):
        p_s[f] = lon_ref[2 * f].astype(F32) + lon_ref[2 * f + 1].astype(F32)
    rate = [by_lane(lambda z: rate_ref[q, z]) for q in range(6)]
    speeds = [by_lane(lambda z: speed_ref[class_ref[z], t]) for t in range(9)]
    for rb in range(2):
        rows = slice(8 * rb, 8 * rb + 8)
        adj = [(lon_ref[2 * t].astype(F32) + lon_ref[2 * t + 1].astype(F32))[rows] for t in range(9)]
        done = coag(adj, [lon_ref[24 + t].astype(F32)[rows] for t in range(9)], rate)
        mark = p_s[11, rows, :]
        land = ((mark < 0) & (z_lane == 0)).astype(F32)
        size = jnp.abs(mark)
        above = jnp.where(z_lane == 15, 0.0, size)
        below = jnp.where(z_lane == 0, 0.0, lane_roll(size, 8))
        base = 1.0 - above - below - jnp.where(z_lane == 0, 0.1 + 0.3 * land, 0.0)
        for t in range(9):
            under = jnp.where(z_lane == 0, 0.0, lane_roll(done[t], 8))
            p_s[t, rows, :] = (
                done[t] * (base - speeds[t]) + under * (below + speeds[t]) + lane_roll(done[t], 120) * above
            )
    land_halo = (lane_roll(p_s[11], shift_of(0)) < 0).astype(F32)
    deposit = 0.1 + 0.3 * jnp.where(halo, land_halo, land_ref[...].astype(F32))
    land_out[...] = deposit
    last_lat = lat == lat_count - 1

    def assemble(z, sums):
        shift = shift_of(z)
        shift_0 = lax.rem(shift + jnp.where(core == 0, 4, 124), 128)
        for t in range(9):
            c_first[t, z, 8:24, :] = jnp.where(halo, lane_roll(p_s[t], shift), c_own[t, z, 8:24, :])
            traj_out[1, t, z] = jnp.where(halo_16, lane_roll(lon_ref[33 + t], shift), traj_own[1, t, z])
            traj_out[0, t, z] = jnp.where(halo_16, lane_roll(lon_ref[33 + t], shift_0), traj_own[0, t, z])
        north = jnp.where(halo, lane_roll(p_s[9], shift), wind_own[1, z])
        north = jnp.where((row == 15) & last_lat, 0.0, north)
        east = jnp.where(halo, lane_roll(p_s[10], shift), wind_own[0, z])
        mix = jnp.where(halo, jnp.abs(lane_roll(p_s[11], shift)), mix_own[z])
        n_out[z, 0:8, :] = zero[:8]
        n_out[z, 8:24, :] = north
        n_out[z, 24:32, :] = zero[:8]
        e_out[z] = east
        d_out[z + 1] = jnp.where(z == 15, 0.0, mix)
        return sums

    def weigh(z, sums):
        shifted = [n_out[z, 6 + j : 22 + j, :] for j in range(4)]
        for j, value in enumerate(weights(e_out[z], shifted)):
            w_s[j, z] = value
        return sums

    steps = stages(scalars, c_first, w_s, a_s, b_s, traj_out, 1, lambda z: d_out[z + 1], land_out[...], c_next, 2)
    sums = pipeline([(0, assemble), (1, weigh)] + steps, no_sums())
    sums = total(lat_count, 1, sums)
    for m in range(3):
        em_ref[m] = em_in[m] + sums[m]


def stages(scalars, c_in, w_ref, a_s, b_s, traj_ref, k, d, deposit, c_out, lag):
    def move(z, sums):
        moved(c_in, w_ref, a_s, z)
        return sums

    def do_react(z, sums):
        return react(scalars, lambda t: traj_ref[k, t, z], lambda t, rows: a_s[t, z, rows, :], b_s, z, sums)

    def mix(z, sums):
        mixed(scalars, b_s, d, deposit, c_out, z)
        return sums

    return [(lag, move), (lag + 1, do_react), (lag + 3, mix)]


def third_kernel(lat_count, *refs):
    traj_ref, d_ref, land_ref, w_ref, c_in, em_in = refs[0:6]
    scalars = refs[6:11]
    c_next, out_ref, em_ref = refs[11:14]
    a_s, b_s = refs[14:]
    zero_rows(c_next, 16)
    zero_ends(b_s)
    steps = stages(scalars, c_in, w_ref, a_s, b_s, traj_ref, 0, lambda z: d_ref[z + 1], land_ref[...], c_next, 0)

    def last(z, sums):
        moved(c_next, w_ref, out_ref, z)
        return sums

    sums = pipeline(steps + [(4, last)], no_sums())
    sums = total(lat_count, 2, sums)
    for m in range(3):
        em_ref[m] = em_in[m] + sums[m]


def edge_kernel(lat_count, *refs):
    edges = 1 if lat_count == 2 else 2
    traj_ref, c_first, c_next, n_ref, e_ref, d_ref, land_ref, c_last, out_ref, em_ref = refs[0:10]
    lat_refs = refs[10 : 10 + 2 * edges]
    corner_refs = refs[10 + 2 * edges : 10 + 3 * edges]
    rate_ref, speed_ref, class_ref, prof_ref, coef_ref = refs[10 + 3 * edges : 15 + 3 * edges]
    keep_ref, send_ref = refs[15 + 3 * edges : 17 + 3 * edges]
    b_0, b_1, c_0, c_1, c_2, t_s, n_s, e_s, d_s, l_s, a_s, em_s, fin_s = refs[17 + 3 * edges :]
    core = lax.axis_index("lev")
    lat = lax.axis_index("lat")
    edge = jnp.where(core == 0, 120, 0)
    flip = 1 - core
    halo = halo_lanes(core, 8)
    sub = iota((8, 128), 0)
    zero = jnp.zeros((8, 128), F32)

    def rolled(value, shift):
        return pltpu.roll(value, shift, 0)

    def run(upper, e):
        own_at, halo_at = (0, 8) if upper else (8, 0)
        own_row = 8 if upper else 0
        corner_ref = corner_refs[e]
        keep = (sub < 6) if upper else (sub >= 2)
        starts = (6, 4, 0) if upper else (2, 4, 8)
        b_bufs, c_bufs = (b_0, b_1, b_0), (c_0, c_1, c_2)

        def shift_of(z):
            return lax.rem(edge + 128 - 8 * jnp.bitwise_xor(z, 8 * flip), 128)

        def corner(tile, z):
            return lane_roll(halves(corner_ref[tile])[0 if upper else 1], shift_of(z))

        def corner_sum(f, z):
            high = halves(corner_ref[2 * f])[0 if upper else 1]
            low = halves(corner_ref[2 * f + 1])[0 if upper else 1]
            return lane_roll(high + low, shift_of(z))

        land_c = corner_sum(11, 0)
        land_l = jnp.where(core == 0, sum(halves(lat_refs[2 * e][124])), sum(halves(lat_refs[2 * e + 1][124])))
        l_s[pl.ds(halo_at, 8), :] = 0.1 + 0.3 * (jnp.where(halo, land_c, land_l) < 0).astype(F32)
        l_s[pl.ds(own_at, 8), :] = land_ref[pl.ds(own_row, 8), :]
        d_s[0] = jnp.zeros((16, 128), F32)

        def pads(t, _):
            for b in (b_0, b_1):
                b[t, 0] = zero
                b[t, 17] = zero
            for c in c_bufs:
                for z in range(16):
                    c[t, z, 0:8, :] = zero
                    c[t, z, 24:32, :] = zero
            return 0

        lax.fori_loop(0, 9, pads, 0)

        for s in range(2):
            msg = lat_refs[2 * e + s]

            def receive(pair, _):
                for i in range(2):
                    l = 2 * pair + i
                    z = 8 * jnp.bitwise_xor(s, core) + l
                    rate = [rate_ref[q, z] for q in range(6)]
                    adj, state = [], []
                    for t in range(9):
                        v0, v1 = halves(msg[t * 8 + l])
                        v2 = halves(msg[72 + t * 4 + pair])[i]
                        adj.append(jnp.where(halo, corner_sum(t, z), jnp.where(keep, v0 + v1, 0.0)))
                        tr2, tr1 = corner(24 + t, z), corner(33 + t, z)
                        tr0 = lane_roll(tr1, jnp.where(core == 0, 4, 124))
                        state.append(jnp.where(halo, tr2, v2))
                        if upper:
                            own1 = jnp.where(sub < 2, rolled(v1, 2), rolled(v2, 4))
                            own0 = rolled(v0, 2)
                        else:
                            own1 = jnp.where(sub >= 6, rolled(v1, 6), rolled(v2, 4))
                            own0 = rolled(v0, 6)
                        t_s[1, t, z, pl.ds(halo_at, 8), :] = jnp.where(halo, tr1, own1)
                        t_s[0, t, z, pl.ds(halo_at, 8), :] = jnp.where(halo, tr0, own0)
                        near = 1 if upper else 0
                        t_s[1, t, z, pl.ds(own_at, 8), :] = halves(traj_ref[1, t, z])[near]
                        t_s[0, t, z, pl.ds(own_at, 8), :] = halves(traj_ref[0, t, z])[near]
                    done = coag(adj, state, rate)
                    for t in range(9):
                        b_0[t, z + 1] = done[t]
                    winds = []
                    for q in range(3):
                        high, low = halves(msg[108 + q * 8 + l])
                        winds.append(jnp.where(halo, corner_sum(9 + q, z), high + low))
                    n_s[z, 0:8, :] = zero
                    n_s[z, 24:32, :] = zero
                    n_s[z, pl.ds(8 + halo_at, 8), :] = winds[0]
                    n_s[z, pl.ds(8 + own_at, 8), :] = n_ref[z, pl.ds(8 + own_row, 8), :]
                    e_s[z, pl.ds(halo_at, 8), :] = winds[1]
                    e_s[z, pl.ds(own_at, 8), :] = e_ref[z, pl.ds(own_row, 8), :]
                    d_s[z + 1, pl.ds(halo_at, 8), :] = jnp.where(z == 15, 0.0, jnp.abs(winds[2]))
                    d_s[z + 1, pl.ds(own_at, 8), :] = d_ref[z + 1, pl.ds(own_row, 8), :]
                return 0

            lax.fori_loop(0, 4, receive, 0)

        for m in range(3):
            for part in range(3):
                em_s[m, 8 * part : 8 * part + 8, :] = zero

        def mix(step, z):
            at = halo_at if step == 0 else starts[step - 1]
            b, c = b_bufs[step], c_bufs[step]
            c_ref = (c_first, c_next, c_last)[step]
            kind = class_ref[z]
            below, above = d_s[z, at : at + 8, :], d_s[z + 1, at : at + 8, :]
            base = 1.0 - above - below
            base = jnp.where(z == 0, base - l_s[at : at + 8, :], base)
            for t in range(9):
                speed = speed_ref[kind, t]
                value = b[t, z + 1] * (base - speed) + b[t, z] * (below + speed) + b[t, z + 2] * above
                c[t, z, 8 + own_at : 16 + own_at, :] = c_ref[t, z, 8 + own_row : 16 + own_row, :]
                c[t, z, 8 + at : 16 + at, :] = value

        def move(step, z, sums):
            at = starts[step]
            c = c_bufs[step]
            shifted = [n_s[z, 6 + at + i : 14 + at + i, :] for i in range(4)]
            w = weights(e_s[z, at : at + 8, :], shifted)
            adj = []
            for t in range(9):
                rows = [c[t, z, 6 + at + i : 14 + at + i, :] for i in range(5)]
                adj.append(transported(rows, w))
            if step == 2:
                for t in range(9):
                    fin_s[e, t, z] = adj[t]
                return sums
            share = [prof_ref[z] * coef_ref[t] for t in range(9)]
            sums = [sums[m] + sum(share[3 * m + j] * adj[3 * m + j] for j in range(3)) for m in range(3)]
            rate = [rate_ref[q, z] for q in range(6)]
            state = [t_s[1 - step, t, z, at : at + 8, :] for t in range(9)]
            done = coag(adj, state, rate)
            for t in range(9):
                b_bufs[step + 1][t, z + 1] = done[t]
            return sums

        def count(step, sums):
            at = starts[step]
            buf_row = sub + at
            rows = 2 + 2 * step
            if upper:
                good = (buf_row >= 8 - rows) & (buf_row < 8)
            else:
                good = (buf_row >= 8) & (buf_row < 8 + rows)
            for m in range(3):
                em_s[m, at : at + 8, :] = em_s[m, at : at + 8, :] + jnp.where(good, sums[m], 0.0)

        none = [zero, zero, zero]

        def mixing(step):
            def stage(z, sums):
                mix(step, z)
                return sums

            return stage

        def moving(step):
            return lambda z, sums: move(step, z, sums)

        count(0, pipeline([(0, mixing(0)), (1, moving(0)), (3, mixing(1))], none))
        count(1, pipeline([(0, moving(1)), (2, mixing(2)), (3, moving(2))], none))
        for m in range(3):
            a_s[e, m] = em_s[m, own_at : own_at + 8, :]

    def finish(has_upper, has_lower, e_upper, e_lower):
        mine = (iota((16, 128), 1) < 64) == (core == 0)
        row8 = sub

        def rows_of(t, z):
            low = out_ref[t, z, 0:8, :]
            high = out_ref[t, z, 8:16, :]
            if has_upper:
                high = jnp.where(row8 >= 2, fin_s[e_upper, t, z], high)
            if has_lower:
                low = jnp.where(row8 < 6, fin_s[e_lower, t, z], low)
            return stack_rows(low, high)

        def tracer(t, _):
            for l in range(8):
                keep_ref[t, l] = rows_of(t, 8 * core + l)
            for l in range(4):
                z = 8 * (1 - core) + l
                send_ref[t * 4 + l] = jnp.where(mine, rows_of(t, z), lane_roll(rows_of(t, z + 4), 64))
            return 0

        lax.fori_loop(0, 9, tracer, 0)
        for m in range(3):
            low = em_ref[m, 0:8, :]
            high = em_ref[m, 8:16, :]
            if has_upper:
                high = high + a_s[e_upper, m]
            if has_lower:
                low = low + a_s[e_lower, m]
            send_ref[36 + m] = stack_rows(low, high)

    if lat_count == 2:

        def south():
            run(True, 0)
            finish(True, False, 0, 0)

        def north():
            run(False, 0)
            finish(False, True, 0, 0)

        pl.when(lat == 0)(south)
        pl.when(lat == 1)(north)
    else:
        run(True, 0)
        run(False, 1)
        finish(True, True, 0, 1)


def join_kernel(keep_ref, send_ref, recv_ref, source_ref, out_ref, em_ref):
    core = lax.axis_index("lev")
    mine = (iota((16, 128), 1) < 64) == (core == 0)

    def tracer(t, _):
        for l in range(4):
            got = recv_ref[t * 4 + l]
            out_ref[t, l] = jnp.where(mine, keep_ref[t, l], got)
            out_ref[t, l + 4] = jnp.where(mine, keep_ref[t, l + 4], lane_roll(got, 64))
        return 0

    lax.fori_loop(0, 9, tracer, 0)
    source = source_ref[...].astype(F32)
    for m in range(3):
        em_ref[m] = jnp.where(mine, send_ref[36 + m], recv_ref[36 + m]) * source


def shape(*dims, dtype=F32):
    return jax.ShapeDtypeStruct(dims, dtype)


def call(kernel, outs, scratch, *args, specs=None, mib=32):
    return pl.pallas_call(
        kernel,
        out_shape=outs,
        in_specs=specs or [VMEM] * len(args),
        out_specs=[VMEM] * len(outs),
        scratch_shapes=scratch,
        compiler_params=pltpu.CompilerParams(vmem_limit_bytes=mib * 1024 * 1024),
    )(*args)


def shards(
    adjoint_in,
    trajectory,
    courant,
    mixing,
    coag_rates,
    settle_speed,
    settle_class,
    emis_profile,
    emis_coef,
    land_mask,
    source_mask,
):
    lat_count = lax.axis_size("lat")
    lon_count = lax.axis_size("lon")
    edges = 1 if lat_count == 2 else 2
    swap = [(0, 1), (1, 0)]

    def over_lev(value):
        return lax.ppermute(value, "lev", swap)

    def lat_moves(messages):
        if edges == 1:
            return [lax.ppermute(messages[0], "lat", swap)]
        up = [(j, j + 1) for j in range(lat_count - 1)]
        down = [(j + 1, j) for j in range(lat_count - 1)]
        return [lax.ppermute(messages[-1], "lat", down), lax.ppermute(messages[0], "lat", up)]

    def bind(kernel):
        def run(*refs):
            return kernel(lat_count, *refs)

        return run

    given = (adjoint_in, trajectory, courant, mixing)
    other = tuple(over_lev(value) for value in given)
    *own, land = call(
        load_kernel,
        [jax.ShapeDtypeStruct(v.shape, v.dtype) for v in given + (land_mask,)],
        [pltpu.SemaphoreType.DMA((5,))],
        *[pltpu.with_memory_space_constraint(v, pltpu.HBM) for v in given + (land_mask,)],
        specs=[pl.BlockSpec(memory_space=pltpu.HBM)] * 5,
        mib=16,
    )
    (lon_out,) = call(
        bind(lon_pack_kernel), [shape(LON_TILES, 16, 128, dtype=BF16)], [], *own, *other, land, mib=16
    )
    *own, lon_out = lax.optimization_barrier((*own, lon_out))
    lat_out = call(
        bind(lat_pack_kernel), [shape(LAT_TILES, 16, 128, dtype=BF16)] * edges, [], *own, land, mib=16
    )
    lat_in = lat_moves(lat_out)
    lon_pairs = []
    for i in range(lon_count):
        lon_pairs.append((2 * i + 1, 2 * ((i + 1) % lon_count)))
        lon_pairs.append((2 * i, 2 * ((i - 1) % lon_count) + 1))
    lon_in = lax.ppermute(lon_out, ("lon", "lev"), lon_pairs)
    scalars = (coag_rates, settle_speed, settle_class, emis_profile, emis_coef)
    state = pltpu.VMEM((9, 16, 16, 128), F32)
    between = pltpu.VMEM((9, 18, 16, 128), F32)
    padded = shape(9, 16, 32, 128)
    c_own, emis, traj_own, wind_own, mix_own = call(
        bind(first_kernel),
        [
            padded,
            shape(3, 16, 128),
            shape(2, 9, 16, 16, 128, dtype=BF16),
            shape(2, 16, 16, 128),
            shape(16, 16, 128),
        ],
        [between],
        *own,
        *other,
        land,
        *scalars,
        specs=[VMEM] * 9 + [SMEM] * 5,
    )
    lon_in, c_own = lax.optimization_barrier((lon_in, c_own))
    corner_in = lat_moves([lon_in])
    traj_all, c_first, c_next, north, east, mix, land_all, weight, emis = call(
        bind(second_kernel),
        [
            shape(2, 9, 16, 16, 128, dtype=BF16),
            padded,
            padded,
            shape(16, 32, 128),
            shape(16, 16, 128),
            shape(17, 16, 128),
            shape(16, 128),
            shape(9, 16, 16, 128),
            shape(3, 16, 128),
        ],
        [state, between, pltpu.VMEM((12, 16, 128), F32)],
        land,
        lon_in,
        c_own,
        emis,
        traj_own,
        wind_own,
        mix_own,
        *scalars,
        specs=[VMEM] * 7 + [SMEM] * 5,
    )
    c_next, *lat_in = lax.optimization_barrier((c_next, *lat_in))
    c_last, final, emis = call(
        bind(third_kernel),
        [padded, shape(9, 16, 16, 128), shape(3, 16, 128)],
        [state, between],
        traj_all,
        mix,
        land_all,
        weight,
        c_next,
        emis,
        *scalars,
        specs=[VMEM] * 6 + [SMEM] * 5,
    )
    inner = (traj_all, c_first, c_next, north, east, mix, land_all, c_last, final, emis)
    lat_all = []
    for value in lat_in:
        lat_all += [value, over_lev(value)]
    keep, send = call(
        bind(edge_kernel),
        [shape(9, 8, 16, 128), shape(39, 16, 128)],
        [
            pltpu.VMEM((9, 18, 8, 128), F32),
            pltpu.VMEM((9, 18, 8, 128), F32),
            pltpu.VMEM((9, 16, 32, 128), F32),
            pltpu.VMEM((9, 16, 32, 128), F32),
            pltpu.VMEM((9, 16, 32, 128), F32),
            pltpu.VMEM((2, 9, 16, 16, 128), F32),
            pltpu.VMEM((16, 32, 128), F32),
            pltpu.VMEM((16, 16, 128), F32),
            pltpu.VMEM((17, 16, 128), F32),
            pltpu.VMEM((16, 128), F32),
            pltpu.VMEM((edges, 3, 8, 128), F32),
            pltpu.VMEM((3, 24, 128), F32),
            pltpu.VMEM((edges, 9, 16, 8, 128), F32),
        ],
        *inner,
        *lat_all,
        *corner_in,
        *scalars,
        specs=[VMEM] * (10 + 3 * edges) + [SMEM] * 5,
        mib=40,
    )
    recv = over_lev(send)
    out, emis = call(
        join_kernel, [shape(9, 8, 16, 128), shape(3, 16, 128)], [], keep, send, recv, source_mask
    )
    return (out, emis)


def solution(mesh):
    return jax.shard_map(
        shards,
        mesh=mesh,
        in_specs=(
            P(None, "lev", "lat", "lon"),
            P(None, None, "lev", "lat", "lon"),
            P(None, "lev", "lat", "lon"),
            P("lev", "lat", "lon"),
            P(),
            P(),
            P(),
            P(),
            P(),
            P("lat", "lon"),
            P("lat", "lon"),
        ),
        out_specs=(P(None, "lev", "lat", "lon"), P(None, "lat", "lon")),
        check_vma=False,
    )
```

```python
import jax
import jax.numpy as jnp
from jax import lax
from jax.experimental import pallas as pl
from jax.experimental.pallas import tpu as pltpu
from jax.sharding import PartitionSpec as P

F32 = jnp.float32
BF16 = jnp.bfloat16
VMEM = pl.BlockSpec(memory_space=pltpu.VMEM)
SMEM = pl.BlockSpec(memory_space=pltpu.SMEM)
PAIRS = ((0, 1, 3), (0, 2, 4), (1, 2, 5))
LAT_TILES = 132
LON_TILES = 21


def iota(shape, axis):
    return lax.broadcasted_iota(jnp.int32, shape, axis)


def split(value):
    high = value.astype(BF16)
    low = (value - high.astype(F32)).astype(BF16)
    return high, low


def stack_rows(top, bottom):
    return jnp.concatenate([top, bottom], axis=0)


def halves(tile):
    wide = tile.astype(F32)
    return wide[:8], wide[8:]


def coag(adj, state, rate):
    out = list(adj)
    kn = {}
    for m, p, q in PAIRS:
        kn[m, p] = rate[q] * state[3 * p]
    for m in range(3):
        total = (2.0 * rate[m]) * state[3 * m]
        for p in range(m + 1, 3):
            total = total + kn[m, p]
        out[3 * m] = out[3 * m] - total * adj[3 * m]
        out[3 * m + 1] = out[3 * m + 1] + (2.0 * rate[m]) * (state[3 * m + 1] * adj[3 * m + 2])
    for m, p, q in PAIRS:
        d_vol = adj[3 * p + 1] - adj[3 * m + 1]
        d_six = adj[3 * p + 2] - adj[3 * m + 2]
        inner = d_vol * state[3 * m + 1] + d_six * state[3 * m + 2] - adj[3 * m] * state[3 * m]
        cross = (2.0 * rate[q]) * adj[3 * p + 2]
        out[3 * p] = out[3 * p] + rate[q] * inner
        out[3 * m + 1] = out[3 * m + 1] + (kn[m, p] * d_vol + cross * state[3 * p + 1])
        out[3 * p + 1] = out[3 * p + 1] + cross * state[3 * m + 1]
        out[3 * m + 2] = out[3 * m + 2] + kn[m, p] * d_six
    return out


def lane_roll(value, shift):
    return pltpu.roll(value, shift, 1)


def weights(east, north):
    pos = jnp.maximum(east, 0.0)
    neg = jnp.minimum(east, 0.0)
    pos_1 = lane_roll(pos, 127)
    neg_1 = lane_roll(neg, 1)
    neg_2 = lane_roll(neg, 2)
    n_pos = jnp.maximum(north[2], 0.0)
    n_pos_1 = jnp.maximum(north[3], 0.0)
    n_neg_1 = jnp.minimum(north[1], 0.0)
    n_neg_2 = jnp.minimum(north[0], 0.0)
    centre = 1.0 + 1.5 * ((neg_1 - pos) + (n_neg_1 - n_pos))
    return (
        centre,
        0.5 * neg_2,
        -1.5 * neg_1 - 0.5 * neg_2,
        1.5 * pos + 0.5 * pos_1,
        -0.5 * pos_1,
        0.5 * n_neg_2,
        -1.5 * n_neg_1 - 0.5 * n_neg_2,
        1.5 * n_pos + 0.5 * n_pos_1,
        -0.5 * n_pos_1,
    )


def transported(rows, w):
    mid = rows[2]
    lon = (w[1] * lane_roll(mid, 2) + w[2] * lane_roll(mid, 1)) + (
        w[3] * lane_roll(mid, 127) + w[4] * lane_roll(mid, 126)
    )
    lat = (w[5] * rows[0] + w[6] * rows[1]) + (w[7] * rows[3] + w[8] * rows[4])
    return w[0] * mid + (lon + lat)


def level_scalars(z, rate_ref, speed_ref, class_ref):
    rate = [rate_ref[q, z] for q in range(6)]
    kind = class_ref[z]
    speed = [speed_ref[kind, t] for t in range(9)]
    return rate, speed


def halo_lanes(core, rows):
    lane = iota((rows, 128), 1)
    return jnp.where(core == 0, (lane >= 120).astype(jnp.int32), (lane < 8).astype(jnp.int32)) > 0


def load_kernel(*refs):
    given, kept, sems = refs[0:5], refs[5:10], refs[10]
    copies = [pltpu.make_async_copy(given[i], kept[i], sems.at[i]) for i in range(5)]
    for copy in copies:
        copy.start()
    for copy in copies:
        copy.wait()


def marked(mix, land, z):
    return jnp.where((land * (z == 0).astype(jnp.int32)) > 0, -mix, mix)


def lat_pack_kernel(lat_count, adj_ref, traj_ref, wind_ref, mix_ref, land_ref, *outs):
    core = lax.axis_index("lev")
    lat = lax.axis_index("lat")

    def fill(out_ref, high_rows):
        base = 8 if high_rows else 0
        sub = iota((8, 128), 0)
        keep = (sub >= 2) if high_rows else (sub < 6)

        def rolled(value, shift):
            return pltpu.roll(value, shift, 0)

        def tracer(t, _):
            v2s = []
            for l in range(8):
                adj = adj_ref[t, l, base : base + 8, :]
                high = adj.astype(BF16).astype(F32)
                low = adj - high
                tr = [traj_ref[k, t, l].astype(F32)[base : base + 8] for k in range(3)]
                if high_rows:
                    extra = (rolled(tr[0], 2), rolled(tr[1], 2), rolled(tr[1], 4))
                else:
                    extra = (rolled(tr[0], 6), rolled(tr[1], 6), rolled(tr[1], 4))
                v0 = jnp.where(keep, high, extra[0])
                v1 = jnp.where(keep, low, extra[1])
                v2s.append(jnp.where(keep, tr[2], extra[2]))
                out_ref[t * 8 + l] = stack_rows(v0, v1).astype(BF16)
            for j in range(4):
                out_ref[72 + t * 4 + j] = stack_rows(v2s[2 * j], v2s[2 * j + 1]).astype(BF16)
            return 0

        lax.fori_loop(0, 9, tracer, 0)

        def level(l, _):
            for q in range(3):
                if q == 2:
                    value = marked(mix_ref[l, base : base + 8, :], land_ref[base : base + 8, :], l + 8 * core)
                else:
                    value = wind_ref[1 - q, l, base : base + 8, :]
                high = value.astype(BF16).astype(F32)
                out_ref[108 + q * 8 + l] = stack_rows(high, value - high).astype(BF16)
            return 0

        lax.fori_loop(0, 8, level, 0)

    if lat_count == 2:
        pl.when(lat == 0)(lambda: fill(outs[0], True))
        pl.when(lat == 1)(lambda: fill(outs[0], False))
    else:
        fill(outs[0], True)
        fill(outs[1], False)


def lon_pack_kernel(lat_count, *refs):
    own, other = refs[0:4], refs[4:8]
    land_ref = refs[8]
    out_ref = refs[9]
    core = lax.axis_index("lev")
    edge = jnp.where(core == 0, 0, 120)
    lane = iota((16, 128), 1)
    slot = lane // 8
    slot_16 = slot.astype(BF16)
    far = (jnp.bitwise_xor((lane // 4) % 2, core)).astype(F32).astype(BF16)
    zero_32 = jnp.zeros((16, 128), F32)
    zero_16 = jnp.zeros((16, 128), BF16)

    def gather(read, zero, at):
        acc = zero
        for s in range(2):
            for l in range(8):
                g = 8 * s + l
                shift = lax.rem(8 * g - edge + 128, 128)
                acc = jnp.where(at == g, lane_roll(read((own, other)[s], l, jnp.bitwise_xor(s, core)), shift), acc)
        return acc

    def emit(f, value):
        high, low = split(value)
        pair(f, high, low)

    def pair(f, first, second):
        tops, bottoms = halves(first), halves(second)
        for h in range(2):
            out_ref[h, f] = stack_rows(tops[h], bottoms[h]).astype(BF16)

    def tracer(t, _):
        emit(t, gather(lambda r, l, h: r[0][t, l], zero_32, slot))
        tr = [gather(lambda r, l, h: r[1][k, t, l], zero_16, slot_16) for k in range(3)]
        both = jnp.where(far > 0, lane_roll(tr[0], jnp.where(core == 0, 4, 124)), tr[1])
        pair(12 + t, tr[2], both)
        return 0

    for t in range(9):
        tracer(t, 0)
    emit(9, gather(lambda r, l, h: r[2][1, l], zero_32, slot))
    emit(10, gather(lambda r, l, h: r[2][0, l], zero_32, slot))
    land = land_ref[...]
    emit(11, gather(lambda r, l, h: marked(r[3][l], land, l + 8 * h) if l == 0 else r[3][l], zero_32, slot))


def put_rows(ref, t, z, value):
    zero = jnp.zeros((8, 128), F32)
    ref[t, z, 0:8, :] = zero
    ref[t, z, 8:24, :] = value
    ref[t, z, 24:32, :] = zero


def zero_ends(ref):
    for t in range(9):
        for z in (0, 17):
            ref[t, z] = jnp.zeros(ref.shape[2:], F32)


def react(scalars, traj, a_in, b_s, z, sums):
    rate_ref, speed_ref, class_ref, prof_ref, coef_ref = scalars
    rate = [rate_ref[q, z] for q in range(6)]
    share = [prof_ref[z] * coef_ref[t] for t in range(9)]
    tiles = [traj(t).astype(F32) for t in range(9)]
    parts = []
    for rb in range(2):
        rows = slice(8 * rb, 8 * rb + 8)
        adj = [a_in(t, rows) for t in range(9)]
        done = coag(adj, [tile[rows] for tile in tiles], rate)
        for t in range(9):
            b_s[t, z + 1, rows, :] = done[t]
        parts.append([sums[rb][m] + sum(share[3 * m + j] * adj[3 * m + j] for j in range(3)) for m in range(3)])
    return parts


def mixed(scalars, b_s, d, deposit, put, z):
    rate_ref, speed_ref, class_ref, prof_ref, coef_ref = scalars
    kind = class_ref[z]
    below, above = d(z - 1), d(z)
    base = 1.0 - above - below
    base = jnp.where(z == 0, base - deposit, base)
    for t in range(9):
        speed = speed_ref[kind, t]
        put(t, z, b_s[t, z + 1] * (base - speed) + b_s[t, z] * (below + speed) + b_s[t, z + 2] * above)


def moved(c_in, w_ref, a_to, z):
    for rb in range(2):
        rows = slice(8 * rb, 8 * rb + 8)
        w = [w_ref[i, z, rows, :] for i in range(9)]
        for t in range(9):
            shifted = [c_in[t, z, 8 * rb + 6 + i : 8 * rb + 14 + i, :] for i in range(5)]
            a_to[t, z, rows, :] = transported(shifted, w)


def no_sums():
    return [[jnp.zeros((8, 128), F32)] * 3, [jnp.zeros((8, 128), F32)] * 3]


def total(lat_count, step, sums):
    lat = lax.axis_index("lat")
    row = iota((16, 128), 0)
    sums = [stack_rows(sums[0][m], sums[1][m]) for m in range(3)]
    if step == 0:
        return sums
    low, high = 2 * step, 15 - 2 * step
    if lat_count == 2:
        good = ((row <= high) | (lat != 0)) & ((row >= low) | (lat == 0))
    else:
        good = (row <= high) & (row >= low)
    return [jnp.where(good, v, 0.0) for v in sums]


def pipeline(stages, carry=None):
    stages = sorted(stages, key=lambda stage: -stage[0])
    depth = stages[0][0]

    def at(z, carry):
        for lag, stage in stages:
            if 0 <= z - lag < 16:
                carry = stage(z - lag, carry)
        return carry

    for z in range(depth):
        carry = at(z, carry)
    for z in range(depth, 16 + depth):
        carry = at(z, carry)
    return carry


def first_kernel(lat_count, *refs):
    own, other = refs[0:4], refs[4:8]
    land_ref = refs[8]
    scalars = refs[9:14]
    c_out, em_ref, traj_out, wind_out, mix_out = refs[14:19]
    b_s = refs[19]
    core = lax.axis_index("lev")
    zero_ends(b_s)
    deposit = 0.1 + 0.3 * land_ref[...].astype(F32)
    nothing = jnp.zeros((16, 128), F32)

    def put(t, z, value):
        c_out[t, z] = value

    def run(low, high):
        def level(r, z, l, sums):
            for k in range(2):
                for t in range(9):
                    traj_out[k, t, z] = r[1][k, t, l]
            for i in range(2):
                wind_out[i, z] = r[2][i, l]
            mix_out[z] = r[3][l]
            return react(scalars, lambda t: r[1][2, t, l], lambda t, rows: r[0][t, l, rows, :], b_s, z, sums)

        def mix(z):
            def d(i):
                if isinstance(i, int) and i in (-1, 15):
                    return nothing
                return mix_out[i]

            mixed(scalars, b_s, d, deposit, put, z)

        sums = no_sums()
        for z in range(3):
            sums = level(low, z, z, sums)
        mix(0)

        def lower(z, sums):
            mix(z - 2)
            return level(low, z, z, sums)

        sums = lax.fori_loop(3, 8, lower, sums)

        def upper(z, sums):
            mix(z - 2)
            return level(high, z, z - 8, sums)

        sums = lax.fori_loop(8, 16, upper, sums)
        mix(14)
        mix(15)
        sums = total(lat_count, 0, sums)
        for m in range(3):
            em_ref[m] = sums[m]

    pl.when(core == 0)(lambda: run(own, other))
    pl.when(core == 1)(lambda: run(other, own))


def second_kernel(lat_count, *refs):
    land_ref, lon_ref, c_own, em_in, traj_own, wind_own, mix_own = refs[0:7]
    scalars = refs[7:12]
    rate_ref, speed_ref, class_ref, prof_ref, coef_ref = scalars
    traj_out, c_first, c_next, n_out, e_out, d_out, land_out, w_s, em_ref = refs[12:21]
    a_s, b_s, p_s, q_s = refs[21:]
    core = lax.axis_index("lev")
    lat = lax.axis_index("lat")
    edge = jnp.where(core == 0, 120, 0)
    halo = halo_lanes(core, 16)
    edge_f = jnp.where(core == 0, 123.5, 3.5).astype(F32)
    halo_16 = jnp.abs(iota((16, 128), 1).astype(F32) - edge_f).astype(BF16) <= jnp.full((16, 128), 3.5, BF16)
    row = iota((16, 128), 0)
    zero = jnp.zeros((16, 128), F32)
    z_lane = jnp.bitwise_xor(iota((8, 128), 1) // 8, 8 * (1 - core))
    zero_ends(b_s)
    d_out[0] = zero

    def shift_of(z):
        return lax.rem(edge + 128 - 8 * jnp.bitwise_xor(z, 8 * (1 - core)), 128)

    def by_lane(read):
        acc = jnp.zeros((8, 128), F32)
        for z in range(16):
            acc = jnp.where(z_lane == z, read(z), acc)
        return acc

    for f in range(9, 12):
        for h in range(2):
            p_s[f, 8 * h : 8 * h + 8, :] = sum(halves(lon_ref[h, f]))
    for t in range(9):
        q_s[t] = stack_rows(halves(lon_ref[0, 12 + t])[1], halves(lon_ref[1, 12 + t])[1]).astype(BF16)
    rate = [by_lane(lambda z: rate_ref[q, z]) for q in range(6)]
    speeds = [by_lane(lambda z: speed_ref[class_ref[z], t]) for t in range(9)]
    for rb in range(2):
        rows = slice(8 * rb, 8 * rb + 8)
        adj = [sum(halves(lon_ref[rb, t])) for t in range(9)]
        done = coag(adj, [halves(lon_ref[rb, 12 + t])[0] for t in range(9)], rate)
        mark = p_s[11, rows, :]
        land = ((mark < 0) & (z_lane == 0)).astype(F32)
        size = jnp.abs(mark)
        above = jnp.where(z_lane == 15, 0.0, size)
        below = jnp.where(z_lane == 0, 0.0, lane_roll(size, 8))
        base = 1.0 - above - below - jnp.where(z_lane == 0, 0.1 + 0.3 * land, 0.0)
        for t in range(9):
            under = jnp.where(z_lane == 0, 0.0, lane_roll(done[t], 8))
            p_s[t, rows, :] = (
                done[t] * (base - speeds[t]) + under * (below + speeds[t]) + lane_roll(done[t], 120) * above
            )
    land_halo = (lane_roll(p_s[11], shift_of(0)) < 0).astype(F32)
    deposit = 0.1 + 0.3 * jnp.where(halo, land_halo, land_ref[...].astype(F32))
    land_out[...] = deposit
    last_lat = lat == lat_count - 1

    def assemble(z, sums):
        shift = shift_of(z)
        shift_0 = lax.rem(shift + jnp.where(core == 0, 4, 124), 128)
        for t in range(9):
            put_rows(c_first, t, z, jnp.where(halo, lane_roll(p_s[t], shift), c_own[t, z]))
            traj_out[1, t, z] = jnp.where(halo_16, lane_roll(q_s[t], shift), traj_own[1, t, z])
            traj_out[0, t, z] = jnp.where(halo_16, lane_roll(q_s[t], shift_0), traj_own[0, t, z])
        north = jnp.where(halo, lane_roll(p_s[9], shift), wind_own[1, z])
        north = jnp.where((row == 15) & last_lat, 0.0, north)
        east = jnp.where(halo, lane_roll(p_s[10], shift), wind_own[0, z])
        mix = jnp.where(halo, jnp.abs(lane_roll(p_s[11], shift)), mix_own[z])
        n_out[z, 0:8, :] = zero[:8]
        n_out[z, 8:24, :] = north
        n_out[z, 24:32, :] = zero[:8]
        e_out[z] = east
        d_out[z + 1] = jnp.where(z == 15, 0.0, mix)
        return sums

    def weigh(z, sums):
        shifted = [n_out[z, 6 + j : 22 + j, :] for j in range(4)]
        for j, value in enumerate(weights(e_out[z], shifted)):
            w_s[j, z] = value
        return sums

    steps = stages(scalars, c_first, w_s, a_s, b_s, traj_out, 1, lambda z: d_out[z + 1], land_out[...], c_next, 2)
    sums = pipeline([(0, assemble), (1, weigh)] + steps, no_sums())
    sums = total(lat_count, 1, sums)
    for m in range(3):
        em_ref[m] = em_in[m] + sums[m]


def stages(scalars, c_in, w_ref, a_s, b_s, traj_ref, k, d, deposit, c_out, lag):
    def move(z, sums):
        moved(c_in, w_ref, a_s, z)
        return sums

    def do_react(z, sums):
        return react(scalars, lambda t: traj_ref[k, t, z], lambda t, rows: a_s[t, z, rows, :], b_s, z, sums)

    def mix(z, sums):
        mixed(scalars, b_s, d, deposit, lambda t, i, value: put_rows(c_out, t, i, value), z)
        return sums

    return [(lag, move), (lag + 1, do_react), (lag + 3, mix)]


def third_kernel(lat_count, *refs):
    traj_ref, d_ref, land_ref, w_ref, c_in, em_in = refs[0:6]
    scalars = refs[6:11]
    c_next, em_ref = refs[11:13]
    a_s, b_s = refs[13:]
    zero_ends(b_s)
    steps = stages(scalars, c_in, w_ref, a_s, b_s, traj_ref, 0, lambda z: d_ref[z + 1], land_ref[...], c_next, 0)
    sums = total(lat_count, 2, pipeline(steps, no_sums()))
    for m in range(3):
        em_ref[m] = em_in[m] + sums[m]


def edge_kernel(lat_count, *refs):
    edges = 1 if lat_count == 2 else 2
    traj_ref, c_first, c_next, n_ref, e_ref, d_ref, land_ref, c_last, w_ref, em_ref = refs[0:10]
    lat_refs = refs[10 : 10 + 2 * edges]
    corner_refs = refs[10 + 2 * edges : 10 + 3 * edges]
    rate_ref, speed_ref, class_ref, prof_ref, coef_ref = refs[10 + 3 * edges : 15 + 3 * edges]
    keep_ref, send_ref = refs[15 + 3 * edges : 17 + 3 * edges]
    b_0, b_1, c_0, c_1, c_2, t_s, n_s, e_s, d_s, l_s, a_s, em_s, fin_s = refs[17 + 3 * edges :]
    far = 2 - edges
    core = lax.axis_index("lev")
    lat = lax.axis_index("lat")
    edge = jnp.where(core == 0, 120, 0)
    flip = 1 - core
    halo = halo_lanes(core, 8)
    sub = iota((8, 128), 0)
    zero = jnp.zeros((8, 128), F32)

    def rolled(value, shift):
        return pltpu.roll(value, shift, 0)

    def run(upper, e):
        own_at, halo_at = (0, 8) if upper else (8, 0)
        own_row = 8 if upper else 0
        corner_ref = corner_refs[e]
        keep = (sub < 6) if upper else (sub >= 2)
        starts = (6, 4, 0) if upper else (2, 4, 8)
        b_bufs, c_bufs = (b_0, b_1, b_0), (c_0, c_1, c_2)

        def shift_of(z):
            return lax.rem(edge + 128 - 8 * jnp.bitwise_xor(z, 8 * flip), 128)

        def corner(tile, z):
            return halves(lane_roll(corner_ref[tile], shift_of(z)))

        def corner_sum(f, z):
            return sum(corner(f, z))

        land_c = corner_sum(11, 0)
        land_l = jnp.where(core == 0, sum(halves(lat_refs[2 * e][124])), sum(halves(lat_refs[2 * e + 1][124])))
        l_s[pl.ds(halo_at, 8), :] = 0.1 + 0.3 * (jnp.where(halo, land_c, land_l) < 0).astype(F32)
        l_s[pl.ds(own_at, 8), :] = land_ref[pl.ds(own_row, 8), :]
        d_s[0] = jnp.zeros((16, 128), F32)

        zero_ends(b_0)
        zero_ends(b_1)

        for s in range(2):
            msg = lat_refs[2 * e + s]

            def receive(pair, _):
                for i in range(2):
                    l = 2 * pair + i
                    z = 8 * jnp.bitwise_xor(s, core) + l
                    rate = [rate_ref[q, z] for q in range(6)]
                    adj, state = [], []
                    for t in range(9):
                        v0, v1 = halves(msg[t * 8 + l])
                        v2 = halves(msg[72 + t * 4 + pair])[i]
                        adj.append(jnp.where(halo, corner_sum(t, z), jnp.where(keep, v0 + v1, 0.0)))
                        tr2, tr1 = corner(12 + t, z)
                        tr0 = lane_roll(tr1, jnp.where(core == 0, 4, 124))
                        state.append(jnp.where(halo, tr2, v2))
                        if upper:
                            own1 = jnp.where(sub < 2, rolled(v1, 2), rolled(v2, 4))
                            own0 = rolled(v0, 2)
                        else:
                            own1 = jnp.where(sub >= 6, rolled(v1, 6), rolled(v2, 4))
                            own0 = rolled(v0, 6)
                        t_s[1, t, z, pl.ds(halo_at, 8), :] = jnp.where(halo, tr1, own1)
                        t_s[0, t, z, pl.ds(halo_at, 8), :] = jnp.where(halo, tr0, own0)
                        near = 1 if upper else 0
                        t_s[1, t, z, pl.ds(own_at, 8), :] = halves(traj_ref[1, t, z])[near]
                        t_s[0, t, z, pl.ds(own_at, 8), :] = halves(traj_ref[0, t, z])[near]
                    done = coag(adj, state, rate)
                    for t in range(9):
                        b_0[t, z + 1] = done[t]
                    winds = []
                    for q in range(3):
                        high, low = halves(msg[108 + q * 8 + l])
                        winds.append(jnp.where(halo, corner_sum(9 + q, z), high + low))
                    if upper:
                        n_s[z, 0:8, :] = n_ref[z, 8:16, :]
                    else:
                        n_s[z, 24:32, :] = n_ref[z, 16:24, :]
                    n_s[z, pl.ds(8 + halo_at, 8), :] = winds[0]
                    n_s[z, pl.ds(8 + own_at, 8), :] = n_ref[z, pl.ds(8 + own_row, 8), :]
                    e_s[z, pl.ds(halo_at, 8), :] = winds[1]
                    e_s[z, pl.ds(own_at, 8), :] = e_ref[z, pl.ds(own_row, 8), :]
                    d_s[z + 1, pl.ds(halo_at, 8), :] = jnp.where(z == 15, 0.0, jnp.abs(winds[2]))
                    d_s[z + 1, pl.ds(own_at, 8), :] = d_ref[z + 1, pl.ds(own_row, 8), :]
                return 0

            lax.fori_loop(0, 4, receive, 0)

        for m in range(3):
            for part in range(3):
                em_s[m, 8 * part : 8 * part + 8, :] = zero

        def mix(step, z):
            at = halo_at if step == 0 else starts[step - 1]
            b, c = b_bufs[step], c_bufs[step]
            c_ref = (c_first, c_next, c_last)[step]
            kind = class_ref[z]
            below, above = d_s[z, at : at + 8, :], d_s[z + 1, at : at + 8, :]
            base = 1.0 - above - below
            base = jnp.where(z == 0, base - l_s[at : at + 8, :], base)
            for t in range(9):
                speed = speed_ref[kind, t]
                value = b[t, z + 1] * (base - speed) + b[t, z] * (below + speed) + b[t, z + 2] * above
                if step < 2:
                    c[t, z, 8 + own_at : 16 + own_at, :] = c_ref[t, z, 8 + own_row : 16 + own_row, :]
                elif upper:
                    c[t, z, 0:16, :] = c_ref[t, z, 8:24, :]
                else:
                    c[t, z, 16:32, :] = c_ref[t, z, 8:24, :]
                c[t, z, 8 + at : 16 + at, :] = value

        def move(step, z, sums):
            at = starts[step]
            c = c_bufs[step]
            shifted = [n_s[z, 6 + at + i : 14 + at + i, :] for i in range(4)]
            w = weights(e_s[z, at : at + 8, :], shifted)
            adj = []
            for t in range(9):
                rows = [c[t, z, 6 + at + i : 14 + at + i, :] for i in range(5)]
                adj.append(transported(rows, w))
            if step == 2:
                for t in range(9):
                    fin_s[e, t, z] = adj[t]
                return sums
            share = [prof_ref[z] * coef_ref[t] for t in range(9)]
            sums = [sums[m] + sum(share[3 * m + j] * adj[3 * m + j] for j in range(3)) for m in range(3)]
            rate = [rate_ref[q, z] for q in range(6)]
            state = [t_s[1 - step, t, z, at : at + 8, :] for t in range(9)]
            done = coag(adj, state, rate)
            for t in range(9):
                b_bufs[step + 1][t, z + 1] = done[t]
            return sums

        def count(step, sums):
            at = starts[step]
            buf_row = sub + at
            rows = 2 + 2 * step
            if upper:
                good = (buf_row >= 8 - rows) & (buf_row < 8)
            else:
                good = (buf_row >= 8) & (buf_row < 8 + rows)
            for m in range(3):
                em_s[m, at : at + 8, :] = em_s[m, at : at + 8, :] + jnp.where(good, sums[m], 0.0)

        none = [zero, zero, zero]

        def mixing(step):
            def stage(z, sums):
                mix(step, z)
                return sums

            return stage

        def moving(step):
            return lambda z, sums: move(step, z, sums)

        count(0, pipeline([(0, mixing(0)), (1, moving(0)), (3, mixing(1))], none))

        def far_moving(z, sums):
            near = 0 if upper else 8
            w = [w_ref[i, z, near : near + 8, :] for i in range(9)]
            for t in range(9):
                rows = [c_last[t, z, near + 6 + i : near + 14 + i, :] for i in range(5)]
                fin_s[1, t, z] = transported(rows, w)
            return sums

        later = [(0, moving(1)), (2, mixing(2)), (3, moving(2))] + [(3, far_moving)] * far
        count(1, pipeline(later, none))
        for m in range(3):
            a_s[e, m] = em_s[m, own_at : own_at + 8, :]

    def finish(has_upper, has_lower, e_upper, e_lower):
        mine = (iota((16, 128), 1) < 64) == (core == 0)

        def rows_of(t, z):
            low = fin_s[e_lower, t, z]
            high = fin_s[e_upper, t, z]
            return stack_rows(low, high)

        def tracer(t, _):
            for l in range(8):
                keep_ref[t, l] = rows_of(t, 8 * core + l)
            for l in range(4):
                z = 8 * (1 - core) + l
                send_ref[t * 4 + l] = jnp.where(mine, rows_of(t, z), lane_roll(rows_of(t, z + 4), 64))
            return 0

        lax.fori_loop(0, 9, tracer, 0)
        for m in range(3):
            low = em_ref[m, 0:8, :]
            high = em_ref[m, 8:16, :]
            if has_upper:
                high = high + a_s[e_upper, m]
            if has_lower:
                low = low + a_s[e_lower, m]
            send_ref[36 + m] = stack_rows(low, high)

    if lat_count == 2:

        def south():
            run(True, 0)
            finish(True, False, 0, 1)

        def north():
            run(False, 0)
            finish(False, True, 1, 0)

        pl.when(lat == 0)(south)
        pl.when(lat == 1)(north)
    else:
        run(True, 0)
        run(False, 1)
        finish(True, True, 0, 1)


def join_kernel(keep_ref, send_ref, recv_ref, source_ref, out_ref, em_ref, part, em_part, sems):
    core = lax.axis_index("lev")
    mine = (iota((16, 128), 1) < 64) == (core == 0)
    source = source_ref[...].astype(F32)
    for m in range(3):
        em_part[m] = jnp.where(mine, send_ref[36 + m], recv_ref[36 + m]) * source
    copies = [pltpu.make_async_copy(em_part, em_ref, sems.at[9])]
    copies[0].start()
    for t in range(9):
        for l in range(4):
            got = recv_ref[t * 4 + l]
            part[t, l] = jnp.where(mine, keep_ref[t, l], got)
            part[t, l + 4] = jnp.where(mine, keep_ref[t, l + 4], lane_roll(got, 64))
        copies.append(pltpu.make_async_copy(part.at[t], out_ref.at[t], sems.at[t]))
        copies[-1].start()
    for copy in copies:
        copy.wait()


def corner_kernel(lon_ref, out_ref):
    out_ref[...] = lon_ref[1 - lax.axis_index("lat")]


def shape(*dims, dtype=F32):
    return jax.ShapeDtypeStruct(dims, dtype)


def call(kernel, outs, scratch, *args, specs=None, out_specs=None, mib=32):
    return pl.pallas_call(
        kernel,
        out_shape=outs,
        in_specs=specs or [VMEM] * len(args),
        out_specs=out_specs or [VMEM] * len(outs),
        scratch_shapes=scratch,
        compiler_params=pltpu.CompilerParams(vmem_limit_bytes=mib * 1024 * 1024),
    )(*args)


def shards(
    adjoint_in,
    trajectory,
    courant,
    mixing,
    coag_rates,
    settle_speed,
    settle_class,
    emis_profile,
    emis_coef,
    land_mask,
    source_mask,
):
    lat_count = lax.axis_size("lat")
    lon_count = lax.axis_size("lon")
    edges = 1 if lat_count == 2 else 2
    swap = [(0, 1), (1, 0)]

    def over_lev(value):
        return lax.ppermute(value, "lev", swap)

    def lat_moves(messages):
        if edges == 1:
            return [lax.ppermute(messages[0], "lat", swap)]
        up = [(j, j + 1) for j in range(lat_count - 1)]
        down = [(j + 1, j) for j in range(lat_count - 1)]
        return [lax.ppermute(messages[-1], "lat", down), lax.ppermute(messages[0], "lat", up)]

    def bind(kernel):
        def run(*refs):
            return kernel(lat_count, *refs)

        return run

    given = (adjoint_in, trajectory, courant, mixing)
    wind_other, mix_other = over_lev(courant), over_lev(mixing)
    other = (over_lev(adjoint_in), over_lev(trajectory), wind_other, mix_other)
    *own, land = call(
        load_kernel,
        [jax.ShapeDtypeStruct(v.shape, v.dtype) for v in given + (land_mask,)],
        [pltpu.SemaphoreType.DMA((5,))],
        *[pltpu.with_memory_space_constraint(v, pltpu.HBM) for v in given + (land_mask,)],
        specs=[pl.BlockSpec(memory_space=pltpu.HBM)] * 5,
        mib=16,
    )
    (lon_out,) = call(
        bind(lon_pack_kernel), [shape(2, LON_TILES, 16, 128, dtype=BF16)], [], *own, *other, land, mib=16
    )
    lat_out = call(
        bind(lat_pack_kernel), [shape(LAT_TILES, 16, 128, dtype=BF16)] * edges, [], *own, land, mib=16
    )
    lat_in = lat_moves(lat_out)
    lon_pairs = []
    for i in range(lon_count):
        lon_pairs.append((2 * i + 1, 2 * ((i + 1) % lon_count)))
        lon_pairs.append((2 * i, 2 * ((i - 1) % lon_count) + 1))
    lon_in = lax.ppermute(lon_out, ("lon", "lev"), lon_pairs)
    scalars = (coag_rates, settle_speed, settle_class, emis_profile, emis_coef)
    state = pltpu.VMEM((9, 16, 16, 128), F32)
    between = pltpu.VMEM((9, 18, 16, 128), F32)
    padded = shape(9, 16, 32, 128)
    c_own, emis, traj_own, wind_own, mix_own = call(
        bind(first_kernel),
        [
            shape(9, 16, 16, 128),
            shape(3, 16, 128),
            shape(2, 9, 16, 16, 128, dtype=BF16),
            shape(2, 16, 16, 128),
            shape(16, 16, 128),
        ],
        [between],
        *own,
        *other,
        land,
        *scalars,
        specs=[VMEM] * 9 + [SMEM] * 5,
    )
    lon_in, c_own = lax.optimization_barrier((lon_in, c_own))
    if edges == 1:
        corner_out = call(corner_kernel, [shape(LON_TILES, 16, 128, dtype=BF16)], [], lon_in, mib=16)
    else:
        corner_out = [lon_in[1], lon_in[0]]
    corner_in = lat_moves(corner_out)
    traj_all, c_first, c_next, north, east, mix, land_all, weight, emis = call(
        bind(second_kernel),
        [
            shape(2, 9, 16, 16, 128, dtype=BF16),
            padded,
            padded,
            shape(16, 32, 128),
            shape(16, 16, 128),
            shape(17, 16, 128),
            shape(16, 128),
            shape(9, 16, 16, 128),
            shape(3, 16, 128),
        ],
        [state, between, pltpu.VMEM((12, 16, 128), F32), pltpu.VMEM((9, 16, 128), BF16)],
        land,
        lon_in,
        c_own,
        emis,
        traj_own,
        wind_own,
        mix_own,
        *scalars,
        specs=[VMEM] * 7 + [SMEM] * 5,
    )
    c_next, *lat_in = lax.optimization_barrier((c_next, *lat_in))
    c_last, emis = call(
        bind(third_kernel),
        [padded, shape(3, 16, 128)],
        [state, between],
        traj_all,
        mix,
        land_all,
        weight,
        c_next,
        emis,
        *scalars,
        specs=[VMEM] * 6 + [SMEM] * 5,
    )
    inner = (traj_all, c_first, c_next, north, east, mix, land_all, c_last, weight, emis)
    lat_all = []
    for value in lat_in:
        lat_all += [value, over_lev(value)]
    keep, send = call(
        bind(edge_kernel),
        [shape(9, 8, 16, 128), shape(39, 16, 128)],
        [
            pltpu.VMEM((9, 18, 8, 128), F32),
            pltpu.VMEM((9, 18, 8, 128), F32),
            pltpu.VMEM((9, 16, 32, 128), F32),
            pltpu.VMEM((9, 16, 32, 128), F32),
            pltpu.VMEM((9, 16, 32, 128), F32),
            pltpu.VMEM((2, 9, 16, 16, 128), F32),
            pltpu.VMEM((16, 32, 128), F32),
            pltpu.VMEM((16, 16, 128), F32),
            pltpu.VMEM((17, 16, 128), F32),
            pltpu.VMEM((16, 128), F32),
            pltpu.VMEM((edges, 3, 8, 128), F32),
            pltpu.VMEM((3, 24, 128), F32),
            pltpu.VMEM((2, 9, 16, 8, 128), F32),
        ],
        *inner,
        *lat_all,
        *corner_in,
        *scalars,
        specs=[VMEM] * (10 + 3 * edges) + [SMEM] * 5,
        mib=40,
    )
    recv = over_lev(send)
    out, emis = call(
        join_kernel,
        [shape(9, 8, 16, 128), shape(3, 16, 128)],
        [pltpu.VMEM((9, 8, 16, 128), F32), pltpu.VMEM((3, 16, 128), F32), pltpu.SemaphoreType.DMA((10,))],
        keep,
        send,
        recv,
        source_mask,
        out_specs=[pl.BlockSpec(memory_space=pltpu.HBM)] * 2,
    )
    return (out, emis)


def solution(mesh):
    return jax.shard_map(
        shards,
        mesh=mesh,
        in_specs=(
            P(None, "lev", "lat", "lon"),
            P(None, None, "lev", "lat", "lon"),
            P(None, "lev", "lat", "lon"),
            P("lev", "lat", "lon"),
            P(),
            P(),
            P(),
            P(),
            P(),
            P("lat", "lon"),
            P("lat", "lon"),
        ),
        out_specs=(P(None, "lev", "lat", "lon"), P(None, "lat", "lon")),
        check_vma=False,
    )
```

```python
import jax
import jax.numpy as jnp
from jax import lax
from jax.experimental import pallas as pl
from jax.experimental.pallas import tpu as pltpu
from jax.sharding import PartitionSpec as P

F32 = jnp.float32
BF16 = jnp.bfloat16
VMEM = pl.BlockSpec(memory_space=pltpu.VMEM)
SMEM = pl.BlockSpec(memory_space=pltpu.SMEM)
PAIRS = ((0, 1, 3), (0, 2, 4), (1, 2, 5))
LAT_TILES = 124
LON_TILES = 21


def iota(shape, axis):
    return lax.broadcasted_iota(jnp.int32, shape, axis)


def split(value):
    high = value.astype(BF16)
    low = (value - high.astype(F32)).astype(BF16)
    return high, low


def stack_rows(top, bottom):
    return jnp.concatenate([top, bottom], axis=0)


def halves(tile):
    wide = tile.astype(F32)
    return wide[:8], wide[8:]


def coag(adj, state, rate):
    out = list(adj)
    kn = {}
    for m, p, q in PAIRS:
        kn[m, p] = rate[q] * state[3 * p]
    for m in range(3):
        total = (2.0 * rate[m]) * state[3 * m]
        for p in range(m + 1, 3):
            total = total + kn[m, p]
        out[3 * m] = out[3 * m] - total * adj[3 * m]
        out[3 * m + 1] = out[3 * m + 1] + (2.0 * rate[m]) * (state[3 * m + 1] * adj[3 * m + 2])
    for m, p, q in PAIRS:
        d_vol = adj[3 * p + 1] - adj[3 * m + 1]
        d_six = adj[3 * p + 2] - adj[3 * m + 2]
        inner = d_vol * state[3 * m + 1] + d_six * state[3 * m + 2] - adj[3 * m] * state[3 * m]
        cross = (2.0 * rate[q]) * adj[3 * p + 2]
        out[3 * p] = out[3 * p] + rate[q] * inner
        out[3 * m + 1] = out[3 * m + 1] + (kn[m, p] * d_vol + cross * state[3 * p + 1])
        out[3 * p + 1] = out[3 * p + 1] + cross * state[3 * m + 1]
        out[3 * m + 2] = out[3 * m + 2] + kn[m, p] * d_six
    return out


def lane_roll(value, shift):
    return pltpu.roll(value, shift, 1)


def weights(east, north):
    pos = jnp.maximum(east, 0.0)
    neg = jnp.minimum(east, 0.0)
    pos_1 = lane_roll(pos, 127)
    neg_1 = lane_roll(neg, 1)
    neg_2 = lane_roll(neg, 2)
    n_pos = jnp.maximum(north[2], 0.0)
    n_pos_1 = jnp.maximum(north[3], 0.0)
    n_neg_1 = jnp.minimum(north[1], 0.0)
    n_neg_2 = jnp.minimum(north[0], 0.0)
    centre = 1.0 + 1.5 * ((neg_1 - pos) + (n_neg_1 - n_pos))
    return (
        centre,
        0.5 * neg_2,
        -1.5 * neg_1 - 0.5 * neg_2,
        1.5 * pos + 0.5 * pos_1,
        -0.5 * pos_1,
        0.5 * n_neg_2,
        -1.5 * n_neg_1 - 0.5 * n_neg_2,
        1.5 * n_pos + 0.5 * n_pos_1,
        -0.5 * n_pos_1,
    )


def transported(rows, w):
    mid = rows[2]
    lon = (w[1] * lane_roll(mid, 2) + w[2] * lane_roll(mid, 1)) + (
        w[3] * lane_roll(mid, 127) + w[4] * lane_roll(mid, 126)
    )
    lat = (w[5] * rows[0] + w[6] * rows[1]) + (w[7] * rows[3] + w[8] * rows[4])
    return w[0] * mid + (lon + lat)


def level_scalars(z, rate_ref, speed_ref, class_ref):
    rate = [rate_ref[q, z] for q in range(6)]
    kind = class_ref[z]
    speed = [speed_ref[kind, t] for t in range(9)]
    return rate, speed


def halo_lanes(core, rows):
    lane = iota((rows, 128), 1)
    return jnp.where(core == 0, (lane >= 120).astype(jnp.int32), (lane < 8).astype(jnp.int32)) > 0


def halo_lanes_16(core):
    middle = jnp.where(core == 0, 123.5, 3.5).astype(F32)
    return jnp.abs(iota((16, 128), 1).astype(F32) - middle).astype(BF16) <= jnp.full((16, 128), 3.5, BF16)


def load_kernel(adj_ref, traj_ref, wind_ref, mix_ref, land_ref, field_out, traj_out, land_out, sems):
    pairs = [(adj_ref.at[pl.ds(3 * i, 3)], field_out.at[pl.ds(3 * i, 3)]) for i in range(3)]
    pairs += [(wind_ref, field_out.at[pl.ds(9, 2)]), (mix_ref, field_out.at[11]), (land_ref, land_out)]
    pairs += [(traj_ref.at[k], traj_out.at[k]) for k in range(3)]
    copies = [pltpu.make_async_copy(source, target, sems.at[i]) for i, (source, target) in enumerate(pairs)]
    for copy in copies:
        copy.start()
    for copy in copies:
        copy.wait()


def parts_of(field_ref, traj_ref):
    return field_ref.at[pl.ds(0, 9)], traj_ref, field_ref.at[pl.ds(9, 2)], field_ref.at[11]


def marked(mix, land, z):
    return jnp.where((land * (z == 0).astype(jnp.int32)) > 0, -mix, mix)


def lat_pack_kernel(lat_count, field_ref, traj_ref, land_ref, *outs):
    adj_ref, traj_ref, wind_ref, mix_ref = parts_of(field_ref, traj_ref)
    core = lax.axis_index("lev")
    lat = lax.axis_index("lat")

    def fill(out_ref, high_rows):
        base = 8 if high_rows else 0
        sub = iota((8, 128), 0)
        keep = (sub >= 2) if high_rows else (sub < 6)

        def rolled(value, shift):
            return pltpu.roll(value, shift, 0)

        def tracer(t, _):
            v2s = []
            for l in range(8):
                adj = adj_ref[t, l, base : base + 8, :]
                high = adj.astype(BF16).astype(F32)
                low = adj - high
                tr = [traj_ref[k, t, l].astype(F32)[base : base + 8] for k in range(3)]
                if high_rows:
                    extra = (rolled(tr[0], 2), rolled(tr[1], 2), rolled(tr[1], 4))
                else:
                    extra = (rolled(tr[0], 6), rolled(tr[1], 6), rolled(tr[1], 4))
                v0 = jnp.where(keep, high, extra[0])
                v1 = jnp.where(keep, low, extra[1])
                v2s.append(jnp.where(keep, tr[2], extra[2]))
                out_ref[t * 8 + l] = stack_rows(v0, v1).astype(BF16)
            for j in range(4):
                out_ref[72 + t * 4 + j] = stack_rows(v2s[2 * j], v2s[2 * j + 1]).astype(BF16)
            return 0

        lax.fori_loop(0, 9, tracer, 0)

        def level(l, _):
            rows = slice(base, base + 8)
            z = l + 8 * core
            north, east = wind_ref[1, l, rows, :], wind_ref[0, l, rows, :]
            parts = []
            for value in (north, marked(mix_ref[l, rows, :], land_ref[rows, :], z), east):
                high = value.astype(BF16).astype(F32)
                parts += [high, value - high]
            one, two = (2, 4) if high_rows else (6, 4)
            north_h, north_l, mix_h, mix_l, east_h, east_l = parts
            out_ref[108 + l] = stack_rows(
                jnp.where(keep, north_h, rolled(east_h, one)), jnp.where(keep, north_l, rolled(east_h, two))
            ).astype(BF16)
            out_ref[116 + l] = stack_rows(
                jnp.where(keep, mix_h, rolled(east_l, one)), jnp.where(keep, mix_l, rolled(east_l, two))
            ).astype(BF16)
            return 0

        lax.fori_loop(0, 8, level, 0)

    if lat_count == 2:
        pl.when(lat == 0)(lambda: fill(outs[0], True))
        pl.when(lat == 1)(lambda: fill(outs[0], False))
    else:
        fill(outs[0], True)
        fill(outs[1], False)


def gather_edges(core, s, blocks, land, f_kind, t_kind, f_done, t_done):
    edge = jnp.where(core == 0, 0, 120)
    slot = iota((16, 128), 1) // 8
    slot_16 = slot.astype(BF16)
    adj_ref, traj_ref, wind_ref, mix_ref = blocks

    def gather(read, acc, at):
        for l in range(8):
            g = 8 * s + l
            shift = lax.rem(8 * g - edge + 128, 128)
            acc = jnp.where(at == g, lane_roll(read(l), shift), acc)
        return acc

    for t in range(9):
        f_done(t, gather(lambda l: adj_ref[t, l], f_kind(t), slot))
        t_done(t, [gather(lambda l: traj_ref[k, t, l], t_kind(9 * k + t), slot_16) for k in range(3)])
    bottom = jnp.bitwise_xor(s, core)
    f_done(9, gather(lambda l: wind_ref[1, l], f_kind(9), slot))
    f_done(10, gather(lambda l: wind_ref[0, l], f_kind(10), slot))
    f_done(11, gather(lambda l: marked(mix_ref[l], land, bottom) if l == 0 else mix_ref[l], f_kind(11), slot))


def lon_start_kernel(field_ref, traj_ref, land_ref, f_ref, t_ref):
    def f_done(f, value):
        f_ref[f] = value

    def t_done(t, values):
        for k in range(3):
            t_ref[9 * k + t] = values[k]

    gather_edges(
        lax.axis_index("lev"),
        0,
        parts_of(field_ref, traj_ref),
        land_ref[...],
        lambda f: jnp.zeros((16, 128), F32),
        lambda f: jnp.zeros((16, 128), BF16),
        f_done,
        t_done,
    )


def lon_pack_kernel(field_ref, traj_ref, land_ref, f_ref, t_ref, out_ref):
    core = lax.axis_index("lev")
    far = (jnp.bitwise_xor((iota((16, 128), 1) // 4) % 2, core)).astype(F32).astype(BF16)

    def pair(f, first, second):
        tops, bottoms = halves(first), halves(second)
        for h in range(2):
            out_ref[h, f] = stack_rows(tops[h], bottoms[h]).astype(BF16)

    def f_done(f, value):
        high, low = split(value)
        pair(f, high, low)

    def t_done(t, tr):
        both = jnp.where(far > 0, lane_roll(tr[0], jnp.where(core == 0, 4, 124)), tr[1])
        pair(12 + t, tr[2], both)

    gather_edges(
        core,
        1,
        parts_of(field_ref, traj_ref),
        land_ref[...],
        lambda f: f_ref[f],
        lambda f: t_ref[f],
        f_done,
        t_done,
    )


def put_rows(ref, t, z, value):
    zero = jnp.zeros((8, 128), F32)
    ref[t, z, 0:8, :] = zero
    ref[t, z, 8:24, :] = value
    ref[t, z, 24:32, :] = zero


def zero_ends(ref):
    for t in range(9):
        for z in (0, 17):
            ref[t, z] = jnp.zeros(ref.shape[2:], F32)


def react(scalars, traj, a_in, b_s, z, sums):
    rate_ref, speed_ref, class_ref, prof_ref, coef_ref = scalars
    rate = [rate_ref[q, z] for q in range(6)]
    share = [prof_ref[z] * coef_ref[t] for t in range(9)]
    tiles = [traj(t).astype(F32) for t in range(9)]
    parts = []
    for rb in range(2):
        rows = slice(8 * rb, 8 * rb + 8)
        adj = [a_in(t, rows) for t in range(9)]
        done = coag(adj, [tile[rows] for tile in tiles], rate)
        for t in range(9):
            b_s[t, z + 1, rows, :] = done[t]
        parts.append([sums[rb][m] + sum(share[3 * m + j] * adj[3 * m + j] for j in range(3)) for m in range(3)])
    return parts


def mixed(scalars, b_s, d, deposit, put, z):
    rate_ref, speed_ref, class_ref, prof_ref, coef_ref = scalars
    kind = class_ref[z]
    below, above = d(z - 1), d(z)
    base = 1.0 - above - below
    base = jnp.where(z == 0, base - deposit, base)
    for t in range(9):
        speed = speed_ref[kind, t]
        put(t, z, b_s[t, z + 1] * (base - speed) + b_s[t, z] * (below + speed) + b_s[t, z + 2] * above)


def moved(c_in, w_ref, a_to, z):
    for rb in range(2):
        rows = slice(8 * rb, 8 * rb + 8)
        w = [w_ref[i, z, rows, :] for i in range(9)]
        for t in range(9):
            shifted = [c_in[t, z, 8 * rb + 6 + i : 8 * rb + 14 + i, :] for i in range(5)]
            a_to[t, z, rows, :] = transported(shifted, w)


def no_sums():
    return [[jnp.zeros((8, 128), F32)] * 3, [jnp.zeros((8, 128), F32)] * 3]


def total(lat_count, step, sums):
    lat = lax.axis_index("lat")
    row = iota((16, 128), 0)
    sums = [stack_rows(sums[0][m], sums[1][m]) for m in range(3)]
    if step == 0:
        return sums
    low, high = 2 * step, 15 - 2 * step
    if lat_count == 2:
        good = ((row <= high) | (lat != 0)) & ((row >= low) | (lat == 0))
    else:
        good = (row <= high) & (row >= low)
    return [jnp.where(good, v, 0.0) for v in sums]


def pipeline(stages, carry=None):
    stages = sorted(stages, key=lambda stage: -stage[0])
    depth = stages[0][0]

    def at(z, carry):
        for lag, stage in stages:
            if 0 <= z - lag < 16:
                carry = stage(z - lag, carry)
        return carry

    for z in range(depth):
        carry = at(z, carry)
    for z in range(depth, 16 + depth):
        carry = at(z, carry)
    return carry


def first_kernel(lat_count, *refs):
    own, other = parts_of(*refs[0:2]), parts_of(*refs[2:4])
    land_ref = refs[4]
    scalars = refs[5:10]
    c_out, em_ref, traj_out, wind_out, mix_out = refs[10:15]
    b_s = refs[15]
    core = lax.axis_index("lev")
    zero_ends(b_s)
    deposit = 0.1 + 0.3 * land_ref[...].astype(F32)
    nothing = jnp.zeros((16, 128), F32)

    def put(t, z, value):
        c_out[t, z] = value

    def run(low, high):
        def level(r, z, l, sums):
            for k in range(2):
                for t in range(9):
                    traj_out[k, t, z] = r[1][k, t, l]
            for i in range(2):
                wind_out[i, z] = r[2][i, l]
            mix_out[z] = r[3][l]
            return react(scalars, lambda t: r[1][2, t, l], lambda t, rows: r[0][t, l, rows, :], b_s, z, sums)

        def mix(z):
            def d(i):
                if isinstance(i, int) and i in (-1, 15):
                    return nothing
                return mix_out[i]

            mixed(scalars, b_s, d, deposit, put, z)

        sums = no_sums()
        for z in range(3):
            sums = level(low, z, z, sums)
        mix(0)

        def lower(z, sums):
            mix(z - 2)
            return level(low, z, z, sums)

        sums = lax.fori_loop(3, 8, lower, sums)

        def upper(z, sums):
            mix(z - 2)
            return level(high, z, z - 8, sums)

        sums = lax.fori_loop(8, 16, upper, sums)
        mix(14)
        mix(15)
        sums = total(lat_count, 0, sums)
        for m in range(3):
            em_ref[m] = sums[m]

    pl.when(core == 0)(lambda: run(own, other))
    pl.when(core == 1)(lambda: run(other, own))


def second_kernel(lat_count, *refs):
    land_ref, lon_ref, c_own, em_in, traj_own, wind_own, mix_own = refs[0:7]
    scalars = refs[7:12]
    rate_ref, speed_ref, class_ref, prof_ref, coef_ref = scalars
    traj_out, c_first, c_next, n_out, e_out, d_out, land_out, w_s, em_ref, q_s = refs[12:22]
    a_s, b_s, p_s = refs[22:]
    core = lax.axis_index("lev")
    lat = lax.axis_index("lat")
    edge = jnp.where(core == 0, 120, 0)
    halo = halo_lanes(core, 16)
    halo_16 = halo_lanes_16(core)
    row = iota((16, 128), 0)
    zero = jnp.zeros((16, 128), F32)
    z_lane = jnp.bitwise_xor(iota((8, 128), 1) // 8, 8 * (1 - core))
    zero_ends(b_s)
    d_out[0] = zero

    def shift_of(z):
        return lax.rem(edge + 128 - 8 * jnp.bitwise_xor(z, 8 * (1 - core)), 128)

    def by_lane(read):
        acc = jnp.zeros((8, 128), F32)
        for z in range(16):
            acc = jnp.where(z_lane == z, read(z), acc)
        return acc

    for f in range(9, 12):
        for h in range(2):
            p_s[f, 8 * h : 8 * h + 8, :] = sum(halves(lon_ref[h, f]))
    for t in range(9):
        q_s[t] = stack_rows(halves(lon_ref[0, 12 + t])[1], halves(lon_ref[1, 12 + t])[1]).astype(BF16)
    rate = [by_lane(lambda z: rate_ref[q, z]) for q in range(6)]
    speeds = [by_lane(lambda z: speed_ref[class_ref[z], t]) for t in range(9)]
    for rb in range(2):
        rows = slice(8 * rb, 8 * rb + 8)
        adj = [sum(halves(lon_ref[rb, t])) for t in range(9)]
        done = coag(adj, [halves(lon_ref[rb, 12 + t])[0] for t in range(9)], rate)
        mark = p_s[11, rows, :]
        land = ((mark < 0) & (z_lane == 0)).astype(F32)
        size = jnp.abs(mark)
        above = jnp.where(z_lane == 15, 0.0, size)
        below = jnp.where(z_lane == 0, 0.0, lane_roll(size, 8))
        base = 1.0 - above - below - jnp.where(z_lane == 0, 0.1 + 0.3 * land, 0.0)
        for t in range(9):
            under = jnp.where(z_lane == 0, 0.0, lane_roll(done[t], 8))
            p_s[t, rows, :] = (
                done[t] * (base - speeds[t]) + under * (below + speeds[t]) + lane_roll(done[t], 120) * above
            )
    land_halo = (lane_roll(p_s[11], shift_of(0)) < 0).astype(F32)
    deposit = 0.1 + 0.3 * jnp.where(halo, land_halo, land_ref[...].astype(F32))
    land_out[...] = deposit
    last_lat = lat == lat_count - 1

    def assemble(z, sums):
        shift = shift_of(z)
        for t in range(9):
            put_rows(c_first, t, z, jnp.where(halo, lane_roll(p_s[t], shift), c_own[t, z]))
            traj_out[t, z] = jnp.where(halo_16, lane_roll(q_s[t], shift), traj_own[1, t, z])
        north = jnp.where(halo, lane_roll(p_s[9], shift), wind_own[1, z])
        north = jnp.where((row == 15) & last_lat, 0.0, north)
        east = jnp.where(halo, lane_roll(p_s[10], shift), wind_own[0, z])
        mix = jnp.where(halo, jnp.abs(lane_roll(p_s[11], shift)), mix_own[z])
        n_out[z, 0:8, :] = zero[:8]
        n_out[z, 8:24, :] = north
        n_out[z, 24:32, :] = zero[:8]
        e_out[z] = east
        d_out[z + 1] = jnp.where(z == 15, 0.0, mix)
        return sums

    def weigh(z, sums):
        shifted = [n_out[z, 6 + j : 22 + j, :] for j in range(4)]
        for j, value in enumerate(weights(e_out[z], shifted)):
            w_s[j, z] = value
        return sums

    steps = stages(scalars, c_first, w_s, a_s, b_s, traj_out, lambda z: d_out[z + 1], land_out[...], c_next, 2)
    sums = pipeline([(0, assemble), (1, weigh)] + steps, no_sums())
    sums = total(lat_count, 1, sums)
    for m in range(3):
        em_ref[m] = em_in[m] + sums[m]


def stages(scalars, c_in, w_ref, a_s, b_s, traj_ref, d, deposit, c_out, lag):
    def move(z, sums):
        moved(c_in, w_ref, a_s, z)
        return sums

    def do_react(z, sums):
        return react(scalars, lambda t: traj_ref[t, z], lambda t, rows: a_s[t, z, rows, :], b_s, z, sums)

    def mix(z, sums):
        mixed(scalars, b_s, d, deposit, lambda t, i, value: put_rows(c_out, t, i, value), z)
        return sums

    return [(lag, move), (lag + 1, do_react), (lag + 3, mix)]


def third_kernel(lat_count, *refs):
    traj_own, q_ref, d_ref, land_ref, w_ref, c_in, em_in = refs[0:7]
    scalars = refs[7:12]
    c_next, em_ref, traj_out = refs[12:15]
    a_s, b_s = refs[15:]
    core = lax.axis_index("lev")
    edge = 124
    halo_16 = halo_lanes_16(core)
    zero_ends(b_s)

    def complete(z, sums):
        shift = lax.rem(edge + 128 - 8 * jnp.bitwise_xor(z, 8 * (1 - core)), 128)
        for t in range(9):
            traj_out[t, z] = jnp.where(halo_16, lane_roll(q_ref[t], shift), traj_own[0, t, z])
        return sums

    steps = stages(scalars, c_in, w_ref, a_s, b_s, traj_out, lambda z: d_ref[z + 1], land_ref[...], c_next, 0)
    sums = total(lat_count, 2, pipeline(steps + [(0, complete)], no_sums()))
    for m in range(3):
        em_ref[m] = em_in[m] + sums[m]


def edge_kernel(lat_count, *refs):
    edges = 1 if lat_count == 2 else 2
    traj_1, c_first, c_next, n_ref, e_ref, d_ref, land_ref, c_last, w_ref, traj_0, em_ref = refs[0:11]
    lat_refs = refs[11 : 11 + 2 * edges]
    corner_refs = refs[11 + 2 * edges : 11 + 3 * edges]
    rate_ref, speed_ref, class_ref, prof_ref, coef_ref = refs[11 + 3 * edges : 16 + 3 * edges]
    keep_ref, send_ref = refs[16 + 3 * edges : 18 + 3 * edges]
    b_0, b_1, c_0, c_1, c_2, t_s, n_s, e_s, d_s, l_s, a_s, em_s, fin_s = refs[18 + 3 * edges :]
    far = 2 - edges
    core = lax.axis_index("lev")
    lat = lax.axis_index("lat")
    edge = jnp.where(core == 0, 120, 0)
    flip = 1 - core
    halo = halo_lanes(core, 8)
    sub = iota((8, 128), 0)
    zero = jnp.zeros((8, 128), F32)

    def run(upper, e):
        own_at, halo_at = (0, 8) if upper else (8, 0)
        own_row = 8 if upper else 0
        corner_ref = corner_refs[e]
        starts = (6, 4, 0) if upper else (2, 4, 8)
        b_bufs, c_bufs = (b_0, b_1, b_0), (c_0, c_1, c_2)

        def shift_of(z):
            return lax.rem(edge + 128 - 8 * jnp.bitwise_xor(z, 8 * flip), 128)

        def corner(tile, z):
            return halves(lane_roll(corner_ref[tile], shift_of(z)))

        def corner_sum(f, z):
            return sum(corner(f, z))

        land_c = corner_sum(11, 0)
        land_l = jnp.where(core == 0, sum(halves(lat_refs[2 * e][116])), sum(halves(lat_refs[2 * e + 1][116])))
        l_s[pl.ds(halo_at, 8), :] = 0.1 + 0.3 * (jnp.where(halo, land_c, land_l) < 0).astype(F32)
        l_s[pl.ds(own_at, 8), :] = land_ref[pl.ds(own_row, 8), :]
        d_s[0] = jnp.zeros((16, 128), F32)

        zero_ends(b_0)
        zero_ends(b_1)

        for s in range(2):
            msg = lat_refs[2 * e + s]

            def receive(pair, _):
                for i in range(2):
                    l = 2 * pair + i
                    z = 8 * jnp.bitwise_xor(s, core) + l
                    rate = [rate_ref[q, z] for q in range(6)]
                    adj, state = [], []
                    for t in range(9):
                        v0, v1 = halves(msg[t * 8 + l])
                        v2 = halves(msg[72 + t * 4 + pair])[i]
                        adj.append(jnp.where(halo, corner_sum(t, z), v0 + v1))
                        tr2, tr1 = corner(12 + t, z)
                        tr0 = lane_roll(tr1, jnp.where(core == 0, 4, 124))
                        state.append(jnp.where(halo, tr2, v2))
                        near, rest = (1, -1) if upper else (0, 1)
                        t_s[1, t, z, pl.ds(halo_at + 4 * rest, 8), :] = v2
                        t_s[1, t, z, pl.ds(halo_at + 6 * rest, 8), :] = v1
                        t_s[0, t, z, pl.ds(halo_at + 6 * rest, 8), :] = v0
                        t_s[1, t, z, pl.ds(own_at, 8), :] = halves(traj_1[t, z])[near]
                        t_s[0, t, z, pl.ds(own_at, 8), :] = halves(traj_0[t, z])[near]
                        pltpu.store(t_s.at[1, t, z, pl.ds(halo_at, 8), :], tr1, mask=halo)
                        pltpu.store(t_s.at[0, t, z, pl.ds(halo_at, 8), :], tr0, mask=halo)
                    done = coag(adj, state, rate)
                    for t in range(9):
                        b_0[t, z + 1] = done[t]
                    north_h, north_l = halves(msg[108 + l])
                    mix_h, mix_l = halves(msg[116 + l])
                    north = jnp.where(halo, corner_sum(9, z), north_h + north_l)
                    mixing = jnp.where(halo, corner_sum(11, z), mix_h + mix_l)
                    e_s[z, pl.ds(halo_at + 4 * rest, 8), :] = north_l + mix_l
                    e_s[z, pl.ds(halo_at + 6 * rest, 8), :] = north_h + mix_h
                    if upper:
                        n_s[z, 0:8, :] = n_ref[z, 8:16, :]
                    else:
                        n_s[z, 24:32, :] = n_ref[z, 16:24, :]
                    n_s[z, pl.ds(8 + halo_at, 8), :] = north
                    n_s[z, pl.ds(8 + own_at, 8), :] = n_ref[z, pl.ds(8 + own_row, 8), :]
                    e_s[z, pl.ds(own_at, 8), :] = e_ref[z, pl.ds(own_row, 8), :]
                    pltpu.store(e_s.at[z, pl.ds(halo_at, 8), :], corner_sum(10, z), mask=halo)
                    d_s[z + 1, pl.ds(halo_at, 8), :] = jnp.where(z == 15, 0.0, jnp.abs(mixing))
                    d_s[z + 1, pl.ds(own_at, 8), :] = d_ref[z + 1, pl.ds(own_row, 8), :]
                return 0

            lax.fori_loop(0, 4, receive, 0)

        for m in range(3):
            for part in range(3):
                em_s[m, 8 * part : 8 * part + 8, :] = zero

        def mix(step, z):
            at = halo_at if step == 0 else starts[step - 1]
            b, c = b_bufs[step], c_bufs[step]
            c_ref = (c_first, c_next, c_last)[step]
            kind = class_ref[z]
            below, above = d_s[z, at : at + 8, :], d_s[z + 1, at : at + 8, :]
            base = 1.0 - above - below
            base = jnp.where(z == 0, base - l_s[at : at + 8, :], base)
            for t in range(9):
                speed = speed_ref[kind, t]
                value = b[t, z + 1] * (base - speed) + b[t, z] * (below + speed) + b[t, z + 2] * above
                if step < 2:
                    c[t, z, 8 + own_at : 16 + own_at, :] = c_ref[t, z, 8 + own_row : 16 + own_row, :]
                elif upper:
                    c[t, z, 0:16, :] = c_ref[t, z, 8:24, :]
                else:
                    c[t, z, 16:32, :] = c_ref[t, z, 8:24, :]
                c[t, z, 8 + at : 16 + at, :] = value

        def move(step, z, sums):
            at = starts[step]
            c = c_bufs[step]
            shifted = [n_s[z, 6 + at + i : 14 + at + i, :] for i in range(4)]
            w = weights(e_s[z, at : at + 8, :], shifted)
            adj = []
            for t in range(9):
                rows = [c[t, z, 6 + at + i : 14 + at + i, :] for i in range(5)]
                adj.append(transported(rows, w))
            if step == 2:
                for t in range(9):
                    fin_s[e, t, z] = adj[t]
                return sums
            share = [prof_ref[z] * coef_ref[t] for t in range(9)]
            sums = [sums[m] + sum(share[3 * m + j] * adj[3 * m + j] for j in range(3)) for m in range(3)]
            rate = [rate_ref[q, z] for q in range(6)]
            state = [t_s[1 - step, t, z, at : at + 8, :] for t in range(9)]
            done = coag(adj, state, rate)
            for t in range(9):
                b_bufs[step + 1][t, z + 1] = done[t]
            return sums

        def count(step, sums):
            at = starts[step]
            buf_row = sub + at
            rows = 2 + 2 * step
            if upper:
                good = (buf_row >= 8 - rows) & (buf_row < 8)
            else:
                good = (buf_row >= 8) & (buf_row < 8 + rows)
            for m in range(3):
                em_s[m, at : at + 8, :] = em_s[m, at : at + 8, :] + jnp.where(good, sums[m], 0.0)

        none = [zero, zero, zero]

        def mixing(step):
            def stage(z, sums):
                mix(step, z)
                return sums

            return stage

        def moving(step):
            return lambda z, sums: move(step, z, sums)

        count(0, pipeline([(0, mixing(0)), (1, moving(0)), (3, mixing(1))], none))

        def far_moving(z, sums):
            near = 0 if upper else 8
            w = [w_ref[i, z, near : near + 8, :] for i in range(9)]
            for t in range(9):
                rows = [c_last[t, z, near + 6 + i : near + 14 + i, :] for i in range(5)]
                fin_s[1, t, z] = transported(rows, w)
            return sums

        later = [(0, moving(1)), (2, mixing(2)), (3, moving(2))] + [(3, far_moving)] * far
        count(1, pipeline(later, none))
        for m in range(3):
            a_s[e, m] = em_s[m, own_at : own_at + 8, :]

    def finish(has_upper, has_lower, e_upper, e_lower):
        mine = (iota((16, 128), 1) < 64) == (core == 0)

        def rows_of(t, z):
            low = fin_s[e_lower, t, z]
            high = fin_s[e_upper, t, z]
            return stack_rows(low, high)

        def tracer(t, _):
            for l in range(8):
                keep_ref[t, l] = rows_of(t, 8 * core + l)
            for l in range(4):
                z = 8 * (1 - core) + l
                send_ref[t * 4 + l] = jnp.where(mine, rows_of(t, z), lane_roll(rows_of(t, z + 4), 64))
            return 0

        lax.fori_loop(0, 9, tracer, 0)
        for m in range(3):
            low = em_ref[m, 0:8, :]
            high = em_ref[m, 8:16, :]
            if has_upper:
                high = high + a_s[e_upper, m]
            if has_lower:
                low = low + a_s[e_lower, m]
            send_ref[36 + m] = stack_rows(low, high)

    if lat_count == 2:

        def south():
            run(True, 0)
            finish(True, False, 0, 1)

        def north():
            run(False, 0)
            finish(False, True, 1, 0)

        pl.when(lat == 0)(south)
        pl.when(lat == 1)(north)
    else:
        run(True, 0)
        run(False, 1)
        finish(True, True, 0, 1)


def join_kernel(keep_ref, send_ref, recv_ref, source_ref, out_ref, em_ref, part, em_part, sems):
    core = lax.axis_index("lev")
    mine = (iota((16, 128), 1) < 64) == (core == 0)
    source = source_ref[...].astype(F32)
    for m in range(3):
        em_part[m] = jnp.where(mine, send_ref[36 + m], recv_ref[36 + m]) * source
    copies = [pltpu.make_async_copy(em_part, em_ref, sems.at[9])]
    copies[0].start()
    for t in range(9):
        for l in range(4):
            got = recv_ref[t * 4 + l]
            part[t, l] = jnp.where(mine, keep_ref[t, l], got)
            part[t, l + 4] = jnp.where(mine, keep_ref[t, l + 4], lane_roll(got, 64))
        copies.append(pltpu.make_async_copy(part.at[t], out_ref.at[t], sems.at[t]))
        copies[-1].start()
    for copy in copies:
        copy.wait()


def corner_kernel(lon_ref, out_ref):
    out_ref[...] = lon_ref[1 - lax.axis_index("lat")]


def shape(*dims, dtype=F32):
    return jax.ShapeDtypeStruct(dims, dtype)


def call(kernel, outs, scratch, *args, specs=None, out_specs=None, mib=32):
    return pl.pallas_call(
        kernel,
        out_shape=outs,
        in_specs=specs or [VMEM] * len(args),
        out_specs=out_specs or [VMEM] * len(outs),
        scratch_shapes=scratch,
        compiler_params=pltpu.CompilerParams(vmem_limit_bytes=mib * 1024 * 1024),
    )(*args)


def shards(
    adjoint_in,
    trajectory,
    courant,
    mixing,
    coag_rates,
    settle_speed,
    settle_class,
    emis_profile,
    emis_coef,
    land_mask,
    source_mask,
):
    lat_count = lax.axis_size("lat")
    lon_count = lax.axis_size("lon")
    edges = 1 if lat_count == 2 else 2
    swap = [(0, 1), (1, 0)]

    def over_lev(value):
        return lax.ppermute(value, "lev", swap)

    def lat_moves(messages):
        if edges == 1:
            return [lax.ppermute(messages[0], "lat", swap)]
        up = [(j, j + 1) for j in range(lat_count - 1)]
        down = [(j + 1, j) for j in range(lat_count - 1)]
        return [lax.ppermute(messages[-1], "lat", down), lax.ppermute(messages[0], "lat", up)]

    def bind(kernel):
        def run(*refs):
            return kernel(lat_count, *refs)

        return run

    given = (adjoint_in, trajectory, courant, mixing, land_mask)
    field, traj, land = call(
        load_kernel,
        [
            shape(12, *adjoint_in.shape[1:]),
            jax.ShapeDtypeStruct(trajectory.shape, trajectory.dtype),
            jax.ShapeDtypeStruct(land_mask.shape, land_mask.dtype),
        ],
        [pltpu.SemaphoreType.DMA((9,))],
        *[pltpu.with_memory_space_constraint(v, pltpu.HBM) for v in given],
        specs=[pl.BlockSpec(memory_space=pltpu.HBM)] * 5,
        mib=16,
    )
    own = (field, traj)
    other = (over_lev(field), over_lev(trajectory))
    half = call(
        lon_start_kernel, [shape(12, 16, 128), shape(27, 16, 128, dtype=BF16)], [], *own, land, mib=16
    )
    (lon_out,) = call(
        lon_pack_kernel, [shape(2, LON_TILES, 16, 128, dtype=BF16)], [], *other, land, *half, mib=16
    )
    lat_out = call(
        bind(lat_pack_kernel), [shape(LAT_TILES, 16, 128, dtype=BF16)] * edges, [], *own, land, mib=16
    )
    lat_in = lat_moves(lat_out)
    lon_pairs = []
    for i in range(lon_count):
        lon_pairs.append((2 * i + 1, 2 * ((i + 1) % lon_count)))
        lon_pairs.append((2 * i, 2 * ((i - 1) % lon_count) + 1))
    lon_in = lax.ppermute(lon_out, ("lon", "lev"), lon_pairs)
    scalars = (coag_rates, settle_speed, settle_class, emis_profile, emis_coef)
    state = pltpu.VMEM((9, 16, 16, 128), F32)
    between = pltpu.VMEM((9, 18, 16, 128), F32)
    padded = shape(9, 16, 32, 128)
    c_own, emis, traj_own, wind_own, mix_own = call(
        bind(first_kernel),
        [
            shape(9, 16, 16, 128),
            shape(3, 16, 128),
            shape(2, 9, 16, 16, 128, dtype=BF16),
            shape(2, 16, 16, 128),
            shape(16, 16, 128),
        ],
        [between],
        *own,
        *other,
        land,
        *scalars,
        specs=[VMEM] * 5 + [SMEM] * 5,
    )
    lon_in, c_own = lax.optimization_barrier((lon_in, c_own))
    if edges == 1:
        corner_out = call(corner_kernel, [shape(LON_TILES, 16, 128, dtype=BF16)], [], lon_in, mib=16)
    else:
        corner_out = [lon_in[1], lon_in[0]]
    corner_in = lat_moves(corner_out)
    traj_1, c_first, c_next, north, east, mix, land_all, weight, emis, strip = call(
        bind(second_kernel),
        [
            shape(9, 16, 16, 128, dtype=BF16),
            padded,
            padded,
            shape(16, 32, 128),
            shape(16, 16, 128),
            shape(17, 16, 128),
            shape(16, 128),
            shape(9, 16, 16, 128),
            shape(3, 16, 128),
            shape(9, 16, 128, dtype=BF16),
        ],
        [state, between, pltpu.VMEM((12, 16, 128), F32)],
        land,
        lon_in,
        c_own,
        emis,
        traj_own,
        wind_own,
        mix_own,
        *scalars,
        specs=[VMEM] * 7 + [SMEM] * 5,
    )
    c_next, *lat_in = lax.optimization_barrier((c_next, *lat_in))
    c_last, emis, traj_0 = call(
        bind(third_kernel),
        [padded, shape(3, 16, 128), shape(9, 16, 16, 128, dtype=BF16)],
        [state, between],
        traj_own,
        strip,
        mix,
        land_all,
        weight,
        c_next,
        emis,
        *scalars,
        specs=[VMEM] * 7 + [SMEM] * 5,
    )
    inner = (traj_1, c_first, c_next, north, east, mix, land_all, c_last, weight, traj_0, emis)
    lat_all = []
    for value in lat_in:
        lat_all += [value, over_lev(value)]
    keep, send = call(
        bind(edge_kernel),
        [shape(9, 8, 16, 128), shape(39, 16, 128)],
        [
            pltpu.VMEM((9, 18, 8, 128), F32),
            pltpu.VMEM((9, 18, 8, 128), F32),
            pltpu.VMEM((9, 16, 32, 128), F32),
            pltpu.VMEM((9, 16, 32, 128), F32),
            pltpu.VMEM((9, 16, 32, 128), F32),
            pltpu.VMEM((2, 9, 16, 16, 128), F32),
            pltpu.VMEM((16, 32, 128), F32),
            pltpu.VMEM((16, 16, 128), F32),
            pltpu.VMEM((17, 16, 128), F32),
            pltpu.VMEM((16, 128), F32),
            pltpu.VMEM((edges, 3, 8, 128), F32),
            pltpu.VMEM((3, 24, 128), F32),
            pltpu.VMEM((2, 9, 16, 8, 128), F32),
        ],
        *inner,
        *lat_all,
        *corner_in,
        *scalars,
        specs=[VMEM] * (11 + 3 * edges) + [SMEM] * 5,
        mib=40,
    )
    recv = over_lev(send)
    out, emis = call(
        join_kernel,
        [shape(9, 8, 16, 128), shape(3, 16, 128)],
        [pltpu.VMEM((9, 8, 16, 128), F32), pltpu.VMEM((3, 16, 128), F32), pltpu.SemaphoreType.DMA((10,))],
        keep,
        send,
        recv,
        source_mask,
        out_specs=[pl.BlockSpec(memory_space=pltpu.HBM)] * 2,
    )
    return (out, emis)


def solution(mesh):
    return jax.shard_map(
        shards,
        mesh=mesh,
        in_specs=(
            P(None, "lev", "lat", "lon"),
            P(None, None, "lev", "lat", "lon"),
            P(None, "lev", "lat", "lon"),
            P("lev", "lat", "lon"),
            P(),
            P(),
            P(),
            P(),
            P(),
            P("lat", "lon"),
            P("lat", "lon"),
        ),
        out_specs=(P(None, "lev", "lat", "lon"), P(None, "lat", "lon")),
        check_vma=False,
    )
```

```python
import jax
import jax.numpy as jnp
from jax import lax
from jax.experimental import pallas as pl
from jax.experimental.pallas import tpu as pltpu
from jax.sharding import PartitionSpec as P

F32 = jnp.float32
BF16 = jnp.bfloat16
VMEM = pl.BlockSpec(memory_space=pltpu.VMEM)
SMEM = pl.BlockSpec(memory_space=pltpu.SMEM)
PAIRS = ((0, 1, 3), (0, 2, 4), (1, 2, 5))
LAT_TILES = 124
LON_TILES = 21


def iota(shape, axis):
    return lax.broadcasted_iota(jnp.int32, shape, axis)


def split(value):
    high = value.astype(BF16)
    low = (value - high.astype(F32)).astype(BF16)
    return high, low


def stack_rows(top, bottom):
    return jnp.concatenate([top, bottom], axis=0)


def halves(tile):
    wide = tile.astype(F32)
    return wide[:8], wide[8:]


def coag(adj, state, rate):
    out = list(adj)
    kn = {}
    for m, p, q in PAIRS:
        kn[m, p] = rate[q] * state[3 * p]
    for m in range(3):
        total = (2.0 * rate[m]) * state[3 * m]
        for p in range(m + 1, 3):
            total = total + kn[m, p]
        out[3 * m] = out[3 * m] - total * adj[3 * m]
        out[3 * m + 1] = out[3 * m + 1] + (2.0 * rate[m]) * (state[3 * m + 1] * adj[3 * m + 2])
    for m, p, q in PAIRS:
        d_vol = adj[3 * p + 1] - adj[3 * m + 1]
        d_six = adj[3 * p + 2] - adj[3 * m + 2]
        inner = d_vol * state[3 * m + 1] + d_six * state[3 * m + 2] - adj[3 * m] * state[3 * m]
        cross = (2.0 * rate[q]) * adj[3 * p + 2]
        out[3 * p] = out[3 * p] + rate[q] * inner
        out[3 * m + 1] = out[3 * m + 1] + (kn[m, p] * d_vol + cross * state[3 * p + 1])
        out[3 * p + 1] = out[3 * p + 1] + cross * state[3 * m + 1]
        out[3 * m + 2] = out[3 * m + 2] + kn[m, p] * d_six
    return out


def lane_roll(value, shift):
    return pltpu.roll(value, shift, 1)


def weights(east, north):
    pos = jnp.maximum(east, 0.0)
    neg = jnp.minimum(east, 0.0)
    pos_1 = lane_roll(pos, 127)
    neg_1 = lane_roll(neg, 1)
    neg_2 = lane_roll(neg, 2)
    n_pos = jnp.maximum(north[2], 0.0)
    n_pos_1 = jnp.maximum(north[3], 0.0)
    n_neg_1 = jnp.minimum(north[1], 0.0)
    n_neg_2 = jnp.minimum(north[0], 0.0)
    centre = 1.0 + 1.5 * ((neg_1 - pos) + (n_neg_1 - n_pos))
    return (
        centre,
        0.5 * neg_2,
        -1.5 * neg_1 - 0.5 * neg_2,
        1.5 * pos + 0.5 * pos_1,
        -0.5 * pos_1,
        0.5 * n_neg_2,
        -1.5 * n_neg_1 - 0.5 * n_neg_2,
        1.5 * n_pos + 0.5 * n_pos_1,
        -0.5 * n_pos_1,
    )


def transported(rows, w):
    mid = rows[2]
    lon = (w[1] * lane_roll(mid, 2) + w[2] * lane_roll(mid, 1)) + (
        w[3] * lane_roll(mid, 127) + w[4] * lane_roll(mid, 126)
    )
    lat = (w[5] * rows[0] + w[6] * rows[1]) + (w[7] * rows[3] + w[8] * rows[4])
    return w[0] * mid + (lon + lat)


def level_scalars(z, rate_ref, speed_ref, class_ref):
    rate = [rate_ref[q, z] for q in range(6)]
    kind = class_ref[z]
    speed = [speed_ref[kind, t] for t in range(9)]
    return rate, speed


def halo_lanes(core, rows):
    lane = iota((rows, 128), 1)
    return jnp.where(core == 0, (lane >= 120).astype(jnp.int32), (lane < 8).astype(jnp.int32)) > 0


def halo_lanes_16(core):
    middle = jnp.where(core == 0, 123.5, 3.5).astype(F32)
    return jnp.abs(iota((16, 128), 1).astype(F32) - middle).astype(BF16) <= jnp.full((16, 128), 3.5, BF16)


def load_kernel(adj_ref, traj_ref, wind_ref, mix_ref, land_ref, field_out, traj_out, land_out, sems):
    pairs = [(traj_ref, traj_out), (adj_ref, field_out.at[pl.ds(0, 9)]), (wind_ref, field_out.at[pl.ds(9, 2)])]
    pairs += [(mix_ref, field_out.at[11]), (land_ref, land_out)]
    copies = [pltpu.make_async_copy(source, target, sems.at[i]) for i, (source, target) in enumerate(pairs)]
    for copy in copies:
        copy.start()
    for copy in copies:
        copy.wait()


def parts_of(field_ref, traj_ref):
    return field_ref.at[pl.ds(0, 9)], traj_ref, field_ref.at[pl.ds(9, 2)], field_ref.at[11]


def marked(mix, land, z):
    return jnp.where((land * (z == 0).astype(jnp.int32)) > 0, -mix, mix)


def lat_pack_kernel(lat_count, field_ref, traj_ref, land_ref, *outs):
    adj_ref, traj_ref, wind_ref, mix_ref = parts_of(field_ref, traj_ref)
    core = lax.axis_index("lev")
    lat = lax.axis_index("lat")

    def fill(out_ref, high_rows):
        base = 8 if high_rows else 0
        sub = iota((8, 128), 0)
        keep = (sub >= 2) if high_rows else (sub < 6)

        def rolled(value, shift):
            return pltpu.roll(value, shift, 0)

        def tracer(t, _):
            v2s = []
            for l in range(8):
                adj = adj_ref[t, l, base : base + 8, :]
                high = adj.astype(BF16).astype(F32)
                low = adj - high
                tr = [traj_ref[k, t, l].astype(F32)[base : base + 8] for k in range(3)]
                if high_rows:
                    extra = (rolled(tr[0], 2), rolled(tr[1], 2), rolled(tr[1], 4))
                else:
                    extra = (rolled(tr[0], 6), rolled(tr[1], 6), rolled(tr[1], 4))
                v0 = jnp.where(keep, high, extra[0])
                v1 = jnp.where(keep, low, extra[1])
                v2s.append(jnp.where(keep, tr[2], extra[2]))
                out_ref[t * 8 + l] = stack_rows(v0, v1).astype(BF16)
            for j in range(4):
                out_ref[72 + t * 4 + j] = stack_rows(v2s[2 * j], v2s[2 * j + 1]).astype(BF16)

        for t in range(9):
            tracer(t, 0)

        def level(l, _):
            rows = slice(base, base + 8)
            z = l + 8 * core
            north, east = wind_ref[1, l, rows, :], wind_ref[0, l, rows, :]
            parts = []
            for value in (north, marked(mix_ref[l, rows, :], land_ref[rows, :], z), east):
                high = value.astype(BF16).astype(F32)
                parts += [high, value - high]
            one, two = (2, 4) if high_rows else (6, 4)
            north_h, north_l, mix_h, mix_l, east_h, east_l = parts
            out_ref[108 + l] = stack_rows(
                jnp.where(keep, north_h, rolled(east_h, one)), jnp.where(keep, north_l, rolled(east_h, two))
            ).astype(BF16)
            out_ref[116 + l] = stack_rows(
                jnp.where(keep, mix_h, rolled(east_l, one)), jnp.where(keep, mix_l, rolled(east_l, two))
            ).astype(BF16)

        for l in range(8):
            level(l, 0)

    if lat_count == 2:
        pl.when(lat == 0)(lambda: fill(outs[0], True))
        pl.when(lat == 1)(lambda: fill(outs[0], False))
    else:
        fill(outs[0], True)
        fill(outs[1], False)


def gather_edges(core, s, blocks, land, f_kind, t_kind, f_done, t_done):
    edge = jnp.where(core == 0, 0, 120)
    slot = iota((16, 128), 1) // 8
    slot_16 = slot.astype(BF16)
    adj_ref, traj_ref, wind_ref, mix_ref = blocks

    def gather(read, acc, at):
        for l in range(8):
            g = 8 * s + l
            shift = lax.rem(8 * g - edge + 128, 128)
            acc = jnp.where(at == g, lane_roll(read(l), shift), acc)
        return acc

    for t in range(9):
        f_done(t, gather(lambda l: adj_ref[t, l], f_kind(t), slot))
        t_done(t, [gather(lambda l: traj_ref[k, t, l], t_kind(9 * k + t), slot_16) for k in range(3)])
    bottom = jnp.bitwise_xor(s, core)
    f_done(9, gather(lambda l: wind_ref[1, l], f_kind(9), slot))
    f_done(10, gather(lambda l: wind_ref[0, l], f_kind(10), slot))
    f_done(11, gather(lambda l: marked(mix_ref[l], land, bottom) if l == 0 else mix_ref[l], f_kind(11), slot))


def lon_start_kernel(field_ref, traj_ref, land_ref, f_ref, t_ref):
    def f_done(f, value):
        f_ref[f] = value

    def t_done(t, values):
        for k in range(3):
            t_ref[9 * k + t] = values[k]

    gather_edges(
        lax.axis_index("lev"),
        0,
        parts_of(field_ref, traj_ref),
        land_ref[...],
        lambda f: jnp.zeros((16, 128), F32),
        lambda f: jnp.zeros((16, 128), BF16),
        f_done,
        t_done,
    )


def lon_pack_kernel(field_ref, traj_ref, land_ref, f_ref, t_ref, out_ref):
    core = lax.axis_index("lev")
    far = (jnp.bitwise_xor((iota((16, 128), 1) // 4) % 2, core)).astype(F32).astype(BF16)

    def pair(f, first, second):
        tops, bottoms = halves(first), halves(second)
        for h in range(2):
            out_ref[h, f] = stack_rows(tops[h], bottoms[h]).astype(BF16)

    def f_done(f, value):
        high, low = split(value)
        pair(f, high, low)

    def t_done(t, tr):
        both = jnp.where(far > 0, lane_roll(tr[0], jnp.where(core == 0, 4, 124)), tr[1])
        pair(12 + t, tr[2], both)

    gather_edges(
        core,
        1,
        parts_of(field_ref, traj_ref),
        land_ref[...],
        lambda f: f_ref[f],
        lambda f: t_ref[f],
        f_done,
        t_done,
    )


def put_rows(ref, t, z, value):
    zero = jnp.zeros((8, 128), F32)
    ref[t, z, 0:8, :] = zero
    ref[t, z, 8:24, :] = value
    ref[t, z, 24:32, :] = zero


def zero_ends(ref):
    for t in range(9):
        for z in (0, 17):
            ref[t, z] = jnp.zeros(ref.shape[2:], F32)


def react(scalars, traj, a_in, b_s, z, sums):
    rate_ref, speed_ref, class_ref, prof_ref, coef_ref = scalars
    rate = [rate_ref[q, z] for q in range(6)]
    share = [prof_ref[z] * coef_ref[t] for t in range(9)]
    tiles = [traj(t).astype(F32) for t in range(9)]
    parts = []
    for rb in range(2):
        rows = slice(8 * rb, 8 * rb + 8)
        adj = [a_in(t, rows) for t in range(9)]
        done = coag(adj, [tile[rows] for tile in tiles], rate)
        for t in range(9):
            b_s[t, z + 1, rows, :] = done[t]
        parts.append([sums[rb][m] + sum(share[3 * m + j] * adj[3 * m + j] for j in range(3)) for m in range(3)])
    return parts


def mixed(scalars, b_s, d, deposit, put, z):
    rate_ref, speed_ref, class_ref, prof_ref, coef_ref = scalars
    kind = class_ref[z]
    below, above = d(z - 1), d(z)
    base = 1.0 - above - below
    base = jnp.where(z == 0, base - deposit, base)
    for t in range(9):
        speed = speed_ref[kind, t]
        put(t, z, b_s[t, z + 1] * (base - speed) + b_s[t, z] * (below + speed) + b_s[t, z + 2] * above)


def moved(c_in, w_ref, a_to, z):
    for rb in range(2):
        rows = slice(8 * rb, 8 * rb + 8)
        w = [w_ref[i, z, rows, :] for i in range(9)]
        for t in range(9):
            shifted = [c_in[t, z, 8 * rb + 6 + i : 8 * rb + 14 + i, :] for i in range(5)]
            a_to[t, z, rows, :] = transported(shifted, w)


def no_sums():
    return [[jnp.zeros((8, 128), F32)] * 3, [jnp.zeros((8, 128), F32)] * 3]


def total(lat_count, step, sums):
    lat = lax.axis_index("lat")
    row = iota((16, 128), 0)
    sums = [stack_rows(sums[0][m], sums[1][m]) for m in range(3)]
    if step == 0:
        return sums
    low, high = 2 * step, 15 - 2 * step
    if lat_count == 2:
        good = ((row <= high) | (lat != 0)) & ((row >= low) | (lat == 0))
    else:
        good = (row <= high) & (row >= low)
    return [jnp.where(good, v, 0.0) for v in sums]


def pipeline(stages, carry=None):
    stages = sorted(stages, key=lambda stage: -stage[0])
    depth = stages[0][0]

    def at(z, carry):
        for lag, stage in stages:
            if 0 <= z - lag < 16:
                carry = stage(z - lag, carry)
        return carry

    for z in range(depth):
        carry = at(z, carry)
    for z in range(depth, 16 + depth):
        carry = at(z, carry)
    return carry


def first_kernel(lat_count, *refs):
    own, other = parts_of(*refs[0:2]), parts_of(*refs[2:4])
    land_ref = refs[4]
    scalars = refs[5:10]
    c_out, em_ref, traj_out, wind_out, mix_out = refs[10:15]
    b_s = refs[15]
    core = lax.axis_index("lev")
    zero_ends(b_s)
    deposit = 0.1 + 0.3 * land_ref[...].astype(F32)
    nothing = jnp.zeros((16, 128), F32)

    def put(t, z, value):
        c_out[t, z] = value

    def run(low, high):
        def level(r, z, l, sums):
            for k in range(2):
                for t in range(9):
                    traj_out[k, t, z] = r[1][k, t, l]
            for i in range(2):
                wind_out[i, z] = r[2][i, l]
            mix_out[z] = r[3][l]
            return react(scalars, lambda t: r[1][2, t, l], lambda t, rows: r[0][t, l, rows, :], b_s, z, sums)

        def mix(z):
            def d(i):
                if isinstance(i, int) and i in (-1, 15):
                    return nothing
                return mix_out[i]

            mixed(scalars, b_s, d, deposit, put, z)

        sums = no_sums()
        for z in range(3):
            sums = level(low, z, z, sums)
        mix(0)

        def lower(z, sums):
            mix(z - 2)
            return level(low, z, z, sums)

        sums = lax.fori_loop(3, 8, lower, sums)

        def upper(z, sums):
            mix(z - 2)
            return level(high, z, z - 8, sums)

        sums = lax.fori_loop(8, 16, upper, sums)
        mix(14)
        mix(15)
        sums = total(lat_count, 0, sums)
        for m in range(3):
            em_ref[m] = sums[m]

    pl.when(core == 0)(lambda: run(own, other))
    pl.when(core == 1)(lambda: run(other, own))


def second_kernel(lat_count, *refs):
    land_ref, lon_ref, c_own, em_in, traj_own, wind_own, mix_own = refs[0:7]
    scalars = refs[7:12]
    rate_ref, speed_ref, class_ref, prof_ref, coef_ref = scalars
    traj_out, c_first, c_next, n_out, e_out, d_out, land_out, w_s, em_ref, q_s = refs[12:22]
    a_s, b_s, p_s = refs[22:]
    core = lax.axis_index("lev")
    lat = lax.axis_index("lat")
    edge = jnp.where(core == 0, 120, 0)
    halo = halo_lanes(core, 16)
    halo_16 = halo_lanes_16(core)
    row = iota((16, 128), 0)
    zero = jnp.zeros((16, 128), F32)
    z_lane = jnp.bitwise_xor(iota((8, 128), 1) // 8, 8 * (1 - core))
    zero_ends(b_s)
    d_out[0] = zero

    def shift_of(z):
        return lax.rem(edge + 128 - 8 * jnp.bitwise_xor(z, 8 * (1 - core)), 128)

    def by_lane(read):
        acc = jnp.zeros((8, 128), F32)
        for z in range(16):
            acc = jnp.where(z_lane == z, read(z), acc)
        return acc

    for f in range(9, 12):
        for h in range(2):
            p_s[f, 8 * h : 8 * h + 8, :] = sum(halves(lon_ref[h, f]))
    for t in range(9):
        q_s[t] = stack_rows(halves(lon_ref[0, 12 + t])[1], halves(lon_ref[1, 12 + t])[1]).astype(BF16)
    rate = [by_lane(lambda z: rate_ref[q, z]) for q in range(6)]
    speeds = [by_lane(lambda z: speed_ref[class_ref[z], t]) for t in range(9)]
    for rb in range(2):
        rows = slice(8 * rb, 8 * rb + 8)
        adj = [sum(halves(lon_ref[rb, t])) for t in range(9)]
        done = coag(adj, [halves(lon_ref[rb, 12 + t])[0] for t in range(9)], rate)
        mark = p_s[11, rows, :]
        land = ((mark < 0) & (z_lane == 0)).astype(F32)
        size = jnp.abs(mark)
        above = jnp.where(z_lane == 15, 0.0, size)
        below = jnp.where(z_lane == 0, 0.0, lane_roll(size, 8))
        base = 1.0 - above - below - jnp.where(z_lane == 0, 0.1 + 0.3 * land, 0.0)
        for t in range(9):
            under = jnp.where(z_lane == 0, 0.0, lane_roll(done[t], 8))
            p_s[t, rows, :] = (
                done[t] * (base - speeds[t]) + under * (below + speeds[t]) + lane_roll(done[t], 120) * above
            )
    land_halo = (lane_roll(p_s[11], shift_of(0)) < 0).astype(F32)
    deposit = 0.1 + 0.3 * jnp.where(halo, land_halo, land_ref[...].astype(F32))
    land_out[...] = deposit
    last_lat = lat == lat_count - 1

    def assemble(z, sums):
        shift = shift_of(z)
        for t in range(9):
            put_rows(c_first, t, z, jnp.where(halo, lane_roll(p_s[t], shift), c_own[t, z]))
            traj_out[t, z] = jnp.where(halo_16, lane_roll(q_s[t], shift), traj_own[1, t, z])
        north = jnp.where(halo, lane_roll(p_s[9], shift), wind_own[1, z])
        north = jnp.where((row == 15) & last_lat, 0.0, north)
        east = jnp.where(halo, lane_roll(p_s[10], shift), wind_own[0, z])
        mix = jnp.where(halo, jnp.abs(lane_roll(p_s[11], shift)), mix_own[z])
        n_out[z, 0:8, :] = zero[:8]
        n_out[z, 8:24, :] = north
        n_out[z, 24:32, :] = zero[:8]
        e_out[z] = east
        d_out[z + 1] = jnp.where(z == 15, 0.0, mix)
        return sums

    def weigh(z, sums):
        shifted = [n_out[z, 6 + j : 22 + j, :] for j in range(4)]
        for j, value in enumerate(weights(e_out[z], shifted)):
            w_s[j, z] = value
        return sums

    steps = stages(scalars, c_first, w_s, a_s, b_s, traj_out, lambda z: d_out[z + 1], land_out[...], c_next, 2)
    sums = pipeline([(0, assemble), (1, weigh)] + steps, no_sums())
    sums = total(lat_count, 1, sums)
    for m in range(3):
        em_ref[m] = em_in[m] + sums[m]


def stages(scalars, c_in, w_ref, a_s, b_s, traj_ref, d, deposit, c_out, lag):
    def move(z, sums):
        moved(c_in, w_ref, a_s, z)
        return sums

    def do_react(z, sums):
        return react(scalars, lambda t: traj_ref[t, z], lambda t, rows: a_s[t, z, rows, :], b_s, z, sums)

    def mix(z, sums):
        mixed(scalars, b_s, d, deposit, lambda t, i, value: put_rows(c_out, t, i, value), z)
        return sums

    return [(lag, move), (lag + 1, do_react), (lag + 3, mix)]


def third_kernel(lat_count, *refs):
    traj_own, q_ref, d_ref, land_ref, w_ref, c_in, em_in = refs[0:7]
    scalars = refs[7:12]
    c_next, em_ref, traj_out = refs[12:15]
    a_s, b_s = refs[15:]
    core = lax.axis_index("lev")
    edge = 124
    halo_16 = halo_lanes_16(core)
    zero_ends(b_s)

    def complete(z, sums):
        shift = lax.rem(edge + 128 - 8 * jnp.bitwise_xor(z, 8 * (1 - core)), 128)
        for t in range(9):
            traj_out[t, z] = jnp.where(halo_16, lane_roll(q_ref[t], shift), traj_own[0, t, z])
        return sums

    steps = stages(scalars, c_in, w_ref, a_s, b_s, traj_out, lambda z: d_ref[z + 1], land_ref[...], c_next, 0)
    sums = total(lat_count, 2, pipeline(steps + [(0, complete)], no_sums()))
    for m in range(3):
        em_ref[m] = em_in[m] + sums[m]


def edge_kernel(lat_count, *refs):
    edges = 1 if lat_count == 2 else 2
    traj_1, c_first, c_next, n_ref, e_ref, d_ref, land_ref, c_last, w_ref, traj_0, em_ref = refs[0:11]
    lat_refs = refs[11 : 11 + 2 * edges]
    corner_refs = refs[11 + 2 * edges : 11 + 3 * edges]
    rate_ref, speed_ref, class_ref, prof_ref, coef_ref = refs[11 + 3 * edges : 16 + 3 * edges]
    keep_ref, send_ref = refs[16 + 3 * edges : 18 + 3 * edges]
    b_0, b_1, c_0, c_1, c_2, t_s, n_s, e_s, d_s, l_s, a_s, em_s, fin_s = refs[18 + 3 * edges :]
    far = 2 - edges
    core = lax.axis_index("lev")
    lat = lax.axis_index("lat")
    edge = jnp.where(core == 0, 120, 0)
    flip = 1 - core
    halo = halo_lanes(core, 8)
    sub = iota((8, 128), 0)
    zero = jnp.zeros((8, 128), F32)

    def run(upper, e):
        own_at, halo_at = (0, 8) if upper else (8, 0)
        own_row = 8 if upper else 0
        corner_ref = corner_refs[e]
        starts = (6, 4, 0) if upper else (2, 4, 8)
        b_bufs, c_bufs = (b_0, b_1, b_0), (c_0, c_1, c_2)

        def shift_of(z):
            return lax.rem(edge + 128 - 8 * jnp.bitwise_xor(z, 8 * flip), 128)

        def corner(tile, z):
            return halves(lane_roll(corner_ref[tile], shift_of(z)))

        def corner_sum(f, z):
            return sum(corner(f, z))

        land_c = corner_sum(11, 0)
        land_l = jnp.where(core == 0, sum(halves(lat_refs[2 * e][116])), sum(halves(lat_refs[2 * e + 1][116])))
        l_s[pl.ds(halo_at, 8), :] = 0.1 + 0.3 * (jnp.where(halo, land_c, land_l) < 0).astype(F32)
        l_s[pl.ds(own_at, 8), :] = land_ref[pl.ds(own_row, 8), :]
        d_s[0] = jnp.zeros((16, 128), F32)

        zero_ends(b_0)
        zero_ends(b_1)

        for s in range(2):
            msg = lat_refs[2 * e + s]

            def receive(four, _):
                for i in range(4):
                    l = 4 * four + i
                    z = 8 * jnp.bitwise_xor(s, core) + l
                    rate = [rate_ref[q, z] for q in range(6)]
                    adj, state = [], []
                    for t in range(9):
                        v0, v1 = halves(msg[t * 8 + l])
                        v2 = halves(msg[72 + t * 4 + 2 * four + i // 2])[i % 2]
                        adj.append(jnp.where(halo, corner_sum(t, z), v0 + v1))
                        tr2, tr1 = corner(12 + t, z)
                        tr0 = lane_roll(tr1, jnp.where(core == 0, 4, 124))
                        state.append(jnp.where(halo, tr2, v2))
                        near, rest = (1, -1) if upper else (0, 1)
                        t_s[1, t, z, pl.ds(halo_at + 4 * rest, 8), :] = v2
                        t_s[1, t, z, pl.ds(halo_at + 6 * rest, 8), :] = v1
                        t_s[0, t, z, pl.ds(halo_at + 6 * rest, 8), :] = v0
                        t_s[1, t, z, pl.ds(own_at, 8), :] = halves(traj_1[t, z])[near]
                        t_s[0, t, z, pl.ds(own_at, 8), :] = halves(traj_0[t, z])[near]
                        pltpu.store(t_s.at[1, t, z, pl.ds(halo_at, 8), :], tr1, mask=halo)
                        pltpu.store(t_s.at[0, t, z, pl.ds(halo_at, 8), :], tr0, mask=halo)
                    done = coag(adj, state, rate)
                    for t in range(9):
                        b_0[t, z + 1] = done[t]
                    north_h, north_l = halves(msg[108 + l])
                    mix_h, mix_l = halves(msg[116 + l])
                    north = jnp.where(halo, corner_sum(9, z), north_h + north_l)
                    mixing = jnp.where(halo, corner_sum(11, z), mix_h + mix_l)
                    e_s[z, pl.ds(halo_at + 4 * rest, 8), :] = north_l + mix_l
                    e_s[z, pl.ds(halo_at + 6 * rest, 8), :] = north_h + mix_h
                    if upper:
                        n_s[z, 0:8, :] = n_ref[z, 8:16, :]
                    else:
                        n_s[z, 24:32, :] = n_ref[z, 16:24, :]
                    n_s[z, pl.ds(8 + halo_at, 8), :] = north
                    n_s[z, pl.ds(8 + own_at, 8), :] = n_ref[z, pl.ds(8 + own_row, 8), :]
                    e_s[z, pl.ds(own_at, 8), :] = e_ref[z, pl.ds(own_row, 8), :]
                    pltpu.store(e_s.at[z, pl.ds(halo_at, 8), :], corner_sum(10, z), mask=halo)
                    d_s[z + 1, pl.ds(halo_at, 8), :] = jnp.where(z == 15, 0.0, jnp.abs(mixing))
                    d_s[z + 1, pl.ds(own_at, 8), :] = d_ref[z + 1, pl.ds(own_row, 8), :]
                return 0

            lax.fori_loop(0, 2, receive, 0)

        for m in range(3):
            for part in range(3):
                em_s[m, 8 * part : 8 * part + 8, :] = zero

        def mix(step, z):
            at = halo_at if step == 0 else starts[step - 1]
            b, c = b_bufs[step], c_bufs[step]
            c_ref = (c_first, c_next, c_last)[step]
            kind = class_ref[z]
            below, above = d_s[z, at : at + 8, :], d_s[z + 1, at : at + 8, :]
            base = 1.0 - above - below
            base = jnp.where(z == 0, base - l_s[at : at + 8, :], base)
            for t in range(9):
                speed = speed_ref[kind, t]
                value = b[t, z + 1] * (base - speed) + b[t, z] * (below + speed) + b[t, z + 2] * above
                if step < 2:
                    c[t, z, 8 + own_at : 16 + own_at, :] = c_ref[t, z, 8 + own_row : 16 + own_row, :]
                elif upper:
                    c[t, z, 0:16, :] = c_ref[t, z, 8:24, :]
                else:
                    c[t, z, 16:32, :] = c_ref[t, z, 8:24, :]
                c[t, z, 8 + at : 16 + at, :] = value

        def move(step, z, sums):
            at = starts[step]
            c = c_bufs[step]
            shifted = [n_s[z, 6 + at + i : 14 + at + i, :] for i in range(4)]
            w = weights(e_s[z, at : at + 8, :], shifted)
            adj = []
            for t in range(9):
                rows = [c[t, z, 6 + at + i : 14 + at + i, :] for i in range(5)]
                adj.append(transported(rows, w))
            if step == 2:
                for t in range(9):
                    fin_s[e, t, z] = adj[t]
                return sums
            share = [prof_ref[z] * coef_ref[t] for t in range(9)]
            sums = [sums[m] + sum(share[3 * m + j] * adj[3 * m + j] for j in range(3)) for m in range(3)]
            rate = [rate_ref[q, z] for q in range(6)]
            state = [t_s[1 - step, t, z, at : at + 8, :] for t in range(9)]
            done = coag(adj, state, rate)
            for t in range(9):
                b_bufs[step + 1][t, z + 1] = done[t]
            return sums

        def count(step, sums):
            at = starts[step]
            buf_row = sub + at
            rows = 2 + 2 * step
            if upper:
                good = (buf_row >= 8 - rows) & (buf_row < 8)
            else:
                good = (buf_row >= 8) & (buf_row < 8 + rows)
            for m in range(3):
                em_s[m, at : at + 8, :] = em_s[m, at : at + 8, :] + jnp.where(good, sums[m], 0.0)

        none = [zero, zero, zero]

        def mixing(step):
            def stage(z, sums):
                mix(step, z)
                return sums

            return stage

        def moving(step):
            return lambda z, sums: move(step, z, sums)

        count(0, pipeline([(0, mixing(0)), (1, moving(0)), (3, mixing(1))], none))

        def far_moving(z, sums):
            near = 0 if upper else 8
            w = [w_ref[i, z, near : near + 8, :] for i in range(9)]
            for t in range(9):
                rows = [c_last[t, z, near + 6 + i : near + 14 + i, :] for i in range(5)]
                fin_s[1, t, z] = transported(rows, w)
            return sums

        later = [(0, moving(1)), (2, mixing(2)), (3, moving(2))] + [(3, far_moving)] * far
        count(1, pipeline(later, none))
        for m in range(3):
            a_s[e, m] = em_s[m, own_at : own_at + 8, :]

    def finish(has_upper, has_lower, e_upper, e_lower):
        mine = (iota((16, 128), 1) < 64) == (core == 0)

        def rows_of(t, z):
            low = fin_s[e_lower, t, z]
            high = fin_s[e_upper, t, z]
            return stack_rows(low, high)

        def tracer(t, _):
            for l in range(8):
                keep_ref[t, l] = rows_of(t, 8 * core + l)
            for l in range(4):
                z = 8 * (1 - core) + l
                send_ref[t * 4 + l] = jnp.where(mine, rows_of(t, z), lane_roll(rows_of(t, z + 4), 64))

        for t in range(9):
            tracer(t, 0)
        for m in range(3):
            low = em_ref[m, 0:8, :]
            high = em_ref[m, 8:16, :]
            if has_upper:
                high = high + a_s[e_upper, m]
            if has_lower:
                low = low + a_s[e_lower, m]
            send_ref[36 + m] = stack_rows(low, high)

    if lat_count == 2:

        def south():
            run(True, 0)
            finish(True, False, 0, 1)

        def north():
            run(False, 0)
            finish(False, True, 1, 0)

        pl.when(lat == 0)(south)
        pl.when(lat == 1)(north)
    else:
        run(True, 0)
        run(False, 1)
        finish(True, True, 0, 1)


def join_kernel(keep_ref, send_ref, recv_ref, source_ref, out_ref, em_ref, part, em_part, sems):
    core = lax.axis_index("lev")
    mine = (iota((16, 128), 1) < 64) == (core == 0)
    source = source_ref[...].astype(F32)
    for m in range(3):
        em_part[m] = jnp.where(mine, send_ref[36 + m], recv_ref[36 + m]) * source
    copies = [pltpu.make_async_copy(em_part, em_ref, sems.at[9])]
    copies[0].start()
    for t in range(9):
        for l in range(4):
            got = recv_ref[t * 4 + l]
            part[t, l] = jnp.where(mine, keep_ref[t, l], got)
            part[t, l + 4] = jnp.where(mine, keep_ref[t, l + 4], lane_roll(got, 64))
        copies.append(pltpu.make_async_copy(part.at[t], out_ref.at[t], sems.at[t]))
        copies[-1].start()
    for copy in copies:
        copy.wait()


def corner_kernel(lon_ref, out_ref):
    out_ref[...] = lon_ref[1 - lax.axis_index("lat")]


def shape(*dims, dtype=F32):
    return jax.ShapeDtypeStruct(dims, dtype)


def call(kernel, outs, scratch, *args, specs=None, out_specs=None, mib=32):
    return pl.pallas_call(
        kernel,
        out_shape=outs,
        in_specs=specs or [VMEM] * len(args),
        out_specs=out_specs or [VMEM] * len(outs),
        scratch_shapes=scratch,
        compiler_params=pltpu.CompilerParams(vmem_limit_bytes=mib * 1024 * 1024),
    )(*args)


def shards(
    adjoint_in,
    trajectory,
    courant,
    mixing,
    coag_rates,
    settle_speed,
    settle_class,
    emis_profile,
    emis_coef,
    land_mask,
    source_mask,
):
    lat_count = lax.axis_size("lat")
    lon_count = lax.axis_size("lon")
    edges = 1 if lat_count == 2 else 2
    swap = [(0, 1), (1, 0)]

    def over_lev(value):
        return lax.ppermute(value, "lev", swap)

    def lat_moves(messages):
        if edges == 1:
            return [lax.ppermute(messages[0], "lat", swap)]
        up = [(j, j + 1) for j in range(lat_count - 1)]
        down = [(j + 1, j) for j in range(lat_count - 1)]
        return [lax.ppermute(messages[-1], "lat", down), lax.ppermute(messages[0], "lat", up)]

    def bind(kernel):
        def run(*refs):
            return kernel(lat_count, *refs)

        return run

    given = (adjoint_in, trajectory, courant, mixing, land_mask)
    field, traj, land = call(
        load_kernel,
        [
            shape(12, *adjoint_in.shape[1:]),
            jax.ShapeDtypeStruct(trajectory.shape, trajectory.dtype),
            jax.ShapeDtypeStruct(land_mask.shape, land_mask.dtype),
        ],
        [pltpu.SemaphoreType.DMA((5,))],
        *[pltpu.with_memory_space_constraint(v, pltpu.HBM) for v in given],
        specs=[pl.BlockSpec(memory_space=pltpu.HBM)] * 5,
        mib=16,
    )
    own = (field, traj)
    other = (over_lev(field), over_lev(trajectory))
    half = call(
        lon_start_kernel, [shape(12, 16, 128), shape(27, 16, 128, dtype=BF16)], [], *own, land, mib=16
    )
    (lon_out,) = call(
        lon_pack_kernel, [shape(2, LON_TILES, 16, 128, dtype=BF16)], [], *other, land, *half, mib=16
    )
    lat_out = call(
        bind(lat_pack_kernel), [shape(LAT_TILES, 16, 128, dtype=BF16)] * edges, [], *own, land, mib=16
    )
    lat_in = lat_moves(lat_out)
    lon_pairs = []
    for i in range(lon_count):
        lon_pairs.append((2 * i + 1, 2 * ((i + 1) % lon_count)))
        lon_pairs.append((2 * i, 2 * ((i - 1) % lon_count) + 1))
    lon_in = lax.ppermute(lon_out, ("lon", "lev"), lon_pairs)
    scalars = (coag_rates, settle_speed, settle_class, emis_profile, emis_coef)
    state = pltpu.VMEM((9, 16, 16, 128), F32)
    between = pltpu.VMEM((9, 18, 16, 128), F32)
    padded = shape(9, 16, 32, 128)
    c_own, emis, traj_own, wind_own, mix_own = call(
        bind(first_kernel),
        [
            shape(9, 16, 16, 128),
            shape(3, 16, 128),
            shape(2, 9, 16, 16, 128, dtype=BF16),
            shape(2, 16, 16, 128),
            shape(16, 16, 128),
        ],
        [between],
        *own,
        *other,
        land,
        *scalars,
        specs=[VMEM] * 5 + [SMEM] * 5,
    )
    lon_in, c_own = lax.optimization_barrier((lon_in, c_own))
    if edges == 1:
        corner_out = call(corner_kernel, [shape(LON_TILES, 16, 128, dtype=BF16)], [], lon_in, mib=16)
    else:
        corner_out = [lon_in[1], lon_in[0]]
    corner_in = lat_moves(corner_out)
    traj_1, c_first, c_next, north, east, mix, land_all, weight, emis, strip = call(
        bind(second_kernel),
        [
            shape(9, 16, 16, 128, dtype=BF16),
            padded,
            padded,
            shape(16, 32, 128),
            shape(16, 16, 128),
            shape(17, 16, 128),
            shape(16, 128),
            shape(9, 16, 16, 128),
            shape(3, 16, 128),
            shape(9, 16, 128, dtype=BF16),
        ],
        [state, between, pltpu.VMEM((12, 16, 128), F32)],
        land,
        lon_in,
        c_own,
        emis,
        traj_own,
        wind_own,
        mix_own,
        *scalars,
        specs=[VMEM] * 7 + [SMEM] * 5,
    )
    c_next, *lat_in = lax.optimization_barrier((c_next, *lat_in))
    c_last, emis, traj_0 = call(
        bind(third_kernel),
        [padded, shape(3, 16, 128), shape(9, 16, 16, 128, dtype=BF16)],
        [state, between],
        traj_own,
        strip,
        mix,
        land_all,
        weight,
        c_next,
        emis,
        *scalars,
        specs=[VMEM] * 7 + [SMEM] * 5,
    )
    inner = (traj_1, c_first, c_next, north, east, mix, land_all, c_last, weight, traj_0, emis)
    lat_all = []
    for value in lat_in:
        lat_all += [value, over_lev(value)]
    keep, send = call(
        bind(edge_kernel),
        [shape(9, 8, 16, 128), shape(39, 16, 128)],
        [
            pltpu.VMEM((9, 18, 8, 128), F32),
            pltpu.VMEM((9, 18, 8, 128), F32),
            pltpu.VMEM((9, 16, 32, 128), F32),
            pltpu.VMEM((9, 16, 32, 128), F32),
            pltpu.VMEM((9, 16, 32, 128), F32),
            pltpu.VMEM((2, 9, 16, 16, 128), F32),
            pltpu.VMEM((16, 32, 128), F32),
            pltpu.VMEM((16, 16, 128), F32),
            pltpu.VMEM((17, 16, 128), F32),
            pltpu.VMEM((16, 128), F32),
            pltpu.VMEM((edges, 3, 8, 128), F32),
            pltpu.VMEM((3, 24, 128), F32),
            pltpu.VMEM((2, 9, 16, 8, 128), F32),
        ],
        *inner,
        *lat_all,
        *corner_in,
        *scalars,
        specs=[VMEM] * (11 + 3 * edges) + [SMEM] * 5,
        mib=40,
    )
    recv = over_lev(send)
    out, emis = call(
        join_kernel,
        [shape(9, 8, 16, 128), shape(3, 16, 128)],
        [pltpu.VMEM((9, 8, 16, 128), F32), pltpu.VMEM((3, 16, 128), F32), pltpu.SemaphoreType.DMA((10,))],
        keep,
        send,
        recv,
        source_mask,
        out_specs=[pl.BlockSpec(memory_space=pltpu.HBM)] * 2,
    )
    return (out, emis)


def solution(mesh):
    return jax.shard_map(
        shards,
        mesh=mesh,
        in_specs=(
            P(None, "lev", "lat", "lon"),
            P(None, None, "lev", "lat", "lon"),
            P(None, "lev", "lat", "lon"),
            P("lev", "lat", "lon"),
            P(),
            P(),
            P(),
            P(),
            P(),
            P("lat", "lon"),
            P("lat", "lon"),
        ),
        out_specs=(P(None, "lev", "lat", "lon"), P(None, "lat", "lon")),
        check_vma=False,
    )
```

```python
import jax
import jax.numpy as jnp
from jax import lax
from jax.experimental import pallas as pl
from jax.experimental.pallas import tpu as pltpu
from jax.sharding import PartitionSpec as P

F32 = jnp.float32
BF16 = jnp.bfloat16
VMEM = pl.BlockSpec(memory_space=pltpu.VMEM)
SMEM = pl.BlockSpec(memory_space=pltpu.SMEM)
PAIRS = ((0, 1, 3), (0, 2, 4), (1, 2, 5))
LAT_TILES = 124
LON_TILES = 21


def iota(shape, axis):
    return lax.broadcasted_iota(jnp.int32, shape, axis)


def split(value):
    high = value.astype(BF16)
    low = (value - high.astype(F32)).astype(BF16)
    return high, low


def stack_rows(top, bottom):
    return jnp.concatenate([top, bottom], axis=0)


def halves(tile):
    wide = tile.astype(F32)
    return wide[:8], wide[8:]


def coag(adj, state, rate):
    out = list(adj)
    kn = {}
    for m, p, q in PAIRS:
        kn[m, p] = rate[q] * state[3 * p]
    for m in range(3):
        total = (2.0 * rate[m]) * state[3 * m]
        for p in range(m + 1, 3):
            total = total + kn[m, p]
        out[3 * m] = out[3 * m] - total * adj[3 * m]
        out[3 * m + 1] = out[3 * m + 1] + (2.0 * rate[m]) * (state[3 * m + 1] * adj[3 * m + 2])
    for m, p, q in PAIRS:
        d_vol = adj[3 * p + 1] - adj[3 * m + 1]
        d_six = adj[3 * p + 2] - adj[3 * m + 2]
        inner = d_vol * state[3 * m + 1] + d_six * state[3 * m + 2] - adj[3 * m] * state[3 * m]
        cross = (2.0 * rate[q]) * adj[3 * p + 2]
        out[3 * p] = out[3 * p] + rate[q] * inner
        out[3 * m + 1] = out[3 * m + 1] + (kn[m, p] * d_vol + cross * state[3 * p + 1])
        out[3 * p + 1] = out[3 * p + 1] + cross * state[3 * m + 1]
        out[3 * m + 2] = out[3 * m + 2] + kn[m, p] * d_six
    return out


def lane_roll(value, shift):
    return pltpu.roll(value, shift, 1)


def weights(east, north):
    pos = jnp.maximum(east, 0.0)
    neg = jnp.minimum(east, 0.0)
    pos_1 = lane_roll(pos, 127)
    neg_1 = lane_roll(neg, 1)
    neg_2 = lane_roll(neg, 2)
    n_pos = jnp.maximum(north[2], 0.0)
    n_pos_1 = jnp.maximum(north[3], 0.0)
    n_neg_1 = jnp.minimum(north[1], 0.0)
    n_neg_2 = jnp.minimum(north[0], 0.0)
    centre = 1.0 + 1.5 * ((neg_1 - pos) + (n_neg_1 - n_pos))
    return (
        centre,
        0.5 * neg_2,
        -1.5 * neg_1 - 0.5 * neg_2,
        1.5 * pos + 0.5 * pos_1,
        -0.5 * pos_1,
        0.5 * n_neg_2,
        -1.5 * n_neg_1 - 0.5 * n_neg_2,
        1.5 * n_pos + 0.5 * n_pos_1,
        -0.5 * n_pos_1,
    )


def transported(rows, w):
    mid = rows[2]
    lon = (w[1] * lane_roll(mid, 2) + w[2] * lane_roll(mid, 1)) + (
        w[3] * lane_roll(mid, 127) + w[4] * lane_roll(mid, 126)
    )
    lat = (w[5] * rows[0] + w[6] * rows[1]) + (w[7] * rows[3] + w[8] * rows[4])
    return w[0] * mid + (lon + lat)


def level_scalars(z, rate_ref, speed_ref, class_ref):
    rate = [rate_ref[q, z] for q in range(6)]
    kind = class_ref[z]
    speed = [speed_ref[kind, t] for t in range(9)]
    return rate, speed


def halo_lanes(core, rows):
    lane = iota((rows, 128), 1)
    return jnp.where(core == 0, (lane >= 120).astype(jnp.int32), (lane < 8).astype(jnp.int32)) > 0


def halo_lanes_16(core):
    middle = jnp.where(core == 0, 123.5, 3.5).astype(F32)
    return jnp.abs(iota((16, 128), 1).astype(F32) - middle).astype(BF16) <= jnp.full((16, 128), 3.5, BF16)


def load_kernel(adj_ref, traj_ref, wind_ref, mix_ref, land_ref, field_out, traj_out, land_out, sems):
    pairs = [(traj_ref, traj_out), (adj_ref, field_out.at[pl.ds(0, 9)]), (wind_ref, field_out.at[pl.ds(9, 2)])]
    pairs += [(mix_ref, field_out.at[11]), (land_ref, land_out)]
    copies = [pltpu.make_async_copy(source, target, sems.at[i]) for i, (source, target) in enumerate(pairs)]
    for copy in copies:
        copy.start()
    for copy in copies:
        copy.wait()


def parts_of(field_ref, traj_ref):
    return field_ref.at[pl.ds(0, 9)], traj_ref, field_ref.at[pl.ds(9, 2)], field_ref.at[11]


def marked(mix, land, z):
    return jnp.where((land * (z == 0).astype(jnp.int32)) > 0, -mix, mix)


def lat_pack_kernel(lat_count, field_ref, traj_ref, land_ref, *outs):
    adj_ref, traj_ref, wind_ref, mix_ref = parts_of(field_ref, traj_ref)
    core = lax.axis_index("lev")
    lat = lax.axis_index("lat")

    def fill(out_ref, high_rows):
        base = 8 if high_rows else 0
        sub = iota((8, 128), 0)
        keep = (sub >= 2) if high_rows else (sub < 6)

        def rolled(value, shift):
            return pltpu.roll(value, shift, 0)

        def tracer(t, _):
            v2s = []
            for l in range(8):
                adj = adj_ref[t, l, base : base + 8, :]
                high = adj.astype(BF16).astype(F32)
                low = adj - high
                tr = [traj_ref[k, t, l].astype(F32)[base : base + 8] for k in range(3)]
                if high_rows:
                    extra = (rolled(tr[0], 2), rolled(tr[1], 2), rolled(tr[1], 4))
                else:
                    extra = (rolled(tr[0], 6), rolled(tr[1], 6), rolled(tr[1], 4))
                v0 = jnp.where(keep, high, extra[0])
                v1 = jnp.where(keep, low, extra[1])
                v2s.append(jnp.where(keep, tr[2], extra[2]))
                out_ref[t * 8 + l] = stack_rows(v0, v1).astype(BF16)
            for j in range(4):
                out_ref[72 + t * 4 + j] = stack_rows(v2s[2 * j], v2s[2 * j + 1]).astype(BF16)

        for t in range(9):
            tracer(t, 0)

        def level(l, _):
            rows = slice(base, base + 8)
            z = l + 8 * core
            north, east = wind_ref[1, l, rows, :], wind_ref[0, l, rows, :]
            parts = []
            for value in (north, marked(mix_ref[l, rows, :], land_ref[rows, :], z), east):
                high = value.astype(BF16).astype(F32)
                parts += [high, value - high]
            one, two = (2, 4) if high_rows else (6, 4)
            north_h, north_l, mix_h, mix_l, east_h, east_l = parts
            out_ref[108 + l] = stack_rows(
                jnp.where(keep, north_h, rolled(east_h, one)), jnp.where(keep, north_l, rolled(east_h, two))
            ).astype(BF16)
            out_ref[116 + l] = stack_rows(
                jnp.where(keep, mix_h, rolled(east_l, one)), jnp.where(keep, mix_l, rolled(east_l, two))
            ).astype(BF16)

        for l in range(8):
            level(l, 0)

    if lat_count == 2:
        pl.when(lat == 0)(lambda: fill(outs[0], True))
        pl.when(lat == 1)(lambda: fill(outs[0], False))
    else:
        fill(outs[0], True)
        fill(outs[1], False)


def gather_edges(core, s, blocks, land, f_kind, t_kind, f_done, t_done):
    edge = jnp.where(core == 0, 0, 120)
    slot = iota((16, 128), 1) // 8
    slot_16 = slot.astype(BF16)
    adj_ref, traj_ref, wind_ref, mix_ref = blocks

    def gather(read, acc, at):
        for l in range(8):
            g = 8 * s + l
            shift = lax.rem(8 * g - edge + 128, 128)
            acc = jnp.where(at == g, lane_roll(read(l), shift), acc)
        return acc

    for t in range(9):
        f_done(t, gather(lambda l: adj_ref[t, l], f_kind(t), slot))
        t_done(t, [gather(lambda l: traj_ref[k, t, l], t_kind(9 * k + t), slot_16) for k in range(3)])
    bottom = jnp.bitwise_xor(s, core)
    f_done(9, gather(lambda l: wind_ref[1, l], f_kind(9), slot))
    f_done(10, gather(lambda l: wind_ref[0, l], f_kind(10), slot))
    f_done(11, gather(lambda l: marked(mix_ref[l], land, bottom) if l == 0 else mix_ref[l], f_kind(11), slot))


def lon_start_kernel(field_ref, traj_ref, land_ref, f_ref, t_ref):
    def f_done(f, value):
        f_ref[f] = value

    def t_done(t, values):
        for k in range(3):
            t_ref[9 * k + t] = values[k]

    gather_edges(
        lax.axis_index("lev"),
        0,
        parts_of(field_ref, traj_ref),
        land_ref[...],
        lambda f: jnp.zeros((16, 128), F32),
        lambda f: jnp.zeros((16, 128), BF16),
        f_done,
        t_done,
    )


def lon_pack_kernel(field_ref, traj_ref, land_ref, f_ref, t_ref, out_ref):
    core = lax.axis_index("lev")
    far = (jnp.bitwise_xor((iota((16, 128), 1) // 4) % 2, core)).astype(F32).astype(BF16)

    def pair(f, first, second):
        tops, bottoms = halves(first), halves(second)
        for h in range(2):
            out_ref[h, f] = stack_rows(tops[h], bottoms[h]).astype(BF16)

    def f_done(f, value):
        high, low = split(value)
        pair(f, high, low)

    def t_done(t, tr):
        both = jnp.where(far > 0, lane_roll(tr[0], jnp.where(core == 0, 4, 124)), tr[1])
        pair(12 + t, tr[2], both)

    gather_edges(
        core,
        1,
        parts_of(field_ref, traj_ref),
        land_ref[...],
        lambda f: f_ref[f],
        lambda f: t_ref[f],
        f_done,
        t_done,
    )


def put_rows(ref, t, z, value):
    zero = jnp.zeros((8, 128), F32)
    ref[t, z, 0:8, :] = zero
    ref[t, z, 8:24, :] = value
    ref[t, z, 24:32, :] = zero


def zero_ends(ref):
    for t in range(9):
        for z in (0, 17):
            ref[t, z] = jnp.zeros(ref.shape[2:], F32)


def react(scalars, traj, a_in, b_s, z, sums):
    rate_ref, speed_ref, class_ref, prof_ref, coef_ref = scalars
    rate = [rate_ref[q, z] for q in range(6)]
    share = [prof_ref[z] * coef_ref[t] for t in range(9)]
    tiles = [traj(t).astype(F32) for t in range(9)]
    parts = []
    for rb in range(2):
        rows = slice(8 * rb, 8 * rb + 8)
        adj = [a_in(t, rows) for t in range(9)]
        done = coag(adj, [tile[rows] for tile in tiles], rate)
        for t in range(9):
            b_s[t, z + 1, rows, :] = done[t]
        parts.append([sums[rb][m] + sum(share[3 * m + j] * adj[3 * m + j] for j in range(3)) for m in range(3)])
    return parts


def mixed(scalars, b_s, d, deposit, put, z):
    rate_ref, speed_ref, class_ref, prof_ref, coef_ref = scalars
    kind = class_ref[z]
    below, above = d(z - 1), d(z)
    base = 1.0 - above - below
    base = jnp.where(z == 0, base - deposit, base)
    for t in range(9):
        speed = speed_ref[kind, t]
        put(t, z, b_s[t, z + 1] * (base - speed) + b_s[t, z] * (below + speed) + b_s[t, z + 2] * above)


def moved(c_in, w_ref, a_to, z):
    for rb in range(2):
        rows = slice(8 * rb, 8 * rb + 8)
        w = [w_ref[i, z, rows, :] for i in range(9)]
        for t in range(9):
            shifted = [c_in[t, z, 8 * rb + 6 + i : 8 * rb + 14 + i, :] for i in range(5)]
            a_to[t, z, rows, :] = transported(shifted, w)


def no_sums():
    return [[jnp.zeros((8, 128), F32)] * 3, [jnp.zeros((8, 128), F32)] * 3]


def total(lat_count, step, sums):
    lat = lax.axis_index("lat")
    row = iota((16, 128), 0)
    sums = [stack_rows(sums[0][m], sums[1][m]) for m in range(3)]
    if step == 0:
        return sums
    low, high = 2 * step, 15 - 2 * step
    if lat_count == 2:
        good = ((row <= high) | (lat != 0)) & ((row >= low) | (lat == 0))
    else:
        good = (row <= high) & (row >= low)
    return [jnp.where(good, v, 0.0) for v in sums]


def pipeline(stages, carry=None):
    stages = sorted(stages, key=lambda stage: -stage[0])
    depth = stages[0][0]

    def at(z, carry):
        for lag, stage in stages:
            if 0 <= z - lag < 16:
                carry = stage(z - lag, carry)
        return carry

    for z in range(depth):
        carry = at(z, carry)
    for z in range(depth, 16 + depth):
        carry = at(z, carry)
    return carry


def first_kernel(lat_count, *refs):
    own, other = parts_of(*refs[0:2]), parts_of(*refs[2:4])
    land_ref = refs[4]
    scalars = refs[5:10]
    c_out, em_ref, traj_out, wind_out, mix_out = refs[10:15]
    b_s = refs[15]
    core = lax.axis_index("lev")
    zero_ends(b_s)
    deposit = 0.1 + 0.3 * land_ref[...].astype(F32)
    nothing = jnp.zeros((16, 128), F32)

    def put(t, z, value):
        c_out[t, z] = value

    def run(low, high):
        def level(r, z, l, sums):
            for k in range(2):
                for t in range(9):
                    traj_out[k, t, z] = r[1][k, t, l]
            for i in range(2):
                wind_out[i, z] = r[2][i, l]
            mix_out[z] = r[3][l]
            return react(scalars, lambda t: r[1][2, t, l], lambda t, rows: r[0][t, l, rows, :], b_s, z, sums)

        def mix(z):
            def d(i):
                if isinstance(i, int) and i in (-1, 15):
                    return nothing
                return mix_out[i]

            mixed(scalars, b_s, d, deposit, put, z)

        sums = no_sums()
        for z in range(3):
            sums = level(low, z, z, sums)
        mix(0)

        def lower(z, sums):
            mix(z - 2)
            return level(low, z, z, sums)

        sums = lax.fori_loop(3, 8, lower, sums)

        def upper(z, sums):
            mix(z - 2)
            return level(high, z, z - 8, sums)

        sums = lax.fori_loop(8, 16, upper, sums)
        mix(14)
        mix(15)
        sums = total(lat_count, 0, sums)
        for m in range(3):
            em_ref[m] = sums[m]

    pl.when(core == 0)(lambda: run(own, other))
    pl.when(core == 1)(lambda: run(other, own))


def second_kernel(lat_count, *refs):
    land_ref, lon_ref, c_own, em_in, traj_own, wind_own, mix_own = refs[0:7]
    scalars = refs[7:12]
    rate_ref, speed_ref, class_ref, prof_ref, coef_ref = scalars
    traj_out, c_first, c_next, n_out, e_out, d_out, land_out, w_s, em_ref, q_s = refs[12:22]
    a_s, b_s, p_s = refs[22:]
    core = lax.axis_index("lev")
    lat = lax.axis_index("lat")
    edge = jnp.where(core == 0, 120, 0)
    halo = halo_lanes(core, 16)
    halo_16 = halo_lanes_16(core)
    row = iota((16, 128), 0)
    zero = jnp.zeros((16, 128), F32)
    z_lane = jnp.bitwise_xor(iota((8, 128), 1) // 8, 8 * (1 - core))
    zero_ends(b_s)
    d_out[0] = zero

    def shift_of(z):
        return lax.rem(edge + 128 - 8 * jnp.bitwise_xor(z, 8 * (1 - core)), 128)

    def by_lane(read):
        acc = jnp.zeros((8, 128), F32)
        for z in range(16):
            acc = jnp.where(z_lane == z, read(z), acc)
        return acc

    for f in range(9, 12):
        for h in range(2):
            p_s[f, 8 * h : 8 * h + 8, :] = sum(halves(lon_ref[h, f]))
    for t in range(9):
        q_s[t] = stack_rows(halves(lon_ref[0, 12 + t])[1], halves(lon_ref[1, 12 + t])[1]).astype(BF16)
    rate = [by_lane(lambda z: rate_ref[q, z]) for q in range(6)]
    speeds = [by_lane(lambda z: speed_ref[class_ref[z], t]) for t in range(9)]
    for rb in range(2):
        rows = slice(8 * rb, 8 * rb + 8)
        adj = [sum(halves(lon_ref[rb, t])) for t in range(9)]
        done = coag(adj, [halves(lon_ref[rb, 12 + t])[0] for t in range(9)], rate)
        mark = p_s[11, rows, :]
        land = ((mark < 0) & (z_lane == 0)).astype(F32)
        size = jnp.abs(mark)
        above = jnp.where(z_lane == 15, 0.0, size)
        below = jnp.where(z_lane == 0, 0.0, lane_roll(size, 8))
        base = 1.0 - above - below - jnp.where(z_lane == 0, 0.1 + 0.3 * land, 0.0)
        for t in range(9):
            under = jnp.where(z_lane == 0, 0.0, lane_roll(done[t], 8))
            p_s[t, rows, :] = (
                done[t] * (base - speeds[t]) + under * (below + speeds[t]) + lane_roll(done[t], 120) * above
            )
    land_halo = (lane_roll(p_s[11], shift_of(0)) < 0).astype(F32)
    deposit = 0.1 + 0.3 * jnp.where(halo, land_halo, land_ref[...].astype(F32))
    land_out[...] = deposit
    last_lat = lat == lat_count - 1

    def assemble(z, sums):
        shift = shift_of(z)
        for t in range(9):
            put_rows(c_first, t, z, jnp.where(halo, lane_roll(p_s[t], shift), c_own[t, z]))
            traj_out[t, z] = jnp.where(halo_16, lane_roll(q_s[t], shift), traj_own[1, t, z])
        north = jnp.where(halo, lane_roll(p_s[9], shift), wind_own[1, z])
        north = jnp.where((row == 15) & last_lat, 0.0, north)
        east = jnp.where(halo, lane_roll(p_s[10], shift), wind_own[0, z])
        mix = jnp.where(halo, jnp.abs(lane_roll(p_s[11], shift)), mix_own[z])
        n_out[z, 0:8, :] = zero[:8]
        n_out[z, 8:24, :] = north
        n_out[z, 24:32, :] = zero[:8]
        e_out[z] = east
        d_out[z + 1] = jnp.where(z == 15, 0.0, mix)
        return sums

    def weigh(z, sums):
        shifted = [n_out[z, 6 + j : 22 + j, :] for j in range(4)]
        for j, value in enumerate(weights(e_out[z], shifted)):
            w_s[j, z] = value
        return sums

    steps = stages(scalars, c_first, w_s, a_s, b_s, traj_out, lambda z: d_out[z + 1], land_out[...], c_next, 2)
    sums = pipeline([(0, assemble), (1, weigh)] + steps, no_sums())
    sums = total(lat_count, 1, sums)
    for m in range(3):
        em_ref[m] = em_in[m] + sums[m]


def stages(scalars, c_in, w_ref, a_s, b_s, traj_ref, d, deposit, c_out, lag):
    def move(z, sums):
        moved(c_in, w_ref, a_s, z)
        return sums

    def do_react(z, sums):
        return react(scalars, lambda t: traj_ref[t, z], lambda t, rows: a_s[t, z, rows, :], b_s, z, sums)

    def mix(z, sums):
        mixed(scalars, b_s, d, deposit, lambda t, i, value: put_rows(c_out, t, i, value), z)
        return sums

    return [(lag, move), (lag + 2, do_react), (lag + 5, mix)]


def third_kernel(lat_count, *refs):
    traj_own, q_ref, d_ref, land_ref, w_ref, c_in, em_in = refs[0:7]
    scalars = refs[7:12]
    c_next, em_ref, traj_out = refs[12:15]
    a_s, b_s = refs[15:]
    core = lax.axis_index("lev")
    edge = 124
    halo_16 = halo_lanes_16(core)
    zero_ends(b_s)

    def complete(z, sums):
        shift = lax.rem(edge + 128 - 8 * jnp.bitwise_xor(z, 8 * (1 - core)), 128)
        for t in range(9):
            traj_out[t, z] = jnp.where(halo_16, lane_roll(q_ref[t], shift), traj_own[0, t, z])
        return sums

    steps = stages(scalars, c_in, w_ref, a_s, b_s, traj_out, lambda z: d_ref[z + 1], land_ref[...], c_next, 0)
    sums = total(lat_count, 2, pipeline(steps + [(0, complete)], no_sums()))
    for m in range(3):
        em_ref[m] = em_in[m] + sums[m]


def edge_kernel(lat_count, *refs):
    edges = 1 if lat_count == 2 else 2
    traj_1, c_first, c_next, n_ref, e_ref, d_ref, land_ref, c_last, w_ref, traj_0, em_ref = refs[0:11]
    lat_refs = refs[11 : 11 + 2 * edges]
    corner_refs = refs[11 + 2 * edges : 11 + 3 * edges]
    rate_ref, speed_ref, class_ref, prof_ref, coef_ref = refs[11 + 3 * edges : 16 + 3 * edges]
    keep_ref, send_ref = refs[16 + 3 * edges : 18 + 3 * edges]
    b_0, b_1, c_0, c_1, c_2, t_s, n_s, e_s, d_s, l_s, a_s, em_s, fin_s = refs[18 + 3 * edges :]
    far = 2 - edges
    core = lax.axis_index("lev")
    lat = lax.axis_index("lat")
    edge = jnp.where(core == 0, 120, 0)
    flip = 1 - core
    halo = halo_lanes(core, 8)
    sub = iota((8, 128), 0)
    zero = jnp.zeros((8, 128), F32)

    def run(upper, e):
        own_at, halo_at = (0, 8) if upper else (8, 0)
        own_row = 8 if upper else 0
        corner_ref = corner_refs[e]
        starts = (6, 4, 0) if upper else (2, 4, 8)
        b_bufs, c_bufs = (b_0, b_1, b_0), (c_0, c_1, c_2)

        def shift_of(z):
            return lax.rem(edge + 128 - 8 * jnp.bitwise_xor(z, 8 * flip), 128)

        def corner(tile, z):
            return halves(lane_roll(corner_ref[tile], shift_of(z)))

        def corner_sum(f, z):
            return sum(corner(f, z))

        land_c = corner_sum(11, 0)
        land_l = jnp.where(core == 0, sum(halves(lat_refs[2 * e][116])), sum(halves(lat_refs[2 * e + 1][116])))
        l_s[pl.ds(halo_at, 8), :] = 0.1 + 0.3 * (jnp.where(halo, land_c, land_l) < 0).astype(F32)
        l_s[pl.ds(own_at, 8), :] = land_ref[pl.ds(own_row, 8), :]
        d_s[0] = jnp.zeros((16, 128), F32)

        zero_ends(b_0)
        zero_ends(b_1)

        for s in range(2):
            msg = lat_refs[2 * e + s]

            def receive(four, _):
                for i in range(4):
                    l = 4 * four + i
                    z = 8 * jnp.bitwise_xor(s, core) + l
                    rate = [rate_ref[q, z] for q in range(6)]
                    adj, state = [], []
                    for t in range(9):
                        v0, v1 = halves(msg[t * 8 + l])
                        v2 = halves(msg[72 + t * 4 + 2 * four + i // 2])[i % 2]
                        adj.append(jnp.where(halo, corner_sum(t, z), v0 + v1))
                        tr2, tr1 = corner(12 + t, z)
                        tr0 = lane_roll(tr1, jnp.where(core == 0, 4, 124))
                        state.append(jnp.where(halo, tr2, v2))
                        near, rest = (1, -1) if upper else (0, 1)
                        t_s[1, t, z, pl.ds(halo_at + 4 * rest, 8), :] = v2
                        t_s[1, t, z, pl.ds(halo_at + 6 * rest, 8), :] = v1
                        t_s[0, t, z, pl.ds(halo_at + 6 * rest, 8), :] = v0
                        t_s[1, t, z, pl.ds(own_at, 8), :] = halves(traj_1[t, z])[near]
                        t_s[0, t, z, pl.ds(own_at, 8), :] = halves(traj_0[t, z])[near]
                        pltpu.store(t_s.at[1, t, z, pl.ds(halo_at, 8), :], tr1, mask=halo)
                        pltpu.store(t_s.at[0, t, z, pl.ds(halo_at, 8), :], tr0, mask=halo)
                    done = coag(adj, state, rate)
                    for t in range(9):
                        b_0[t, z + 1] = done[t]
                    north_h, north_l = halves(msg[108 + l])
                    mix_h, mix_l = halves(msg[116 + l])
                    north = jnp.where(halo, corner_sum(9, z), north_h + north_l)
                    mixing = jnp.where(halo, corner_sum(11, z), mix_h + mix_l)
                    e_s[z, pl.ds(halo_at + 4 * rest, 8), :] = north_l + mix_l
                    e_s[z, pl.ds(halo_at + 6 * rest, 8), :] = north_h + mix_h
                    if upper:
                        n_s[z, 0:8, :] = n_ref[z, 8:16, :]
                    else:
                        n_s[z, 24:32, :] = n_ref[z, 16:24, :]
                    n_s[z, pl.ds(8 + halo_at, 8), :] = north
                    n_s[z, pl.ds(8 + own_at, 8), :] = n_ref[z, pl.ds(8 + own_row, 8), :]
                    e_s[z, pl.ds(own_at, 8), :] = e_ref[z, pl.ds(own_row, 8), :]
                    pltpu.store(e_s.at[z, pl.ds(halo_at, 8), :], corner_sum(10, z), mask=halo)
                    d_s[z + 1, pl.ds(halo_at, 8), :] = jnp.where(z == 15, 0.0, jnp.abs(mixing))
                    d_s[z + 1, pl.ds(own_at, 8), :] = d_ref[z + 1, pl.ds(own_row, 8), :]
                return 0

            lax.fori_loop(0, 2, receive, 0)

        for m in range(3):
            for part in range(3):
                em_s[m, 8 * part : 8 * part + 8, :] = zero

        def mix(step, z):
            at = halo_at if step == 0 else starts[step - 1]
            b, c = b_bufs[step], c_bufs[step]
            c_ref = (c_first, c_next, c_last)[step]
            kind = class_ref[z]
            below, above = d_s[z, at : at + 8, :], d_s[z + 1, at : at + 8, :]
            base = 1.0 - above - below
            base = jnp.where(z == 0, base - l_s[at : at + 8, :], base)
            for t in range(9):
                speed = speed_ref[kind, t]
                value = b[t, z + 1] * (base - speed) + b[t, z] * (below + speed) + b[t, z + 2] * above
                if step < 2:
                    c[t, z, 8 + own_at : 16 + own_at, :] = c_ref[t, z, 8 + own_row : 16 + own_row, :]
                elif upper:
                    c[t, z, 0:16, :] = c_ref[t, z, 8:24, :]
                else:
                    c[t, z, 16:32, :] = c_ref[t, z, 8:24, :]
                c[t, z, 8 + at : 16 + at, :] = value

        def move(step, z, sums):
            at = starts[step]
            c = c_bufs[step]
            shifted = [n_s[z, 6 + at + i : 14 + at + i, :] for i in range(4)]
            w = weights(e_s[z, at : at + 8, :], shifted)
            adj = []
            for t in range(9):
                rows = [c[t, z, 6 + at + i : 14 + at + i, :] for i in range(5)]
                adj.append(transported(rows, w))
            if step == 2:
                for t in range(9):
                    fin_s[e, t, z] = adj[t]
                return sums
            share = [prof_ref[z] * coef_ref[t] for t in range(9)]
            sums = [sums[m] + sum(share[3 * m + j] * adj[3 * m + j] for j in range(3)) for m in range(3)]
            rate = [rate_ref[q, z] for q in range(6)]
            state = [t_s[1 - step, t, z, at : at + 8, :] for t in range(9)]
            done = coag(adj, state, rate)
            for t in range(9):
                b_bufs[step + 1][t, z + 1] = done[t]
            return sums

        def count(step, sums):
            at = starts[step]
            buf_row = sub + at
            rows = 2 + 2 * step
            if upper:
                good = (buf_row >= 8 - rows) & (buf_row < 8)
            else:
                good = (buf_row >= 8) & (buf_row < 8 + rows)
            for m in range(3):
                em_s[m, at : at + 8, :] = em_s[m, at : at + 8, :] + jnp.where(good, sums[m], 0.0)

        none = [zero, zero, zero]

        def mixing(step):
            def stage(z, sums):
                mix(step, z)
                return sums

            return stage

        def moving(step):
            return lambda z, sums: move(step, z, sums)

        count(0, pipeline([(0, mixing(0)), (2, moving(0)), (5, mixing(1))], none))

        def far_moving(z, sums):
            near = 0 if upper else 8
            w = [w_ref[i, z, near : near + 8, :] for i in range(9)]
            for t in range(9):
                rows = [c_last[t, z, near + 6 + i : near + 14 + i, :] for i in range(5)]
                fin_s[1, t, z] = transported(rows, w)
            return sums

        later = [(0, moving(1)), (3, mixing(2)), (5, moving(2))] + [(4, far_moving)] * far
        count(1, pipeline(later, none))
        for m in range(3):
            a_s[e, m] = em_s[m, own_at : own_at + 8, :]

    def finish(has_upper, has_lower, e_upper, e_lower):
        mine = (iota((16, 128), 1) < 64) == (core == 0)

        def rows_of(t, z):
            low = fin_s[e_lower, t, z]
            high = fin_s[e_upper, t, z]
            return stack_rows(low, high)

        def tracer(t, _):
            for l in range(8):
                keep_ref[t, l] = rows_of(t, 8 * core + l)
            for l in range(4):
                z = 8 * (1 - core) + l
                send_ref[t * 4 + l] = jnp.where(mine, rows_of(t, z), lane_roll(rows_of(t, z + 4), 64))

        for t in range(9):
            tracer(t, 0)
        for m in range(3):
            low = em_ref[m, 0:8, :]
            high = em_ref[m, 8:16, :]
            if has_upper:
                high = high + a_s[e_upper, m]
            if has_lower:
                low = low + a_s[e_lower, m]
            send_ref[36 + m] = stack_rows(low, high)

    if lat_count == 2:

        def south():
            run(True, 0)
            finish(True, False, 0, 1)

        def north():
            run(False, 0)
            finish(False, True, 1, 0)

        pl.when(lat == 0)(south)
        pl.when(lat == 1)(north)
    else:
        run(True, 0)
        run(False, 1)
        finish(True, True, 0, 1)


def join_kernel(keep_ref, send_ref, recv_ref, source_ref, out_ref, em_ref, part, em_part, sems):
    core = lax.axis_index("lev")
    mine = (iota((16, 128), 1) < 64) == (core == 0)
    source = source_ref[...].astype(F32)
    for m in range(3):
        em_part[m] = jnp.where(mine, send_ref[36 + m], recv_ref[36 + m]) * source
    copies = [pltpu.make_async_copy(em_part, em_ref, sems.at[9])]
    copies[0].start()
    for t in range(9):
        for l in range(4):
            got = recv_ref[t * 4 + l]
            part[t, l] = jnp.where(mine, keep_ref[t, l], got)
            part[t, l + 4] = jnp.where(mine, keep_ref[t, l + 4], lane_roll(got, 64))
        copies.append(pltpu.make_async_copy(part.at[t], out_ref.at[t], sems.at[t]))
        copies[-1].start()
    for copy in copies:
        copy.wait()


def corner_kernel(lon_ref, out_ref):
    out_ref[...] = lon_ref[1 - lax.axis_index("lat")]


def shape(*dims, dtype=F32):
    return jax.ShapeDtypeStruct(dims, dtype)


def call(kernel, outs, scratch, *args, specs=None, out_specs=None, mib=32):
    return pl.pallas_call(
        kernel,
        out_shape=outs,
        in_specs=specs or [VMEM] * len(args),
        out_specs=out_specs or [VMEM] * len(outs),
        scratch_shapes=scratch,
        compiler_params=pltpu.CompilerParams(vmem_limit_bytes=mib * 1024 * 1024),
    )(*args)


def shards(
    adjoint_in,
    trajectory,
    courant,
    mixing,
    coag_rates,
    settle_speed,
    settle_class,
    emis_profile,
    emis_coef,
    land_mask,
    source_mask,
):
    lat_count = lax.axis_size("lat")
    lon_count = lax.axis_size("lon")
    edges = 1 if lat_count == 2 else 2
    swap = [(0, 1), (1, 0)]

    def over_lev(value):
        return lax.ppermute(value, "lev", swap)

    def lat_moves(messages):
        if edges == 1:
            return [lax.ppermute(messages[0], "lat", swap)]
        up = [(j, j + 1) for j in range(lat_count - 1)]
        down = [(j + 1, j) for j in range(lat_count - 1)]
        return [lax.ppermute(messages[-1], "lat", down), lax.ppermute(messages[0], "lat", up)]

    def bind(kernel):
        def run(*refs):
            return kernel(lat_count, *refs)

        return run

    given = (adjoint_in, trajectory, courant, mixing, land_mask)
    field, traj, land = call(
        load_kernel,
        [
            shape(12, *adjoint_in.shape[1:]),
            jax.ShapeDtypeStruct(trajectory.shape, trajectory.dtype),
            jax.ShapeDtypeStruct(land_mask.shape, land_mask.dtype),
        ],
        [pltpu.SemaphoreType.DMA((5,))],
        *[pltpu.with_memory_space_constraint(v, pltpu.HBM) for v in given],
        specs=[pl.BlockSpec(memory_space=pltpu.HBM)] * 5,
        mib=16,
    )
    own = (field, traj)
    other = (over_lev(field), over_lev(trajectory))
    half = call(
        lon_start_kernel, [shape(12, 16, 128), shape(27, 16, 128, dtype=BF16)], [], *own, land, mib=16
    )
    (lon_out,) = call(
        lon_pack_kernel, [shape(2, LON_TILES, 16, 128, dtype=BF16)], [], *other, land, *half, mib=16
    )
    lat_out = call(
        bind(lat_pack_kernel), [shape(LAT_TILES, 16, 128, dtype=BF16)] * edges, [], *own, land, mib=16
    )
    lat_in = lat_moves(lat_out)
    lon_pairs = []
    for i in range(lon_count):
        lon_pairs.append((2 * i + 1, 2 * ((i + 1) % lon_count)))
        lon_pairs.append((2 * i, 2 * ((i - 1) % lon_count) + 1))
    lon_in = lax.ppermute(lon_out, ("lon", "lev"), lon_pairs)
    scalars = (coag_rates, settle_speed, settle_class, emis_profile, emis_coef)
    state = pltpu.VMEM((9, 16, 16, 128), F32)
    between = pltpu.VMEM((9, 18, 16, 128), F32)
    padded = shape(9, 16, 32, 128)
    c_own, emis, traj_own, wind_own, mix_own = call(
        bind(first_kernel),
        [
            shape(9, 16, 16, 128),
            shape(3, 16, 128),
            shape(2, 9, 16, 16, 128, dtype=BF16),
            shape(2, 16, 16, 128),
            shape(16, 16, 128),
        ],
        [between],
        *own,
        *other,
        land,
        *scalars,
        specs=[VMEM] * 5 + [SMEM] * 5,
    )
    lon_in, c_own = lax.optimization_barrier((lon_in, c_own))
    if edges == 1:
        corner_out = call(corner_kernel, [shape(LON_TILES, 16, 128, dtype=BF16)], [], lon_in, mib=16)
    else:
        corner_out = [lon_in[1], lon_in[0]]
    corner_in = lat_moves(corner_out)
    traj_1, c_first, c_next, north, east, mix, land_all, weight, emis, strip = call(
        bind(second_kernel),
        [
            shape(9, 16, 16, 128, dtype=BF16),
            padded,
            padded,
            shape(16, 32, 128),
            shape(16, 16, 128),
            shape(17, 16, 128),
            shape(16, 128),
            shape(9, 16, 16, 128),
            shape(3, 16, 128),
            shape(9, 16, 128, dtype=BF16),
        ],
        [state, between, pltpu.VMEM((12, 16, 128), F32)],
        land,
        lon_in,
        c_own,
        emis,
        traj_own,
        wind_own,
        mix_own,
        *scalars,
        specs=[VMEM] * 7 + [SMEM] * 5,
    )
    c_next, *lat_in = lax.optimization_barrier((c_next, *lat_in))
    c_last, emis, traj_0 = call(
        bind(third_kernel),
        [padded, shape(3, 16, 128), shape(9, 16, 16, 128, dtype=BF16)],
        [state, between],
        traj_own,
        strip,
        mix,
        land_all,
        weight,
        c_next,
        emis,
        *scalars,
        specs=[VMEM] * 7 + [SMEM] * 5,
    )
    inner = (traj_1, c_first, c_next, north, east, mix, land_all, c_last, weight, traj_0, emis)
    lat_all = []
    for value in lat_in:
        lat_all += [value, over_lev(value)]
    keep, send = call(
        bind(edge_kernel),
        [shape(9, 8, 16, 128), shape(39, 16, 128)],
        [
            pltpu.VMEM((9, 18, 8, 128), F32),
            pltpu.VMEM((9, 18, 8, 128), F32),
            pltpu.VMEM((9, 16, 32, 128), F32),
            pltpu.VMEM((9, 16, 32, 128), F32),
            pltpu.VMEM((9, 16, 32, 128), F32),
            pltpu.VMEM((2, 9, 16, 16, 128), F32),
            pltpu.VMEM((16, 32, 128), F32),
            pltpu.VMEM((16, 16, 128), F32),
            pltpu.VMEM((17, 16, 128), F32),
            pltpu.VMEM((16, 128), F32),
            pltpu.VMEM((edges, 3, 8, 128), F32),
            pltpu.VMEM((3, 24, 128), F32),
            pltpu.VMEM((2, 9, 16, 8, 128), F32),
        ],
        *inner,
        *lat_all,
        *corner_in,
        *scalars,
        specs=[VMEM] * (11 + 3 * edges) + [SMEM] * 5,
        mib=40,
    )
    recv = over_lev(send)
    out, emis = call(
        join_kernel,
        [shape(9, 8, 16, 128), shape(3, 16, 128)],
        [pltpu.VMEM((9, 8, 16, 128), F32), pltpu.VMEM((3, 16, 128), F32), pltpu.SemaphoreType.DMA((10,))],
        keep,
        send,
        recv,
        source_mask,
        out_specs=[pl.BlockSpec(memory_space=pltpu.HBM)] * 2,
    )
    return (out, emis)


def solution(mesh):
    return jax.shard_map(
        shards,
        mesh=mesh,
        in_specs=(
            P(None, "lev", "lat", "lon"),
            P(None, None, "lev", "lat", "lon"),
            P(None, "lev", "lat", "lon"),
            P("lev", "lat", "lon"),
            P(),
            P(),
            P(),
            P(),
            P(),
            P("lat", "lon"),
            P("lat", "lon"),
        ),
        out_specs=(P(None, "lev", "lat", "lon"), P(None, "lat", "lon")),
        check_vma=False,
    )
```
